256 devices in a mesh: dp: 8 (over z), seq: 16 (over x_lo, y, core), tensor: 2 (over x_hi).
Axes of the slice: x: 4 (x_hi: 2, x_lo: 2; x = x_hi * 2 + x_lo), y: 4, z: 8, core: 2. Of those that a mesh axis runs over, the one named last changes fastest.
Arguments:
- latent: bfloat16 [8, 16, 256, 1152], P('dp', 'seq'), may hold values from -6 to 6
- mod_shift: float32 [8, 1152], P('dp'), may hold values from -3 to 3
- mod_scale: float32 [8, 1152], P('dp'), may hold values from -2.5 to 2.5
- w_qkv: bfloat16 [1152, 3, 1152], P(None, None, 'tensor'), may hold values from -0.1875 to 0.1875
- q_gain: float32 [72], replicated, may hold values from 0.1 to 1.9
- k_gain: float32 [72], replicated, may hold values from 0.1 to 1.9
- cotangent: bfloat16 [8, 16, 256, 1152], P('dp', 'seq', None, 'tensor'), may hold values from -6 to 6
Outputs:
- attended: bfloat16 [8, 16, 256, 1152], P('dp', 'seq', None, 'tensor')
- grad_latent: bfloat16 [8, 16, 256, 1152], P('dp', 'seq', None, 'tensor')
- grad_qkv: bfloat16 [1152, 3, 1152], P(None, None, 'tensor')
The draws below stay inside these ranges and needn't reach their ends.
All inputs are finite; a program needn't handle non-finite values.
Results may differ from the reference program's by a relative error of at most 0.02.
Values may be sent and summed in bfloat16 or wider, within the bound.
No kernel may reach another device: no remote copies, remote signals or barrier semaphores. Data moves between devices by JAX's collectives and lax.ppermute only.
A program may use at most 128 MiB of HBM per device.

```python
import math
from functools import partial
import jax
import jax.numpy as jnp
from jax import lax

D = 1152
HEADS = 16
HD = 72
FRAMES = 16
PATCHES = 256
CLIPS = 8


def block_levels(key, extent, cuts, smallest, largest):
    level = 1.0
    for dim, parts in cuts:
        heights = jax.random.uniform(jax.random.fold_in(jax.random.fold_in(key, 6), dim), (parts,), jnp.float32, smallest / len(cuts), largest / len(cuts))
        level = level * jnp.repeat(jnp.exp(heights), extent[dim] // parts).reshape((-1,) + (1,) * (len(extent) - 1 - dim))
    return level


def bell_draw(own_key, extent, scale, reach, cuts=(), held_as=jnp.bfloat16):
    level = block_levels(own_key, extent, cuts, -0.22, 0.18) if cuts else 1.0
    values = jax.random.normal(own_key, extent, jnp.float32) * scale * level
    return jnp.minimum(jnp.maximum(values, -reach), reach).astype(held_as)


def setup_inputs(seed: int = 0) -> dict:
    arg_keys = jax.random.split(jax.random.key(seed), 8)
    latent = bell_draw(arg_keys[0], (CLIPS, FRAMES, PATCHES, D), 1.0, 6.0, ((0, 8), (1, 16)))
    mod_shift = bell_draw(arg_keys[1], (CLIPS, D), 0.5, 3.0, ((0, 8),), jnp.float32)
    mod_scale = bell_draw(arg_keys[2], (CLIPS, D), 0.3, 2.5, ((0, 8),), jnp.float32)
    w_qkv = bell_draw(arg_keys[3], (D, 3, HEADS * HD), D ** -0.5, 0.1875, ((2, 2),))
    q_gain = jnp.clip(1.0 + 0.18 * jax.random.normal(arg_keys[4], (HD,), jnp.float32), 0.1, 1.9)
    k_gain = jnp.clip(1.0 + 0.18 * jax.random.normal(arg_keys[5], (HD,), jnp.float32), 0.1, 1.9)
    cotangent = bell_draw(arg_keys[6], (CLIPS, FRAMES, PATCHES, HEADS * HD), 1.0, 6.0, ((0, 8), (1, 16), (3, 2)))
    return dict(latent=latent, mod_shift=mod_shift, mod_scale=mod_scale, w_qkv=w_qkv, q_gain=q_gain, k_gain=k_gain, cotangent=cotangent)


def modulate(values, mod_shift, mod_scale):
    centred = values - lax.optimization_barrier(jnp.mean(values, axis=-1, keepdims=True))
    inverse = lax.rsqrt(lax.optimization_barrier(jnp.mean(centred * centred, axis=-1, keepdims=True)) + 1e-06)
    return centred * inverse * (1.0 + mod_scale) + mod_shift

def head_norm(values, gain_row):
    return values * lax.rsqrt(lax.optimization_barrier(jnp.mean(values * values, axis=-1, keepdims=True)) + 1e-06) * gain_row

def temporal(queries, key_rows, values, q_gain, k_gain):
    queries = head_norm(queries, q_gain)
    key_rows = head_norm(key_rows, k_gain)
    scores = jnp.einsum('...fphd,...gphd->...phfg', queries, key_rows) / math.sqrt(queries.shape[-1])
    weights = jnp.exp(scores)
    weights = weights / lax.optimization_barrier(jnp.sum(weights, axis=-1, keepdims=True))
    return jnp.einsum('...phfg,...gphd->...fphd', weights, values)

def reference(latent, mod_shift, mod_scale, w_qkv, q_gain, k_gain, cotangent):
    flat_w = w_qkv.reshape(D, 3 * HEADS * HD)
    attend = partial(temporal, q_gain=q_gain, k_gain=k_gain)

    def one_clip(accumulated, clip_items):
        clip_rows, shift_row, scale_row, clip_cotangent = clip_items
        mod_float, norm_back = jax.vjp(lambda v: modulate(v, shift_row, scale_row), clip_rows.astype(jnp.float32))
        modulated = mod_float.astype(jnp.bfloat16).reshape(FRAMES * PATCHES, D)
        qkv = jnp.dot(modulated, flat_w, preferred_element_type=jnp.float32).astype(jnp.bfloat16)
        pieces = qkv.reshape(FRAMES, PATCHES, 3, HEADS, HD).astype(jnp.float32)
        attended_float, attend_back = jax.vjp(attend, pieces[:, :, 0], pieces[:, :, 1], pieces[:, :, 2])
        cotangents = attend_back(clip_cotangent.reshape(FRAMES, PATCHES, HEADS, HD).astype(jnp.float32))
        grad_proj = jnp.stack(cotangents, axis=2).reshape(FRAMES * PATCHES, 3 * HEADS * HD).astype(jnp.bfloat16)
        accumulated = accumulated + jnp.dot(modulated.T, grad_proj, preferred_element_type=jnp.float32)
        grad_mod = jnp.dot(grad_proj, flat_w.T, preferred_element_type=jnp.float32)
        grad_clip = norm_back(grad_mod.reshape(FRAMES, PATCHES, D))[0].astype(jnp.bfloat16)
        attended_clip = attended_float.astype(jnp.bfloat16).reshape(FRAMES, PATCHES, HEADS * HD)
        return (accumulated, (attended_clip, grad_clip))
    start_sum = jnp.zeros((D, 3 * HEADS * HD), jnp.float32)
    accumulated, outputs = lax.scan(one_clip, start_sum, (latent, mod_shift, mod_scale, cotangent))
    attended, grad_latent = outputs
    grad_qkv = (accumulated / math.sqrt(CLIPS * FRAMES * PATCHES)).astype(jnp.bfloat16).reshape(D, 3, HEADS * HD)
    return (attended, grad_latent, grad_qkv)
```

```python
import functools
import math

import jax
import jax.numpy as jnp
from jax import lax
from jax.experimental import pallas as pl
from jax.experimental.pallas import tpu as pltpu
from jax.sharding import Mesh, PartitionSpec as P

BF = jnp.bfloat16
F32 = jnp.float32
EPS = 1e-06
NN = (((1,), (0,)), ((), ()))
NT = (((1,), (1,)), ((), ()))
ROWS, LANES = 16, 128
SEQ = ("xlo", "y", "core")


def mm(a, b, dims):
    return lax.dot_general(a, b, dims, preferred_element_type=F32)


def eye(n):
    rows = lax.broadcasted_iota(jnp.int32, (n, n), 0)
    cols = lax.broadcasted_iota(jnp.int32, (n, n), 1)
    return jnp.where(rows == cols, 1.0, 0.0).astype(BF)


def unit_of(x_ref, width):
    values = x_ref[:, :width].astype(F32)
    centred = values - jnp.sum(values, axis=1, keepdims=True) * (1.0 / width)
    inverse = lax.rsqrt(jnp.sum(centred * centred, axis=1, keepdims=True) * (1.0 / width) + EPS)
    return centred * inverse, inverse


def attend_kernel(x_ref, shift_ref, scale_ref, wt_ref, qg_ref, kg_ref,
                  gw_ref, gp_ref, att_ref, mod_s, gpt_s, ot_s, *, patches, heads, hd):
    tokens, total = x_ref.shape
    width = scale_ref.shape[1]
    hw = heads * hd
    unit, _ = unit_of(x_ref, width)
    mod_s[...] = (unit * (1.0 + scale_ref[...]) + shift_ref[...]).astype(BF)
    mod = mod_s[...]
    root = 1.0 / math.sqrt(hd)
    ident = eye(tokens)
    cot_t = mm(eye(hw), x_ref[:, width:], NT).reshape(heads, hd, tokens)

    def project(part):
        rows = mm(wt_ref[part * hw : (part + 1) * hw, :], mod, NT)
        return rows.astype(BF).astype(F32).reshape(heads, hd, tokens)

    def norm(part, gain_ref):
        rows = project(part)
        inverse = lax.rsqrt(jnp.sum(rows * rows, axis=1, keepdims=True) * (1.0 / hd) + EPS)
        return rows * inverse, inverse, gain_ref[...]

    q_hat, q_inv, q_gain = norm(0, qg_ref)
    k_hat, k_inv, k_gain = norm(1, kg_ref)
    values = project(2)
    row_id = lax.broadcasted_iota(jnp.int32, (tokens, tokens), 0)
    col_id = lax.broadcasted_iota(jnp.int32, (tokens, tokens), 1)
    same = lax.rem(row_id, patches) == lax.rem(col_id, patches)

    def back(hat, inverse, gain, grad):
        weighted = grad * gain
        mean = jnp.sum(hat * weighted, axis=0, keepdims=True) * (1.0 / hd)
        return inverse * (weighted - hat * mean)

    for h in range(heads):
        qn = q_hat[h] * q_gain
        kn = k_hat[h] * k_gain
        q_b = qn.astype(BF)
        k_b = kn.astype(BF)
        v_b = values[h].astype(BF)
        o_b = cot_t[h].astype(BF)
        k_rows = mm(ident, k_b, NT).astype(BF)
        v_rows = mm(ident, v_b, NT).astype(BF)
        scores = mm(k_rows, q_b, NN) * root
        weights = jnp.where(same, jnp.exp(scores), 0.0)
        probs = weights * (1.0 / jnp.sum(weights, axis=0, keepdims=True))
        probs_b = probs.astype(BF)
        ot_s[h * hd : (h + 1) * hd, :] = mm(v_b, probs_b, NN)
        grad_v = mm(o_b, probs_b, NT)
        grad_p = mm(v_rows, o_b, NN)
        terms = probs * grad_p
        grad_s = (terms - probs * jnp.sum(terms, axis=0, keepdims=True)) * root
        grad_s = grad_s.astype(BF)
        grad_q = back(q_hat[h], q_inv[h], q_gain, mm(k_b, grad_s, NN))
        grad_k = back(k_hat[h], k_inv[h], k_gain, mm(q_b, grad_s, NT))
        for part, rows in enumerate((grad_q, grad_k, grad_v)):
            start = part * hw + h * hd
            gpt_s[start : start + hd, :] = rows
    for part in range(3):
        lo, hi = part * hw, (part + 1) * hw
        block = gpt_s[lo:hi, :].astype(BF)
        gp_ref[:, lo:hi] = mm(ident, block, NT).astype(BF)
        tiles, base = hw // ROWS, part * (hw // ROWS)
        all_tiles = 3 * tiles
        for j in range(width // LANES):
            cols = slice(j * LANES, (j + 1) * LANES)
            found = mm(block, mod_s[:, cols], NN).astype(BF).reshape(tiles, ROWS, LANES)
            gw_ref[j * all_tiles + base : j * all_tiles + base + tiles] = found
    used = 3 * (hw // ROWS) * (width // LANES)
    gw_ref[used:] = jnp.zeros((gw_ref.shape[0] - used, ROWS, LANES), BF)
    att_ref[...] = mm(ident, ot_s[...].astype(BF), NT).astype(BF)


def attend(x, shift, scale, wt, qg, kg, patches, heads, hd, padded):
    tokens = x.shape[0]
    width = wt.shape[1]
    hw = heads * hd
    return pl.pallas_call(
        functools.partial(attend_kernel, patches=patches, heads=heads, hd=hd),
        out_shape=(
            jax.ShapeDtypeStruct((padded, ROWS, LANES), BF),
            jax.ShapeDtypeStruct((tokens, 3 * hw), BF),
            jax.ShapeDtypeStruct((tokens, hw), BF),
        ),
        scratch_shapes=[
            pltpu.VMEM((tokens, width), BF),
            pltpu.VMEM((3 * hw, tokens), F32),
            pltpu.VMEM((hw, tokens), F32),
        ],
        compiler_params=pltpu.CompilerParams(vmem_limit_bytes=48 * 2**20),
        name="attend",
    )(x, shift, scale, wt, qg, kg)


def window_of(half):
    return -(-half // LANES) * LANES


def split_kernel(which_ref, x_ref, scale_ref, wt_ref, gp_ref, send_ref, keep_ref, unit_ref):
    width = wt_ref.shape[1]
    half = width // 2
    win = window_of(half)
    grad = mm(gp_ref[...], wt_ref[...], NN)
    unit, inverse = unit_of(x_ref, width)
    scaled = grad * (1.0 + scale_ref[...])
    first = jnp.sum(scaled, axis=1, keepdims=True)
    second = jnp.sum(scaled * unit, axis=1, keepdims=True)
    mine_low = which_ref[0] == 0
    col = lax.broadcasted_iota(jnp.int32, (grad.shape[0], win), 1)
    here = jnp.where(mine_low, half, 0)
    there = jnp.where(mine_low, 0, half)
    low, high = scaled[:, :win], scaled[:, width - win :]
    send = jnp.where(mine_low, high, low)
    keep = jnp.where(mine_low, low, high)
    for place, term in enumerate((first, second)):
        coarse = term.astype(BF).astype(F32)
        send = jnp.where(col == there + 2 * place, coarse, send)
        send = jnp.where(col == there + 2 * place + 1, term - coarse, send)
    for place, term in enumerate((first, second, inverse)):
        keep = jnp.where(col == here + place, term, keep)
    send_ref[...] = send.astype(BF)
    keep_ref[...] = keep
    unit_ref[...] = jnp.where(mine_low, unit[:, :win], unit[:, width - win :])


def split(which, x, scale, wt, gp):
    tokens = x.shape[0]
    win = window_of(wt.shape[1] // 2)
    smem = pl.BlockSpec(memory_space=pltpu.SMEM)
    vmem = pl.BlockSpec(memory_space=pltpu.VMEM)
    return pl.pallas_call(
        split_kernel,
        in_specs=[smem, vmem, vmem, vmem, vmem],
        out_shape=(
            jax.ShapeDtypeStruct((tokens, win), BF),
            jax.ShapeDtypeStruct((tokens, win), F32),
            jax.ShapeDtypeStruct((tokens, win), F32),
        ),
        compiler_params=pltpu.CompilerParams(vmem_limit_bytes=40 * 2**20),
        name="split",
    )(which, x, scale, wt, gp)


def finish_kernel(which_ref, recv_ref, keep_ref, unit_ref, out_ref, *, width):
    half = width // 2
    win = recv_ref.shape[1]
    mine_low = which_ref[0] == 0
    recv = recv_ref[...].astype(F32)
    keep = keep_ref[...]

    def column(block, place):
        return jnp.where(mine_low, block[:, half + place : half + place + 1], block[:, place : place + 1])

    first = column(keep, 0) + (column(recv, 0) + column(recv, 1))
    second = column(keep, 1) + (column(recv, 2) + column(recv, 3))
    inverse = column(keep, 2)
    grad = keep + recv
    out = inverse * (grad - first * (1.0 / width) - unit_ref[...] * (second * (1.0 / width)))
    moved = pltpu.roll(out, win - (win - half), 1)
    out_ref[...] = jnp.where(mine_low, out, moved)[:, :half].astype(BF)


def finish(which, recv, keep, unit, width):
    tokens = recv.shape[0]
    smem = pl.BlockSpec(memory_space=pltpu.SMEM)
    vmem = pl.BlockSpec(memory_space=pltpu.VMEM)
    return pl.pallas_call(
        functools.partial(finish_kernel, width=width),
        in_specs=[smem, vmem, vmem, vmem],
        out_shape=jax.ShapeDtypeStruct((tokens, width // 2), BF),
        compiler_params=pltpu.CompilerParams(vmem_limit_bytes=24 * 2**20),
        name="finish",
    )(which, recv, keep, unit)


def untile_kernel(tiles_ref, out_ref, *, factor):
    rows = out_ref.shape[0] // ROWS
    for j in range(out_ref.shape[1] // LANES):
        block = tiles_ref[j * rows : (j + 1) * rows].astype(F32) * factor
        out_ref[:, j * LANES : (j + 1) * LANES] = block.reshape(rows * ROWS, LANES).astype(BF)


def untile(tiles, rows, width, factor):
    return pl.pallas_call(
        functools.partial(untile_kernel, factor=factor),
        out_shape=jax.ShapeDtypeStruct((rows, width), BF),
        compiler_params=pltpu.CompilerParams(vmem_limit_bytes=40 * 2**20),
        name="untile",
    )(tiles)


def exchange(x, axes):
    count = math.prod(lax.axis_size(a) for a in axes)
    parts = x.reshape((count, x.shape[0] // count) + x.shape[1:])
    return lax.all_to_all(parts, axes, split_axis=0, concat_axis=0, tiled=True)


def scatter_sum(x, axes):
    return jnp.sum(exchange(x, axes).astype(F32), axis=0).astype(BF)


def total_of(tiles):
    own = scatter_sum(scatter_sum(scatter_sum(tiles, ("core",)), ("xlo", "y")), ("dp",))
    own = lax.all_gather(own, "dp", axis=0, tiled=True)
    own = lax.all_gather(own, ("xlo", "y"), axis=0, tiled=True)
    return lax.all_gather(own, "core", axis=0, tiled=True)


def body(latent, mod_shift, mod_scale, w_qkv, q_gain, k_gain, cotangent):
    _, _, patches, width = latent.shape
    hw = w_qkv.shape[2]
    hd = q_gain.shape[0]
    heads = hw // hd
    frames = 1
    for a in SEQ:
        frames *= lax.axis_size(a)
    own_patches = patches // frames
    clips = lax.axis_size("dp")
    wt = w_qkv.transpose(1, 2, 0).reshape(3 * hw, width)
    x = jnp.concatenate([latent[0, 0], cotangent[0, 0]], axis=1)
    x = x.reshape(frames, own_patches, width + hw)
    x = lax.all_to_all(x, SEQ, split_axis=0, concat_axis=0, tiled=True).reshape(patches, width + hw)
    group = 2
    for a in ("dp",) + SEQ:
        group *= lax.axis_size(a)
    used = (3 * hw // ROWS) * (width // LANES)
    padded = -(-used // group) * group
    gw, gp, attended = attend(
        x, mod_shift, mod_scale, wt, q_gain[:, None], k_gain[:, None], own_patches, heads, hd, padded
    )
    which = lax.axis_index("tensor").astype(jnp.int32).reshape(1)

    def home(rows):
        rows = rows.reshape(frames, own_patches, hw)
        rows = lax.all_to_all(rows, SEQ, split_axis=0, concat_axis=0, tiled=True)
        return rows.reshape(1, 1, patches, hw)

    send, keep, unit = split(which, x, mod_scale, wt, gp)
    recv = lax.ppermute(send, "tensor", [(0, 1), (1, 0)])
    grad_latent = home(finish(which, recv, keep, unit, width))
    factor = 1.0 / math.sqrt(clips * frames * patches)
    grad_qkv = untile(total_of(gw), 3 * hw, width, factor)
    grad_qkv = grad_qkv.reshape(3, hw, width).transpose(2, 0, 1)
    return (home(attended), grad_latent, grad_qkv)


def solution(mesh):
    fine = Mesh(mesh.devices.reshape(mesh.shape["dp"], 2, 4, 2, 2), ("dp",) + SEQ + ("tensor",))
    in_specs = (
        P("dp", SEQ, None, None),
        P("dp", None),
        P("dp", None),
        P(None, None, "tensor"),
        P(),
        P(),
        P("dp", SEQ, None, "tensor"),
    )
    out_specs = (
        P("dp", SEQ, None, "tensor"),
        P("dp", SEQ, None, "tensor"),
        P(None, None, "tensor"),
    )
    return jax.shard_map(body, mesh=fine, in_specs=in_specs, out_specs=out_specs, check_vma=False)
```

```python
import functools
import math

import jax
import jax.numpy as jnp
from jax import lax
from jax.experimental import pallas as pl
from jax.experimental.pallas import tpu as pltpu
from jax.sharding import Mesh, PartitionSpec as P

BF = jnp.bfloat16
F32 = jnp.float32
EPS = 1e-06
NN = (((1,), (0,)), ((), ()))
NT = (((1,), (1,)), ((), ()))
ROWS, LANES = 16, 128
PLANE = ("xlo", "y")
SEQ = PLANE + ("core",)


def mm(a, b, dims):
    return lax.dot_general(a, b, dims, preferred_element_type=F32)


def eye(n):
    rows = lax.broadcasted_iota(jnp.int32, (n, n), 0)
    cols = lax.broadcasted_iota(jnp.int32, (n, n), 1)
    return jnp.where(rows == cols, 1.0, 0.0).astype(BF)


def unit_of(x_ref, width):
    values = x_ref[:, :width].astype(F32)
    centred = values - jnp.sum(values, axis=1, keepdims=True) * (1.0 / width)
    inverse = lax.rsqrt(jnp.sum(centred * centred, axis=1, keepdims=True) * (1.0 / width) + EPS)
    return centred * inverse, inverse


def attend_kernel(core_ref, x_ref, shift_ref, scale_ref, wt_ref, qg_ref, kg_ref,
                  keep_ref, send_ref, gp_ref, att_ref, mod_s, gpt_s, ot_s, gw_ref, *, patches, heads, hd):
    tokens, total = x_ref.shape
    width = scale_ref.shape[1]
    hw = heads * hd
    unit, _ = unit_of(x_ref, width)
    mod_s[...] = (unit * (1.0 + scale_ref[...]) + shift_ref[...]).astype(BF)
    mod = mod_s[...]
    root = 1.0 / math.sqrt(hd)
    ident = eye(tokens)
    cot_t = mm(eye(hw), x_ref[:, width:], NT).reshape(heads, hd, tokens)

    def project(part):
        rows = mm(wt_ref[part * hw : (part + 1) * hw, :], mod, NT)
        return rows.astype(BF).astype(F32).reshape(heads, hd, tokens)

    def norm(part, gain_ref):
        rows = project(part)
        inverse = lax.rsqrt(jnp.sum(rows * rows, axis=1, keepdims=True) * (1.0 / hd) + EPS)
        return rows * inverse, inverse, gain_ref[...]

    q_hat, q_inv, q_gain = norm(0, qg_ref)
    k_hat, k_inv, k_gain = norm(1, kg_ref)
    values = project(2)
    row_id = lax.broadcasted_iota(jnp.int32, (tokens, tokens), 0)
    col_id = lax.broadcasted_iota(jnp.int32, (tokens, tokens), 1)
    same = lax.rem(row_id, patches) == lax.rem(col_id, patches)

    def back(hat, inverse, gain, grad):
        weighted = grad * gain
        mean = jnp.sum(hat * weighted, axis=0, keepdims=True) * (1.0 / hd)
        return inverse * (weighted - hat * mean)

    for h in range(heads):
        qn = q_hat[h] * q_gain
        kn = k_hat[h] * k_gain
        q_b = qn.astype(BF)
        k_b = kn.astype(BF)
        v_b = values[h].astype(BF)
        o_b = cot_t[h].astype(BF)
        k_rows = mm(ident, k_b, NT).astype(BF)
        v_rows = mm(ident, v_b, NT).astype(BF)
        scores = mm(k_rows, q_b, NN) * root
        weights = jnp.where(same, jnp.exp(scores), 0.0)
        probs = weights * (1.0 / jnp.sum(weights, axis=0, keepdims=True))
        probs_b = probs.astype(BF)
        ot_s[h * hd : (h + 1) * hd, :] = mm(v_b, probs_b, NN)
        grad_v = mm(o_b, probs_b, NT)
        grad_p = mm(v_rows, o_b, NN)
        terms = probs * grad_p
        grad_s = (terms - probs * jnp.sum(terms, axis=0, keepdims=True)) * root
        grad_s = grad_s.astype(BF)
        grad_q = back(q_hat[h], q_inv[h], q_gain, mm(k_b, grad_s, NN))
        grad_k = back(k_hat[h], k_inv[h], k_gain, mm(q_b, grad_s, NT))
        for part, rows in enumerate((grad_q, grad_k, grad_v)):
            start = part * hw + h * hd
            gpt_s[start : start + hd, :] = rows
    for part in range(3):
        lo, hi = part * hw, (part + 1) * hw
        block = gpt_s[lo:hi, :].astype(BF)
        gp_ref[:, lo:hi] = mm(ident, block, NT).astype(BF)
        tiles, base = hw // ROWS, part * (hw // ROWS)
        all_tiles = 3 * tiles
        for j in range(width // LANES):
            cols = slice(j * LANES, (j + 1) * LANES)
            found = mm(block, mod_s[:, cols], NN).astype(BF).reshape(tiles, ROWS, LANES)
            gw_ref[j * all_tiles + base : j * all_tiles + base + tiles] = found
    used = 3 * (hw // ROWS) * (width // LANES)
    gw_ref[used:] = jnp.zeros((gw_ref.shape[0] - used, ROWS, LANES), BF)
    size = keep_ref.shape[0]
    keep_ref[...] = gw_ref[pl.ds(core_ref[0] * size, size)]
    send_ref[...] = gw_ref[pl.ds((1 - core_ref[0]) * size, size)]
    att_ref[...] = mm(ident, ot_s[...].astype(BF), NT).astype(BF)


def attend(core, x, shift, scale, wt, qg, kg, patches, heads, hd, padded):
    tokens = x.shape[0]
    width = wt.shape[1]
    hw = heads * hd
    smem = pl.BlockSpec(memory_space=pltpu.SMEM)
    vmem = pl.BlockSpec(memory_space=pltpu.VMEM)
    return pl.pallas_call(
        functools.partial(attend_kernel, patches=patches, heads=heads, hd=hd),
        in_specs=[smem] + [vmem] * 6,
        out_shape=(
            jax.ShapeDtypeStruct((padded // 2, ROWS, LANES), BF),
            jax.ShapeDtypeStruct((padded // 2, ROWS, LANES), BF),
            jax.ShapeDtypeStruct((tokens, 3 * hw), BF),
            jax.ShapeDtypeStruct((tokens, hw), BF),
        ),
        scratch_shapes=[
            pltpu.VMEM((tokens, width), BF),
            pltpu.VMEM((3 * hw, tokens), F32),
            pltpu.VMEM((hw, tokens), F32),
            pltpu.VMEM((padded, ROWS, LANES), BF),
        ],
        compiler_params=pltpu.CompilerParams(vmem_limit_bytes=24 * 2**20),
        name="attend",
    )(core, x, shift, scale, wt, qg, kg)


def window_of(half):
    return -(-half // LANES) * LANES


def split_kernel(which_ref, x_ref, scale_ref, wt_ref, gp_ref, send_ref, keep_ref, unit_ref):
    width = wt_ref.shape[1]
    half = width // 2
    win = window_of(half)
    grad = mm(gp_ref[...], wt_ref[...], NN)
    unit, inverse = unit_of(x_ref, width)
    scaled = grad * (1.0 + scale_ref[...])
    first = jnp.sum(scaled, axis=1, keepdims=True)
    second = jnp.sum(scaled * unit, axis=1, keepdims=True)
    mine_low = which_ref[0] == 0
    col = lax.broadcasted_iota(jnp.int32, (grad.shape[0], win), 1)
    here = jnp.where(mine_low, half, 0)
    there = jnp.where(mine_low, 0, half)
    low, high = scaled[:, :win], scaled[:, width - win :]
    send = jnp.where(mine_low, high, low)
    keep = jnp.where(mine_low, low, high)
    for place, term in enumerate((first, second)):
        coarse = term.astype(BF).astype(F32)
        send = jnp.where(col == there + 2 * place, coarse, send)
        send = jnp.where(col == there + 2 * place + 1, term - coarse, send)
    for place, term in enumerate((first, second, inverse)):
        keep = jnp.where(col == here + place, term, keep)
    send_ref[...] = send.astype(BF)
    keep_ref[...] = keep
    unit_ref[...] = jnp.where(mine_low, unit[:, :win], unit[:, width - win :])


def split(which, x, scale, wt, gp):
    tokens = x.shape[0]
    win = window_of(wt.shape[1] // 2)
    smem = pl.BlockSpec(memory_space=pltpu.SMEM)
    vmem = pl.BlockSpec(memory_space=pltpu.VMEM)
    return pl.pallas_call(
        split_kernel,
        in_specs=[smem, vmem, vmem, vmem, vmem],
        out_shape=(
            jax.ShapeDtypeStruct((tokens, win), BF),
            jax.ShapeDtypeStruct((tokens, win), F32),
            jax.ShapeDtypeStruct((tokens, win), F32),
        ),
        compiler_params=pltpu.CompilerParams(vmem_limit_bytes=16 * 2**20),
        name="split",
    )(which, x, scale, wt, gp)


def finish_kernel(which_ref, recv_ref, keep_ref, unit_ref, out_ref, *, width):
    half = width // 2
    win = recv_ref.shape[1]
    mine_low = which_ref[0] == 0
    recv = recv_ref[...].astype(F32)
    keep = keep_ref[...]

    def column(block, place):
        return jnp.where(mine_low, block[:, half + place : half + place + 1], block[:, place : place + 1])

    first = column(keep, 0) + (column(recv, 0) + column(recv, 1))
    second = column(keep, 1) + (column(recv, 2) + column(recv, 3))
    inverse = column(keep, 2)
    grad = keep + recv
    out = inverse * (grad - first * (1.0 / width) - unit_ref[...] * (second * (1.0 / width)))
    moved = pltpu.roll(out, win - (win - half), 1)
    out_ref[...] = jnp.where(mine_low, out, moved)[:, :half].astype(BF)


def finish(which, recv, keep, unit, width):
    tokens = recv.shape[0]
    smem = pl.BlockSpec(memory_space=pltpu.SMEM)
    vmem = pl.BlockSpec(memory_space=pltpu.VMEM)
    return pl.pallas_call(
        functools.partial(finish_kernel, width=width),
        in_specs=[smem, vmem, vmem, vmem],
        out_shape=jax.ShapeDtypeStruct((tokens, width // 2), BF),
        compiler_params=pltpu.CompilerParams(vmem_limit_bytes=24 * 2**20),
        name="finish",
    )(which, recv, keep, unit)


def merge_kernel(where_ref, keep_ref, got_ref, *out_refs):
    count = len(out_refs)
    size = keep_ref.shape[0] // count
    for k, out_ref in enumerate(out_refs):
        rows = pl.ds((where_ref[0] ^ k) * size, size)
        out_ref[...] = (keep_ref[rows].astype(F32) + got_ref[rows].astype(F32)).astype(BF)


def merge(where, keep, got, count):
    smem = pl.BlockSpec(memory_space=pltpu.SMEM)
    vmem = pl.BlockSpec(memory_space=pltpu.VMEM)
    shape = (keep.shape[0] // count,) + keep.shape[1:]
    return pl.pallas_call(
        merge_kernel,
        in_specs=[smem, vmem, vmem],
        out_shape=tuple(jax.ShapeDtypeStruct(shape, BF) for _ in range(count)),
        compiler_params=pltpu.CompilerParams(vmem_limit_bytes=24 * 2**20),
        name="merge",
    )(where, keep, got)


def sum_kernel(*refs):
    total = refs[0][...].astype(F32)
    for ref in refs[1:-1]:
        total = total + ref[...].astype(F32)
    refs[-1][...] = total.astype(BF)


def sum_of(parts):
    return pl.pallas_call(
        sum_kernel,
        out_shape=jax.ShapeDtypeStruct(parts[0].shape, BF),
        compiler_params=pltpu.CompilerParams(vmem_limit_bytes=8 * 2**20),
        name="sum_of",
    )(*parts)


def spread_kernel(parts_ref, out_ref, *, factor):
    total = jnp.sum(parts_ref[...].astype(F32), axis=0) * factor
    total = total.astype(BF)
    for k in range(out_ref.shape[0]):
        out_ref[k] = total


def spread(parts, factor):
    return pl.pallas_call(
        functools.partial(spread_kernel, factor=factor),
        out_shape=jax.ShapeDtypeStruct(parts.shape, BF),
        compiler_params=pltpu.CompilerParams(vmem_limit_bytes=8 * 2**20),
        name="spread",
    )(parts)


def untile_kernel(where_ref, half_ref, *refs):
    pieces, (out_ref, tiles_s) = refs[:-2], refs[-2:]
    count = len(pieces) // 2
    size = pieces[0].shape[0]
    for side in range(2):
        half = half_ref[0] ^ side
        for k in range(count):
            base = (half * count + (where_ref[0] ^ k)) * size
            tiles_s[pl.ds(base, size)] = pieces[side * count + k][...]
    rows = out_ref.shape[0] // ROWS
    for j in range(out_ref.shape[1] // LANES):
        block = tiles_s[j * rows : (j + 1) * rows]
        out_ref[:, j * LANES : (j + 1) * LANES] = block.reshape(rows * ROWS, LANES)


def untile(where, half, pieces, rows, width):
    smem = pl.BlockSpec(memory_space=pltpu.SMEM)
    vmem = pl.BlockSpec(memory_space=pltpu.VMEM)
    tiles = len(pieces) * pieces[0].shape[0]
    return pl.pallas_call(
        untile_kernel,
        in_specs=[smem, smem] + [vmem] * len(pieces),
        out_shape=jax.ShapeDtypeStruct((rows, width), BF),
        scratch_shapes=[pltpu.VMEM((tiles, ROWS, LANES), BF)],
        compiler_params=pltpu.CompilerParams(vmem_limit_bytes=16 * 2**20),
        name="untile",
    )(where, half, *pieces)


def swap(x, axes, k):
    count = math.prod(lax.axis_size(a) for a in axes)
    return lax.ppermute(x, axes, [(i, i ^ k) for i in range(count)])


def exchange(x, axis):
    parts = x.reshape((-1,) + x.shape[-3:])
    return lax.all_to_all(parts, axis, split_axis=0, concat_axis=0, tiled=True)


def plane_size():
    return lax.axis_size("xlo") * lax.axis_size("y")


def scatter_plane(keep, send):
    where = lax.axis_index(PLANE).astype(jnp.int32).reshape(1)
    parts = merge(where, keep, swap(send, ("core",), 1), plane_size())
    return [parts[0]] + [swap(part, PLANE, k + 1) for k, part in enumerate(parts[1:])]


def sum_clips(own, factor):
    clips = lax.axis_size("dp")
    parts = own.reshape((clips, own.shape[0] // clips) + own.shape[1:])
    return exchange(spread(exchange(parts, "dp"), factor), "dp").reshape(own.shape)


def gather_plane(own, rows, width):
    where = lax.axis_index(PLANE).astype(jnp.int32).reshape(1)
    half = lax.axis_index("core").astype(jnp.int32).reshape(1)
    pieces = [own] + [swap(own, PLANE, k) for k in range(1, plane_size())]
    pieces = pieces + [swap(piece, ("core",), 1) for piece in pieces]
    return untile(where, half, pieces, rows, width)


def body(latent, mod_shift, mod_scale, w_qkv, q_gain, k_gain, cotangent):
    _, _, patches, width = latent.shape
    hw = w_qkv.shape[2]
    hd = q_gain.shape[0]
    heads = hw // hd
    frames = 1
    for a in SEQ:
        frames *= lax.axis_size(a)
    own_patches = patches // frames
    clips = lax.axis_size("dp")
    wt = w_qkv.transpose(1, 2, 0).reshape(3 * hw, width)
    x = jnp.concatenate([latent[0, 0], cotangent[0, 0]], axis=1)
    x = x.reshape(frames, own_patches, width + hw)
    x = lax.all_to_all(x, SEQ, split_axis=0, concat_axis=0, tiled=True).reshape(patches, width + hw)
    group = 2
    for a in ("dp",) + SEQ:
        group *= lax.axis_size(a)
    used = (3 * hw // ROWS) * (width // LANES)
    padded = -(-used // group) * group
    keep_w, send_w, gp, attended = attend(
        lax.axis_index("core").astype(jnp.int32).reshape(1), x, mod_shift, mod_scale, wt, q_gain[:, None], k_gain[:, None], own_patches, heads, hd, padded
    )
    which = lax.axis_index("tensor").astype(jnp.int32).reshape(1)

    def home(rows):
        rows = rows.reshape(frames, own_patches, hw)
        rows = lax.all_to_all(rows, SEQ, split_axis=0, concat_axis=0, tiled=True)
        return rows.reshape(1, 1, patches, hw)

    attended = home(attended)
    send, keep, unit = split(which, x, mod_scale, wt, gp)
    recv = lax.ppermute(send, "tensor", [(0, 1), (1, 0)])
    parts = scatter_plane(keep_w, send_w)
    parts, recv, attended = lax.optimization_barrier((parts, recv, attended))
    grad_latent = finish(which, recv, keep, unit, width)
    own, grad_latent = lax.optimization_barrier((sum_of(parts), grad_latent))
    grad_latent = home(grad_latent)
    factor = 1.0 / math.sqrt(clips * frames * patches)
    grad_qkv = gather_plane(sum_clips(own, factor), 3 * hw, width)
    grad_qkv = grad_qkv.reshape(3, hw, width).transpose(2, 0, 1)
    return (attended, grad_latent, grad_qkv)


def solution(mesh):
    fine = Mesh(mesh.devices.reshape(mesh.shape["dp"], 2, 4, 2, 2), ("dp",) + SEQ + ("tensor",))
    in_specs = (
        P("dp", SEQ, None, None),
        P("dp", None),
        P("dp", None),
        P(None, None, "tensor"),
        P(),
        P(),
        P("dp", SEQ, None, "tensor"),
    )
    out_specs = (
        P("dp", SEQ, None, "tensor"),
        P("dp", SEQ, None, "tensor"),
        P(None, None, "tensor"),
    )
    return jax.shard_map(body, mesh=fine, in_specs=in_specs, out_specs=out_specs, check_vma=False)
```

```python
import functools
import math

import jax
import jax.numpy as jnp
from jax import lax
from jax.experimental import pallas as pl
from jax.experimental.pallas import tpu as pltpu
from jax.sharding import Mesh, PartitionSpec as P

BF = jnp.bfloat16
F32 = jnp.float32
EPS = 1e-06
NN = (((1,), (0,)), ((), ()))
NT = (((1,), (1,)), ((), ()))
LOG2E = math.log2(math.e)
ROWS, LANES = 16, 128
PLANE = ("xlo", "y")
SEQ = PLANE + ("core",)


def mm(a, b, dims):
    return lax.dot_general(a, b, dims, preferred_element_type=F32)


def eye(n):
    rows = lax.broadcasted_iota(jnp.int32, (n, n), 0)
    cols = lax.broadcasted_iota(jnp.int32, (n, n), 1)
    return jnp.where(rows == cols, 1.0, 0.0).astype(BF)


def pack_kernel(latent_ref, cot_ref, out_ref):
    width = latent_ref.shape[1]
    out_ref[:, :width] = latent_ref[...]
    out_ref[:, width:] = mm(eye(latent_ref.shape[0]), cot_ref[...], NT).astype(BF)


def pack(latent, cot_t):
    tokens, width = latent.shape
    return pl.pallas_call(
        pack_kernel,
        out_shape=jax.ShapeDtypeStruct((tokens, width + cot_t.shape[0]), BF),
        compiler_params=pltpu.CompilerParams(vmem_limit_bytes=8 * 2**20),
        name="pack",
    )(latent, cot_t)


def unpack_kernel(rows_ref, first_ref, second_ref):
    ident = eye(LANES)
    half = first_ref.shape[0]
    for start in range(0, 2 * half, LANES):
        found = mm(ident, rows_ref[:, start : start + LANES], NT).astype(BF)
        cut = min(max(half - start, 0), LANES)
        if cut:
            first_ref[start : start + cut] = found[:cut]
        if cut < LANES:
            second_ref[start + cut - half : start + LANES - half] = found[cut:]


def unpack(rows):
    tokens, width = rows.shape
    shape = jax.ShapeDtypeStruct((width // 2, tokens), BF)
    return pl.pallas_call(
        unpack_kernel,
        out_shape=(shape, shape),
        compiler_params=pltpu.CompilerParams(vmem_limit_bytes=8 * 2**20),
        name="unpack",
    )(rows)


def unit_of(values):
    width = values.shape[1]
    centred = values - jnp.sum(values, axis=1, keepdims=True) * (1.0 / width)
    inverse = lax.rsqrt(jnp.sum(centred * centred, axis=1, keepdims=True) * (1.0 / width) + EPS)
    return centred * inverse, inverse


def attend_kernel(core_ref, which_ref, x_ref, shift_ref, scale_ref, wt_hbm, qg_ref, kg_ref,
                  mod_ref, gp_keep_ref, gp_send_ref, att_ref, send_ref, keep_ref, unit_ref,
                  wt_s, gp_s, ot_s, rows_s, sems, *, patches, heads, hd):
    tokens, _ = x_ref.shape
    width = scale_ref.shape[1]
    hw = heads * hd
    copies = []
    for part in range(3):
        rows = pl.ds(part * hw, hw)
        copy = pltpu.make_async_copy(wt_hbm.at[rows], wt_s.at[rows], sems.at[part])
        copy.start()
        copies.append(copy)
    unit, inverse = unit_of(x_ref[:, :width].astype(F32))
    factor = 1.0 + scale_ref[...]
    mod_ref[...] = (unit * factor + shift_ref[...]).astype(BF)
    mod = mod_ref[...]
    ident = eye(tokens)
    cot_t = mm(eye(hw), x_ref[:, width:], NT)

    def project(part):
        copies[part].wait()
        rows = mm(wt_s[part * hw : (part + 1) * hw, :], mod, NT)
        return rows.astype(BF).astype(F32)

    def norm(rows):
        inv = lax.rsqrt(jnp.sum(rows * rows, axis=0, keepdims=True) * (1.0 / hd) + EPS)
        return rows * inv, inv

    root = 1.0 / math.sqrt(hd)
    q_gain = qg_ref[...] * (root * LOG2E)
    k_gain = kg_ref[...]
    q_back = qg_ref[...] * root
    k_back = kg_ref[...] * (1.0 / LOG2E)
    q_all, k_all, v_all = project(0), project(1), project(2)

    spot = lax.broadcasted_iota(jnp.int32, (patches, tokens), 0)
    token = lax.broadcasted_iota(jnp.int32, (patches, tokens), 1)
    spots = jnp.where(lax.rem(token, patches) == spot, 16.0, 0.0)
    top = lax.broadcasted_iota(jnp.int32, (8, tokens), 0) == 0
    spare = -(hd + patches + 8) % LANES
    zeros = jnp.zeros((spare, tokens), F32)
    q_tail = [spots, jnp.where(top, 16.0, 0.0), zeros]
    k_tail = [spots, jnp.where(top, -16.0, 0.0), zeros]
    ones = jnp.where(top, 1.0, 0.0)
    blank = jnp.zeros((-hd % LANES, tokens), F32)

    def back(hat, inv, gain, grad):
        weighted = grad * gain
        mean = jnp.sum(hat * weighted, axis=0, keepdims=True) * (1.0 / hd)
        return inv * (weighted - hat * mean)

    def put(part, h, rows):
        start = part * hw + h * hd
        rows_s[start : start + hd, :] = rows

    for pair in range(heads // 2):
        hats, tall = [], []
        for h in (2 * pair, 2 * pair + 1):
            at = slice(h * hd, (h + 1) * hd)
            hats.append((norm(q_all[at]), norm(k_all[at])))
            kn = hats[-1][1][0] * k_gain
            tall.append((jnp.concatenate([kn] + k_tail), jnp.concatenate([v_all[at], blank])))
        k_rows = mm(ident, jnp.concatenate([t[0] for t in tall]).astype(BF), NT).astype(BF)
        v_rows = mm(ident, jnp.concatenate([t[1] for t in tall]).astype(BF), NT).astype(BF)
        for i, h in enumerate((2 * pair, 2 * pair + 1)):
            at = slice(h * hd, (h + 1) * hd)
            lanes = slice(i * LANES, (i + 1) * LANES)
            (q_hat, q_inv), (k_hat, k_inv) = hats[i]
            q_b = jnp.concatenate([q_hat * q_gain] + q_tail).astype(BF)
            k_b = (k_hat * k_gain).astype(BF)
            weights = jnp.exp2(mm(k_rows[:, lanes], q_b, NN))
            w_b = weights.astype(BF)
            v_b = jnp.concatenate([v_all[at], ones]).astype(BF)
            summed = mm(v_b, w_b, NN)
            share = 1.0 / summed[hd : hd + 1]
            out = summed[:hd] * share
            ot_s[at, :] = out
            cot = cot_t[at]
            cot_share = cot * share
            cot_b = jnp.concatenate([cot_share, blank]).astype(BF)
            delta = jnp.sum(out * cot_share, axis=0, keepdims=True)
            grad_s = (weights * (mm(v_rows[:, lanes], cot_b, NN) - delta)).astype(BF)
            put(2, h, mm(cot_b, w_b, NT)[:hd])
            put(0, h, back(q_hat, q_inv, q_back, mm(k_b, grad_s, NN)))
            put(1, h, back(k_hat, k_inv, k_back, mm(q_b, grad_s, NT)[:hd]))

    grad = jnp.zeros((tokens, width), F32)
    size = gp_keep_ref.shape[0]
    for part in range(3):
        at = slice(part * hw, (part + 1) * hw)
        block = rows_s[at, :].astype(BF)
        gp_s[at, :] = block
        grad = grad + mm(mm(ident, block, NT).astype(BF), wt_s[at, :], NN)
    gp_keep_ref[...] = gp_s[pl.ds(pl.multiple_of(core_ref[0] * size, ROWS), size), :]
    gp_send_ref[...] = gp_s[pl.ds(pl.multiple_of((1 - core_ref[0]) * size, ROWS), size), :]
    att_ref[...] = mm(ident, ot_s[...].astype(BF), NT).astype(BF)

    half = width // 2
    win = send_ref.shape[1]
    scaled = grad * factor
    first = jnp.sum(scaled, axis=1, keepdims=True)
    second = jnp.sum(scaled * unit, axis=1, keepdims=True)
    mine_low = which_ref[0] == 0
    col = lax.broadcasted_iota(jnp.int32, (tokens, win), 1)
    here = jnp.where(mine_low, half, 0)
    there = jnp.where(mine_low, 0, half)
    low, high = scaled[:, :win], scaled[:, width - win :]
    send = jnp.where(mine_low, high, low)
    keep = jnp.where(mine_low, low, high)
    for place, term in enumerate((first, second)):
        coarse = term.astype(BF).astype(F32)
        send = jnp.where(col == there + 2 * place, coarse, send)
        send = jnp.where(col == there + 2 * place + 1, term - coarse, send)
    for place, term in enumerate((first, second, inverse)):
        keep = jnp.where(col == here + place, term, keep)
    send_ref[...] = send.astype(BF)
    keep_ref[...] = keep
    unit_ref[...] = jnp.where(mine_low, unit[:, :win], unit[:, width - win :]).astype(BF)


def attend(core, which, x, shift, scale, wt, qg, kg, patches, heads, hd):
    tokens = x.shape[0]
    width = wt.shape[1]
    hw = heads * hd
    win = window_of(width // 2)
    smem = pl.BlockSpec(memory_space=pltpu.SMEM)
    vmem = pl.BlockSpec(memory_space=pltpu.VMEM)
    shapes = [
        ((tokens, width), BF),
        ((3 * hw // 2, tokens), BF),
        ((3 * hw // 2, tokens), BF),
        ((tokens, hw), BF),
        ((tokens, win), BF),
        ((tokens, win), F32),
        ((tokens, win), BF),
    ]
    return pl.pallas_call(
        functools.partial(attend_kernel, patches=patches, heads=heads, hd=hd),
        in_specs=[smem, smem, vmem, vmem, vmem, pl.BlockSpec(memory_space=pl.ANY), vmem, vmem],
        out_shape=tuple(jax.ShapeDtypeStruct(*shape) for shape in shapes),
        scratch_shapes=[
            pltpu.VMEM((3 * hw, width), BF),
            pltpu.VMEM((3 * hw, tokens), BF),
            pltpu.VMEM((hw, tokens), F32),
            pltpu.VMEM((3 * hw, tokens), F32),
            pltpu.SemaphoreType.DMA((3,)),
        ],
        compiler_params=pltpu.CompilerParams(vmem_limit_bytes=32 * 2**20),
        name="attend",
    )(core, which, x, shift, scale, wt, qg, kg)


def outer_kernel(where_ref, gp_a, gp_b, mod_a, mod_b, *refs):
    out_refs, tiles_s = refs[:-1], refs[-1]
    rows, width = gp_a.shape[0], mod_a.shape[1]
    tiles = rows // ROWS
    used = tiles * (width // LANES)
    tiles_s[used:] = jnp.zeros((tiles_s.shape[0] - used, ROWS, LANES), BF)
    gp = jnp.concatenate([gp_a[...], gp_b[...]], axis=1)
    for start in range(0, width, 2 * LANES):
        stop = min(start + 2 * LANES, width)
        mod = jnp.concatenate([mod_a[:, start:stop], mod_b[:, start:stop]], axis=0)
        found = mm(gp, mod, NN).astype(BF)
        for at in range(0, stop - start, LANES):
            j = (start + at) // LANES
            tiles_s[j * tiles : (j + 1) * tiles] = found[:, at : at + LANES].reshape(tiles, ROWS, LANES)
    size = out_refs[0].shape[0]
    for k, out_ref in enumerate(out_refs):
        out_ref[...] = tiles_s[pl.ds((where_ref[0] ^ k) * size, size)]


def outer(where, gp_a, gp_b, mod_a, mod_b, count, padded):
    smem = pl.BlockSpec(memory_space=pltpu.SMEM)
    vmem = pl.BlockSpec(memory_space=pltpu.VMEM)
    shape = jax.ShapeDtypeStruct((padded // count, ROWS, LANES), BF)
    return pl.pallas_call(
        outer_kernel,
        in_specs=[smem] + [vmem] * 4,
        out_shape=(shape,) * count,
        scratch_shapes=[pltpu.VMEM((padded, ROWS, LANES), BF)],
        compiler_params=pltpu.CompilerParams(vmem_limit_bytes=16 * 2**20),
        name="outer",
    )(where, gp_a, gp_b, mod_a, mod_b)


def window_of(half):
    return -(-half // LANES) * LANES


def finish_kernel(which_ref, recv_ref, keep_ref, unit_ref, att_ref, out_ref, *, width):
    half = width // 2
    win = recv_ref.shape[1]
    mine_low = which_ref[0] == 0
    recv = recv_ref[...].astype(F32)
    keep = keep_ref[...]

    def column(block, place):
        return jnp.where(mine_low, block[:, half + place : half + place + 1], block[:, place : place + 1])

    first = column(keep, 0) + (column(recv, 0) + column(recv, 1))
    second = column(keep, 1) + (column(recv, 2) + column(recv, 3))
    inverse = column(keep, 2)
    grad = keep + recv
    out = inverse * (grad - first * (1.0 / width) - unit_ref[...].astype(F32) * (second * (1.0 / width)))
    moved = pltpu.roll(out, win - (win - half), 1)
    out_ref[:, :half] = jnp.where(mine_low, out, moved)[:, :half].astype(BF)
    out_ref[:, half:] = att_ref[...]


def finish(which, recv, keep, unit, att, width):
    tokens = recv.shape[0]
    smem = pl.BlockSpec(memory_space=pltpu.SMEM)
    vmem = pl.BlockSpec(memory_space=pltpu.VMEM)
    return pl.pallas_call(
        functools.partial(finish_kernel, width=width),
        in_specs=[smem, vmem, vmem, vmem, vmem],
        out_shape=jax.ShapeDtypeStruct((tokens, width), BF),
        compiler_params=pltpu.CompilerParams(vmem_limit_bytes=24 * 2**20),
        name="finish",
    )(which, recv, keep, unit, att)


def sum_kernel(*refs):
    total = refs[0][...].astype(F32)
    for ref in refs[1:-1]:
        total = total + ref[...].astype(F32)
    refs[-1][...] = total.astype(BF)


def sum_of(parts):
    return pl.pallas_call(
        sum_kernel,
        out_shape=jax.ShapeDtypeStruct(parts[0].shape, BF),
        compiler_params=pltpu.CompilerParams(vmem_limit_bytes=8 * 2**20),
        name="sum_of",
    )(*parts)


def spread_kernel(parts_ref, out_ref, *, factor):
    total = jnp.sum(parts_ref[...].astype(F32), axis=0) * factor
    total = total.astype(BF)
    for k in range(out_ref.shape[0]):
        out_ref[k] = total


def spread(parts, factor):
    return pl.pallas_call(
        functools.partial(spread_kernel, factor=factor),
        out_shape=jax.ShapeDtypeStruct(parts.shape, BF),
        compiler_params=pltpu.CompilerParams(vmem_limit_bytes=8 * 2**20),
        name="spread",
    )(parts)


def untile_kernel(where_ref, half_ref, *refs):
    pieces, (out_ref, tiles_s) = refs[:-2], refs[-2:]
    count = len(pieces) // 2
    size = pieces[0].shape[0]
    for side in range(2):
        half = half_ref[0] ^ side
        for k in range(count):
            base = (half * count + (where_ref[0] ^ k)) * size
            tiles_s[pl.ds(base, size)] = pieces[side * count + k][...]
    rows = out_ref.shape[0] // 2
    tiles = rows // ROWS
    for half in range(2):
        for j in range(out_ref.shape[1] // LANES):
            start = half * count * size + j * tiles
            block = tiles_s[start : start + tiles].reshape(rows, LANES)
            out_ref[half * rows : (half + 1) * rows, j * LANES : (j + 1) * LANES] = block


def untile(where, half, pieces, rows, width):
    smem = pl.BlockSpec(memory_space=pltpu.SMEM)
    vmem = pl.BlockSpec(memory_space=pltpu.VMEM)
    tiles = len(pieces) * pieces[0].shape[0]
    return pl.pallas_call(
        untile_kernel,
        in_specs=[smem, smem] + [vmem] * len(pieces),
        out_shape=jax.ShapeDtypeStruct((rows, width), BF),
        scratch_shapes=[pltpu.VMEM((tiles, ROWS, LANES), BF)],
        compiler_params=pltpu.CompilerParams(vmem_limit_bytes=16 * 2**20),
        name="untile",
    )(where, half, *pieces)


def swap(x, axes, k):
    count = math.prod(lax.axis_size(a) for a in axes)
    return lax.ppermute(x, axes, [(i, i ^ k) for i in range(count)])


def exchange(x, axis):
    parts = x.reshape((-1,) + x.shape[-3:])
    return lax.all_to_all(parts, axis, split_axis=0, concat_axis=0, tiled=True)


def plane_size():
    return lax.axis_size("xlo") * lax.axis_size("y")


ORDER = (6, 2, 5, 7, 4, 1, 3)


def scatter_plane(parts):
    return [parts[0]] + [swap(parts[k], PLANE, k) for k in ORDER]


def sum_clips(own, factor):
    clips = lax.axis_size("dp")
    parts = own.reshape((clips, own.shape[0] // clips) + own.shape[1:])
    return exchange(spread(exchange(parts, "dp"), factor), "dp").reshape(own.shape)


def gather_plane(own, rows, width):
    where = lax.axis_index(PLANE).astype(jnp.int32).reshape(1)
    half = lax.axis_index("core").astype(jnp.int32).reshape(1)
    found = {k: swap(own, PLANE, k) for k in ORDER}
    pieces = [own] + [found[k] for k in range(1, plane_size())]
    pieces = pieces + [swap(piece, ("core",), 1) for piece in pieces]
    return untile(where, half, pieces, rows, width)


def body(latent, mod_shift, mod_scale, w_qkv, q_gain, k_gain, cotangent):
    _, _, patches, width = latent.shape
    hw = w_qkv.shape[2]
    hd = q_gain.shape[0]
    heads = hw // hd
    frames = 1
    for a in SEQ:
        frames *= lax.axis_size(a)
    own_patches = patches // frames
    clips = lax.axis_size("dp")
    wt = w_qkv.transpose(1, 2, 0).reshape(3 * hw, width)
    x = pack(latent[0, 0], cotangent[0, 0].T).reshape(frames, own_patches, width + hw)
    x = lax.all_to_all(x, SEQ, split_axis=0, concat_axis=0, tiled=True).reshape(patches, width + hw)
    core = lax.axis_index("core").astype(jnp.int32).reshape(1)
    which = lax.axis_index("tensor").astype(jnp.int32).reshape(1)
    where = lax.axis_index(PLANE).astype(jnp.int32).reshape(1)
    mod, gp_keep, gp_send, att, send, keep, unit = attend(
        core, which, x, mod_shift, mod_scale, wt, q_gain[:, None], k_gain[:, None], own_patches, heads, hd
    )
    recv = lax.ppermute(send, "tensor", [(0, 1), (1, 0)])
    used = (3 * hw // 2 // ROWS) * (width // LANES)
    group = plane_size() * clips
    padded = -(-used // group) * group
    gp_other, mod_other = swap(gp_send, ("core",), 1), swap(mod, ("core",), 1)
    parts = scatter_plane(outer(where, gp_keep, gp_other, mod, mod_other, plane_size(), padded))
    parts, recv = lax.optimization_barrier((parts, recv))
    home = finish(which, recv, keep, unit, att, width)
    own, home = lax.optimization_barrier((sum_of(parts), home))
    home = home.reshape(frames, own_patches, width)
    home = lax.all_to_all(home, SEQ, split_axis=0, concat_axis=0, tiled=True)
    grad_t, att_t = unpack(home.reshape(patches, width))
    factor = 1.0 / math.sqrt(clips * frames * patches)
    grad_qkv = gather_plane(sum_clips(own, factor), 3 * hw, width)
    grad_qkv = grad_qkv.reshape(3, hw, width).transpose(2, 0, 1)
    return (att_t.T[None, None], grad_t.T[None, None], grad_qkv)


def solution(mesh):
    fine = Mesh(mesh.devices.reshape(mesh.shape["dp"], 2, 4, 2, 2), ("dp",) + SEQ + ("tensor",))
    in_specs = (
        P("dp", SEQ, None, None),
        P("dp", None),
        P("dp", None),
        P(None, None, "tensor"),
        P(),
        P(),
        P("dp", SEQ, None, "tensor"),
    )
    out_specs = (
        P("dp", SEQ, None, "tensor"),
        P("dp", SEQ, None, "tensor"),
        P(None, None, "tensor"),
    )
    return jax.shard_map(body, mesh=fine, in_specs=in_specs, out_specs=out_specs, check_vma=False)
```

```python
import functools
import math

import jax
import jax.numpy as jnp
from jax import lax
from jax.experimental import pallas as pl
from jax.experimental.pallas import tpu as pltpu
from jax.sharding import Mesh, PartitionSpec as P

BF = jnp.bfloat16
F32 = jnp.float32
EPS = 1e-06
NN = (((1,), (0,)), ((), ()))
NT = (((1,), (1,)), ((), ()))
LOG2E = math.log2(math.e)
ROWS, LANES = 16, 128
PLANE = ("xlo", "y")
SEQ = PLANE + ("core",)


def mm(a, b, dims):
    return lax.dot_general(a, b, dims, preferred_element_type=F32)


def eye(n):
    rows = lax.broadcasted_iota(jnp.int32, (n, n), 0)
    cols = lax.broadcasted_iota(jnp.int32, (n, n), 1)
    return jnp.where(rows == cols, 1.0, 0.0).astype(BF)


def pack_kernel(latent_ref, cot_ref, out_ref):
    width = latent_ref.shape[1]
    out_ref[:, :width] = latent_ref[...]
    out_ref[:, width:] = mm(eye(latent_ref.shape[0]), cot_ref[...], NT).astype(BF)


def pack(latent, cot_t):
    tokens, width = latent.shape
    return pl.pallas_call(
        pack_kernel,
        out_shape=jax.ShapeDtypeStruct((tokens, width + cot_t.shape[0]), BF),
        compiler_params=pltpu.CompilerParams(vmem_limit_bytes=8 * 2**20),
        name="pack",
    )(latent, cot_t)


def unpack_kernel(rows_ref, first_ref, second_ref):
    ident = eye(LANES)
    half = first_ref.shape[0]
    for start in range(0, 2 * half, LANES):
        found = mm(ident, rows_ref[:, start : start + LANES], NT).astype(BF)
        cut = min(max(half - start, 0), LANES)
        if cut:
            first_ref[start : start + cut] = found[:cut]
        if cut < LANES:
            second_ref[start + cut - half : start + LANES - half] = found[cut:]


def unpack(rows):
    tokens, width = rows.shape
    shape = jax.ShapeDtypeStruct((width // 2, tokens), BF)
    return pl.pallas_call(
        unpack_kernel,
        out_shape=(shape, shape),
        compiler_params=pltpu.CompilerParams(vmem_limit_bytes=8 * 2**20),
        name="unpack",
    )(rows)


def unit_of(values):
    width = values.shape[1]
    centred = values - jnp.sum(values, axis=1, keepdims=True) * (1.0 / width)
    inverse = lax.rsqrt(jnp.sum(centred * centred, axis=1, keepdims=True) * (1.0 / width) + EPS)
    return centred * inverse, inverse


def attend_kernel(core_ref, which_ref, x_ref, shift_ref, scale_ref, wt_hbm, qg_ref, kg_ref,
                  mod_ref, gp_keep_ref, gp_send_ref, att_ref, send_ref, keep_ref, unit_ref,
                  wt_s, gp_s, ot_s, rows_s, sems, *, patches, heads, hd):
    tokens, _ = x_ref.shape
    width = scale_ref.shape[1]
    hw = heads * hd
    copies = []
    for part in range(3):
        rows = pl.ds(part * hw, hw)
        copy = pltpu.make_async_copy(wt_hbm.at[rows], wt_s.at[rows], sems.at[part])
        copy.start()
        copies.append(copy)
    unit, inverse = unit_of(x_ref[:, :width].astype(F32))
    factor = 1.0 + scale_ref[...]
    mod_ref[...] = (unit * factor + shift_ref[...]).astype(BF)
    mod = mod_ref[...]
    ident = eye(tokens)
    cot_t = mm(eye(hw), x_ref[:, width:], NT)

    def project(part):
        copies[part].wait()
        rows = mm(wt_s[part * hw : (part + 1) * hw, :], mod, NT)
        return rows.astype(BF).astype(F32)

    def norm(rows):
        inv = lax.rsqrt(jnp.sum(rows * rows, axis=0, keepdims=True) * (1.0 / hd) + EPS)
        return rows * inv, inv

    root = 1.0 / math.sqrt(hd)
    q_gain = qg_ref[...] * (root * LOG2E)
    k_gain = kg_ref[...]
    q_back = qg_ref[...] * root
    k_back = kg_ref[...] * (1.0 / LOG2E)
    q_all, k_all, v_all = project(0), project(1), project(2)

    spot = lax.broadcasted_iota(jnp.int32, (patches, tokens), 0)
    token = lax.broadcasted_iota(jnp.int32, (patches, tokens), 1)
    spots = jnp.where(lax.rem(token, patches) == spot, 16.0, 0.0)
    top = lax.broadcasted_iota(jnp.int32, (8, tokens), 0) == 0
    spare = -(hd + patches + 8) % LANES
    zeros = jnp.zeros((spare, tokens), F32)
    q_tail = [spots, jnp.where(top, 16.0, 0.0), zeros]
    k_tail = [spots, jnp.where(top, -16.0, 0.0), zeros]
    ones = jnp.where(top, 1.0, 0.0)
    blank = jnp.zeros((-hd % LANES, tokens), F32)

    def back(hat, inv, gain, grad):
        weighted = grad * gain
        mean = jnp.sum(hat * weighted, axis=0, keepdims=True) * (1.0 / hd)
        return inv * (weighted - hat * mean)

    def put(part, h, rows):
        start = part * hw + h * hd
        rows_s[start : start + hd, :] = rows

    for pair in range(heads // 2):
        hats, tall = [], []
        for h in (2 * pair, 2 * pair + 1):
            at = slice(h * hd, (h + 1) * hd)
            hats.append((norm(q_all[at]), norm(k_all[at])))
            kn = hats[-1][1][0] * k_gain
            tall.append((jnp.concatenate([kn] + k_tail), jnp.concatenate([v_all[at], blank])))
        k_rows = mm(ident, jnp.concatenate([t[0] for t in tall]).astype(BF), NT).astype(BF)
        v_rows = mm(ident, jnp.concatenate([t[1] for t in tall]).astype(BF), NT).astype(BF)
        for i, h in enumerate((2 * pair, 2 * pair + 1)):
            at = slice(h * hd, (h + 1) * hd)
            lanes = slice(i * LANES, (i + 1) * LANES)
            (q_hat, q_inv), (k_hat, k_inv) = hats[i]
            q_b = jnp.concatenate([q_hat * q_gain] + q_tail).astype(BF)
            k_b = (k_hat * k_gain).astype(BF)
            weights = jnp.exp2(mm(k_rows[:, lanes], q_b, NN))
            w_b = weights.astype(BF)
            v_b = jnp.concatenate([v_all[at], ones]).astype(BF)
            summed = mm(v_b, w_b, NN)
            share = 1.0 / summed[hd : hd + 1]
            out = summed[:hd] * share
            ot_s[at, :] = out
            cot = cot_t[at]
            cot_share = cot * share
            cot_b = jnp.concatenate([cot_share, blank]).astype(BF)
            delta = jnp.sum(out * cot_share, axis=0, keepdims=True)
            grad_s = (weights * (mm(v_rows[:, lanes], cot_b, NN) - delta)).astype(BF)
            put(2, h, mm(cot_b, w_b, NT)[:hd])
            put(0, h, back(q_hat, q_inv, q_back, mm(k_b, grad_s, NN)))
            put(1, h, back(k_hat, k_inv, k_back, mm(q_b, grad_s, NT)[:hd]))

    grad = jnp.zeros((tokens, width), F32)
    size = gp_keep_ref.shape[0]
    for part in range(3):
        at = slice(part * hw, (part + 1) * hw)
        block = rows_s[at, :].astype(BF)
        gp_s[at, :] = block
        grad = grad + mm(mm(ident, block, NT).astype(BF), wt_s[at, :], NN)
    gp_keep_ref[...] = gp_s[pl.ds(pl.multiple_of(core_ref[0] * size, ROWS), size), :]
    gp_send_ref[...] = gp_s[pl.ds(pl.multiple_of((1 - core_ref[0]) * size, ROWS), size), :]
    att_ref[...] = mm(ident, ot_s[...].astype(BF), NT).astype(BF)

    half = width // 2
    win = send_ref.shape[1]
    scaled = grad * factor
    first = jnp.sum(scaled, axis=1, keepdims=True)
    second = jnp.sum(scaled * unit, axis=1, keepdims=True)
    mine_low = which_ref[0] == 0
    col = lax.broadcasted_iota(jnp.int32, (tokens, win), 1)
    here = jnp.where(mine_low, half, 0)
    there = jnp.where(mine_low, 0, half)
    low, high = scaled[:, :win], scaled[:, width - win :]
    send = jnp.where(mine_low, high, low)
    keep = jnp.where(mine_low, low, high)
    for place, term in enumerate((first, second)):
        coarse = term.astype(BF).astype(F32)
        send = jnp.where(col == there + 2 * place, coarse, send)
        send = jnp.where(col == there + 2 * place + 1, term - coarse, send)
    for place, term in enumerate((first, second, inverse)):
        keep = jnp.where(col == here + place, term, keep)
    send_ref[...] = send.astype(BF)
    keep_ref[...] = keep
    unit_ref[...] = jnp.where(mine_low, unit[:, :win], unit[:, width - win :]).astype(BF)


def attend(core, which, x, shift, scale, wt, qg, kg, patches, heads, hd):
    tokens = x.shape[0]
    width = wt.shape[1]
    hw = heads * hd
    win = window_of(width // 2)
    smem = pl.BlockSpec(memory_space=pltpu.SMEM)
    vmem = pl.BlockSpec(memory_space=pltpu.VMEM)
    shapes = [
        ((tokens, width), BF),
        ((3 * hw // 2, tokens), BF),
        ((3 * hw // 2, tokens), BF),
        ((tokens, hw), BF),
        ((tokens, win), BF),
        ((tokens, win), F32),
        ((tokens, win), BF),
    ]
    return pl.pallas_call(
        functools.partial(attend_kernel, patches=patches, heads=heads, hd=hd),
        in_specs=[smem, smem, vmem, vmem, vmem, pl.BlockSpec(memory_space=pl.ANY), vmem, vmem],
        out_shape=tuple(jax.ShapeDtypeStruct(*shape) for shape in shapes),
        scratch_shapes=[
            pltpu.VMEM((3 * hw, width), BF),
            pltpu.VMEM((3 * hw, tokens), BF),
            pltpu.VMEM((hw, tokens), F32),
            pltpu.VMEM((3 * hw, tokens), F32),
            pltpu.SemaphoreType.DMA((3,)),
        ],
        compiler_params=pltpu.CompilerParams(vmem_limit_bytes=32 * 2**20),
        name="attend",
    )(core, which, x, shift, scale, wt, qg, kg)


def outer_kernel(where_ref, gp_a, gp_b, mod_a, mod_b, *refs):
    out_refs, tiles_s = refs[:-1], refs[-1]
    rows, width = gp_a.shape[0], mod_a.shape[1]
    tiles = rows // ROWS
    used = tiles * (width // LANES)
    tiles_s[used:] = jnp.zeros((tiles_s.shape[0] - used, ROWS, LANES), BF)
    gp = jnp.concatenate([gp_a[...], gp_b[...]], axis=1)
    for start in range(0, width, 2 * LANES):
        stop = min(start + 2 * LANES, width)
        mod = jnp.concatenate([mod_a[:, start:stop], mod_b[:, start:stop]], axis=0)
        found = mm(gp, mod, NN).astype(BF)
        for at in range(0, stop - start, LANES):
            j = (start + at) // LANES
            tiles_s[j * tiles : (j + 1) * tiles] = found[:, at : at + LANES].reshape(tiles, ROWS, LANES)
    size = tiles_s.shape[0] // 8
    for (lo, hi), order, send_ref, keep_ref in zip(bounds(size), ORDERS, out_refs[::2], out_refs[1::2]):
        for q in range(4):
            k = picked(q, order[1:])
            at = (where_ref[0] ^ k) * size + lo
            keep_ref[q] = tiles_s[pl.ds(at, hi - lo)]
            at = (where_ref[0] ^ (k ^ order[0])) * size + lo
            send_ref[q] = tiles_s[pl.ds(at, hi - lo)]


def outer(where, gp_a, gp_b, mod_a, mod_b, padded):
    smem = pl.BlockSpec(memory_space=pltpu.SMEM)
    vmem = pl.BlockSpec(memory_space=pltpu.VMEM)
    shapes = [jax.ShapeDtypeStruct((4, hi - lo, ROWS, LANES), BF) for lo, hi in bounds(padded // 8)]
    return pl.pallas_call(
        outer_kernel,
        in_specs=[smem] + [vmem] * 4,
        out_shape=tuple(shape for shape in shapes for _ in range(2)),
        scratch_shapes=[pltpu.VMEM((padded, ROWS, LANES), BF)],
        compiler_params=pltpu.CompilerParams(vmem_limit_bytes=16 * 2**20),
        name="outer",
    )(where, gp_a, gp_b, mod_a, mod_b)


ORDERS = ((1, 3, 4), (3, 4, 1), (4, 1, 3))


def bounds(size):
    cuts = [0, -(-size // 3), -(-2 * size // 3), size]
    return list(zip(cuts[:-1], cuts[1:]))


def picked(q, masks):
    return (masks[0] if q % 2 else 0) ^ (masks[1] if q // 2 else 0)


def window_of(half):
    return -(-half // LANES) * LANES


def finish_kernel(which_ref, recv_ref, keep_ref, unit_ref, att_ref, out_ref, *, width):
    half = width // 2
    win = recv_ref.shape[1]
    mine_low = which_ref[0] == 0
    recv = recv_ref[...].astype(F32)
    keep = keep_ref[...]

    def column(block, place):
        return jnp.where(mine_low, block[:, half + place : half + place + 1], block[:, place : place + 1])

    first = column(keep, 0) + (column(recv, 0) + column(recv, 1))
    second = column(keep, 1) + (column(recv, 2) + column(recv, 3))
    inverse = column(keep, 2)
    grad = keep + recv
    out = inverse * (grad - first * (1.0 / width) - unit_ref[...].astype(F32) * (second * (1.0 / width)))
    moved = pltpu.roll(out, win - (win - half), 1)
    out_ref[:, :half] = jnp.where(mine_low, out, moved)[:, :half].astype(BF)
    out_ref[:, half:] = att_ref[...]


def finish(which, recv, keep, unit, att, width):
    tokens = recv.shape[0]
    smem = pl.BlockSpec(memory_space=pltpu.SMEM)
    vmem = pl.BlockSpec(memory_space=pltpu.VMEM)
    return pl.pallas_call(
        functools.partial(finish_kernel, width=width),
        in_specs=[smem, vmem, vmem, vmem, vmem],
        out_shape=jax.ShapeDtypeStruct((tokens, width), BF),
        compiler_params=pltpu.CompilerParams(vmem_limit_bytes=24 * 2**20),
        name="finish",
    )(which, recv, keep, unit, att)


def fold_kernel(*refs):
    count = len(refs) // 4
    for i in range(count):
        keep_ref, got_ref = refs[2 * i : 2 * i + 2]
        send_ref, left_ref = refs[2 * count + 2 * i : 2 * count + 2 * i + 2]
        for q in range(keep_ref.shape[0]):
            total = (keep_ref[q].astype(F32) + got_ref[q].astype(F32)).astype(BF)
            if q % 2:
                send_ref[q // 2] = total
            else:
                left_ref[q // 2] = total


def fold(pairs):
    shapes = []
    for keep, _ in pairs:
        shapes += [jax.ShapeDtypeStruct((keep.shape[0] // 2,) + keep.shape[1:], BF)] * 2
    found = pl.pallas_call(
        fold_kernel,
        out_shape=tuple(shapes),
        compiler_params=pltpu.CompilerParams(vmem_limit_bytes=8 * 2**20),
        name="fold",
    )(*[x for pair in pairs for x in pair])
    return found[::2], found[1::2]


def close_kernel(*refs):
    out_ref, at = refs[-1], 0
    for keep_ref, got_ref in zip(refs[:-1:2], refs[1:-1:2]):
        count = keep_ref.shape[1]
        out_ref[at : at + count] = (keep_ref[0].astype(F32) + got_ref[0].astype(F32)).astype(BF)
        at += count


def close(pairs):
    count = sum(keep.shape[1] for keep, _ in pairs)
    return pl.pallas_call(
        close_kernel,
        out_shape=jax.ShapeDtypeStruct((count, ROWS, LANES), BF),
        compiler_params=pltpu.CompilerParams(vmem_limit_bytes=8 * 2**20),
        name="close",
    )(*[x for pair in pairs for x in pair])


def join_kernel(*refs):
    count = len(refs) // 3
    for i in range(count):
        have_ref, got_ref, out_ref = refs[2 * i], refs[2 * i + 1], refs[2 * count + i]
        size = have_ref.shape[0]
        out_ref[:size] = have_ref[...]
        out_ref[size:] = got_ref[...]


def join(pairs):
    shapes = [jax.ShapeDtypeStruct((2 * have.shape[0],) + have.shape[1:], BF) for have, _ in pairs]
    return pl.pallas_call(
        join_kernel,
        out_shape=tuple(shapes),
        compiler_params=pltpu.CompilerParams(vmem_limit_bytes=8 * 2**20),
        name="join",
    )(*[x for pair in pairs for x in pair])


def reduce_kernel(parts_ref, out_ref, *, factor):
    out_ref[...] = (jnp.sum(parts_ref[...].astype(F32), axis=0) * factor).astype(BF)


def reduce(parts, factor):
    return pl.pallas_call(
        functools.partial(reduce_kernel, factor=factor),
        out_shape=jax.ShapeDtypeStruct(parts.shape[1:], BF),
        compiler_params=pltpu.CompilerParams(vmem_limit_bytes=4 * 2**20),
        name="reduce",
    )(parts)


def place_kernel(clip_ref, *refs):
    clips = len(refs) - 4
    pieces, out_refs, all_s = refs[:clips], refs[clips:-1], refs[-1]
    size = pieces[0].shape[0]
    for shift, piece in enumerate(pieces):
        all_s[pl.ds(lax.rem(clip_ref[0] + shift, clips) * size, size)] = piece[...]
    for (lo, hi), out_ref in zip(bounds(clips * size), out_refs):
        out_ref[0] = all_s[lo:hi]


def place(clip, pieces):
    total = len(pieces) * pieces[0].shape[0]
    smem = pl.BlockSpec(memory_space=pltpu.SMEM)
    vmem = pl.BlockSpec(memory_space=pltpu.VMEM)
    return pl.pallas_call(
        place_kernel,
        in_specs=[smem] + [vmem] * len(pieces),
        out_shape=tuple(jax.ShapeDtypeStruct((1, hi - lo, ROWS, LANES), BF) for lo, hi in bounds(total)),
        scratch_shapes=[pltpu.VMEM((total, ROWS, LANES), BF)],
        compiler_params=pltpu.CompilerParams(vmem_limit_bytes=4 * 2**20),
        name="place",
    )(clip, *pieces)


def untile_kernel(where_ref, half_ref, *refs):
    pieces, (out_ref, tiles_s) = refs[:-2], refs[-2:]
    size = tiles_s.shape[0] // 16
    pieces = iter(pieces)
    for side in range(2):
        half = half_ref[0] ^ side
        for far in range(2):
            for (lo, hi), order in zip(bounds(size), ORDERS):
                piece = next(pieces)
                for q in range(4):
                    k = picked(q, (order[2], order[1])) ^ (order[0] * far)
                    at = (half * 8 + (where_ref[0] ^ k)) * size + lo
                    tiles_s[pl.ds(at, hi - lo)] = piece[q]
    rows = out_ref.shape[0] // 2
    tiles = rows // ROWS
    for half in range(2):
        for j in range(out_ref.shape[1] // LANES):
            start = half * 8 * size + j * tiles
            block = tiles_s[start : start + tiles].reshape(rows, LANES)
            out_ref[half * rows : (half + 1) * rows, j * LANES : (j + 1) * LANES] = block


def untile(where, half, pieces, rows, width):
    smem = pl.BlockSpec(memory_space=pltpu.SMEM)
    vmem = pl.BlockSpec(memory_space=pltpu.VMEM)
    tiles = sum(4 * piece.shape[1] for piece in pieces)
    return pl.pallas_call(
        untile_kernel,
        in_specs=[smem, smem] + [vmem] * len(pieces),
        out_shape=jax.ShapeDtypeStruct((rows, width), BF),
        scratch_shapes=[pltpu.VMEM((tiles, ROWS, LANES), BF)],
        compiler_params=pltpu.CompilerParams(vmem_limit_bytes=16 * 2**20),
        name="untile",
    )(where, half, *pieces)


def swap(x, axes, k):
    count = math.prod(lax.axis_size(a) for a in axes)
    return lax.ppermute(x, axes, [(i, i ^ k) for i in range(count)])


def exchange(x, axis):
    parts = x.reshape((-1,) + x.shape[-3:])
    return lax.all_to_all(parts, axis, split_axis=0, concat_axis=0, tiled=True)


def meet(blocks, level):
    return [swap(block, PLANE, order[level]) for block, order in zip(blocks, ORDERS)]


def sum_plane(found):
    send, keep = found[::2], found[1::2]
    send, keep = fold(list(zip(keep, meet(send, 0))))
    send, keep = fold(list(zip(keep, meet(send, 1))))
    return close(list(zip(keep, meet(send, 2))))


def ring(own, axis):
    count = lax.axis_size(axis)
    pieces = [own] * count
    up = down = own
    for step in range(1, count // 2 + 1):
        up = lax.ppermute(up, axis, [(i, (i + 1) % count) for i in range(count)])
        pieces[count - step] = up
        if step < count - step:
            down = lax.ppermute(down, axis, [(i, (i - 1) % count) for i in range(count)])
            pieces[step] = down
    return pieces


def gather_plane(have, where, half, rows, width):
    have = join(list(zip(have, meet(have, 2))))
    have = join(list(zip(have, meet(have, 1))))
    pieces = list(have) + meet(have, 0)
    pieces = pieces + [swap(piece, ("core",), 1) for piece in pieces]
    return untile(where, half, pieces, rows, width)


def body(latent, mod_shift, mod_scale, w_qkv, q_gain, k_gain, cotangent):
    _, _, patches, width = latent.shape
    hw = w_qkv.shape[2]
    hd = q_gain.shape[0]
    heads = hw // hd
    frames = 1
    for a in SEQ:
        frames *= lax.axis_size(a)
    own_patches = patches // frames
    clips = lax.axis_size("dp")
    wt = w_qkv.transpose(1, 2, 0).reshape(3 * hw, width)
    x = pack(latent[0, 0], cotangent[0, 0].T).reshape(frames, own_patches, width + hw)
    x = lax.all_to_all(x, SEQ, split_axis=0, concat_axis=0, tiled=True).reshape(patches, width + hw)
    core = lax.axis_index("core").astype(jnp.int32).reshape(1)
    which = lax.axis_index("tensor").astype(jnp.int32).reshape(1)
    where = lax.axis_index(PLANE).astype(jnp.int32).reshape(1)
    mod, gp_keep, gp_send, att, send, keep, unit = attend(
        core, which, x, mod_shift, mod_scale, wt, q_gain[:, None], k_gain[:, None], own_patches, heads, hd
    )
    used = (3 * hw // 2 // ROWS) * (width // LANES)
    group = 8 * clips
    padded = -(-used // group) * group
    gp_other, mod_other = swap(gp_send, ("core",), 1), swap(mod, ("core",), 1)
    own = sum_plane(outer(where, gp_keep, gp_other, mod, mod_other, padded))
    own, send = lax.optimization_barrier((own, send))
    recv = lax.ppermute(send, "tensor", [(0, 1), (1, 0)])
    own = exchange(own.reshape((clips, own.shape[0] // clips) + own.shape[1:]), "dp")
    own, recv = lax.optimization_barrier((own, recv))
    own = reduce(own, 1.0 / math.sqrt(clips * frames * patches))
    home = finish(which, recv, keep, unit, att, width).reshape(frames, own_patches, width)
    home = lax.all_to_all(home, SEQ, split_axis=0, concat_axis=0, tiled=True)
    pieces, home = lax.optimization_barrier((ring(own, "dp"), home))
    grad_t, att_t = unpack(home.reshape(patches, width))
    have = place(lax.axis_index("dp").astype(jnp.int32).reshape(1), pieces)
    grad_qkv = gather_plane(have, where, core, 3 * hw, width)
    grad_qkv = grad_qkv.reshape(3, hw, width).transpose(2, 0, 1)
    return (att_t.T[None, None], grad_t.T[None, None], grad_qkv)


def solution(mesh):
    fine = Mesh(mesh.devices.reshape(mesh.shape["dp"], 2, 4, 2, 2), ("dp",) + SEQ + ("tensor",))
    in_specs = (
        P("dp", SEQ, None, None),
        P("dp", None),
        P("dp", None),
        P(None, None, "tensor"),
        P(),
        P(),
        P("dp", SEQ, None, "tensor"),
    )
    out_specs = (
        P("dp", SEQ, None, "tensor"),
        P("dp", SEQ, None, "tensor"),
        P(None, None, "tensor"),
    )
    return jax.shard_map(body, mesh=fine, in_specs=in_specs, out_specs=out_specs, check_vma=False)
```

```python
import functools
import math

import jax
import jax.numpy as jnp
from jax import lax
from jax.experimental import pallas as pl
from jax.experimental.pallas import tpu as pltpu
from jax.sharding import Mesh, PartitionSpec as P

BF = jnp.bfloat16
F32 = jnp.float32
EPS = 1e-06
NN = (((1,), (0,)), ((), ()))
NT = (((1,), (1,)), ((), ()))
LOG2E = math.log2(math.e)
ROWS, LANES = 16, 128
PLANE = ("xlo", "y")
SEQ = PLANE + ("core",)


def mm(a, b, dims):
    return lax.dot_general(a, b, dims, preferred_element_type=F32)


def eye(n):
    rows = lax.broadcasted_iota(jnp.int32, (n, n), 0)
    cols = lax.broadcasted_iota(jnp.int32, (n, n), 1)
    return jnp.where(rows == cols, 1.0, 0.0).astype(BF)


def fetch(pairs, sems):
    copies = [pltpu.make_async_copy(src, dst, sems.at[i]) for i, (src, dst) in enumerate(pairs)]
    for copy in copies:
        copy.start()
    return copies


def pack_kernel(latent_hbm, cot_hbm, out_ref, latent_s, cot_s, sems):
    width = latent_s.shape[1]
    first, second = fetch([(cot_hbm, cot_s), (latent_hbm, latent_s)], sems)
    ident = eye(latent_s.shape[0])
    first.wait()
    out_ref[:, width:] = mm(ident, cot_s[...], NT).astype(BF)
    second.wait()
    out_ref[:, :width] = latent_s[...]


def pack(latent, cot_t):
    tokens, width = latent.shape
    hbm = pl.BlockSpec(memory_space=pltpu.HBM)
    return pl.pallas_call(
        pack_kernel,
        in_specs=[hbm, hbm],
        out_shape=jax.ShapeDtypeStruct((tokens, width + cot_t.shape[0]), BF),
        scratch_shapes=[
            pltpu.VMEM(latent.shape, BF),
            pltpu.VMEM(cot_t.shape, BF),
            pltpu.SemaphoreType.DMA((2,)),
        ],
        compiler_params=pltpu.CompilerParams(vmem_limit_bytes=60 * 2**20),
        name="pack",
    )(latent, cot_t)


def unpack_kernel(rows_ref, first_ref, second_ref):
    ident = eye(LANES)
    half = first_ref.shape[0]
    for start in range(0, 2 * half, LANES):
        found = mm(ident, rows_ref[:, start : start + LANES], NT).astype(BF)
        cut = min(max(half - start, 0), LANES)
        if cut:
            first_ref[start : start + cut] = found[:cut]
        if cut < LANES:
            second_ref[start + cut - half : start + LANES - half] = found[cut:]


def unpack(rows):
    tokens, width = rows.shape
    shape = jax.ShapeDtypeStruct((width // 2, tokens), BF)
    return pl.pallas_call(
        unpack_kernel,
        out_shape=(shape, shape),
        compiler_params=pltpu.CompilerParams(vmem_limit_bytes=8 * 2**20),
        name="unpack",
    )(rows)


def unit_of(values):
    width = values.shape[1]
    centred = values - jnp.sum(values, axis=1, keepdims=True) * (1.0 / width)
    inverse = lax.rsqrt(jnp.sum(centred * centred, axis=1, keepdims=True) * (1.0 / width) + EPS)
    return centred * inverse, inverse


def attend_kernel(core_ref, which_ref, x_hbm, affine_hbm, wt_hbm, qg_ref, kg_ref,
                  mod_ref, gp_keep_ref, gp_send_ref, send_hbm, keep_hbm,
                  x_ref, affine_ref, wt_s, gp_s, ot_s, rows_s, send_ref, keep_ref,
                  in_sems, out_sems, *, patches, heads, hd):
    tokens, _ = x_ref.shape
    width = affine_ref.shape[1]
    hw = heads * hd
    parts = [pl.ds(part * hw, hw) for part in range(3)]
    copies = fetch(
        [(x_hbm, x_ref), (affine_hbm, affine_ref)]
        + [(wt_hbm.at[rows], wt_s.at[rows]) for rows in parts],
        in_sems,
    )
    for copy in copies[:2]:
        copy.wait()
    unit, inverse = unit_of(x_ref[:, :width].astype(F32))
    half = width // 2
    win = send_ref.shape[1]
    mine_low = which_ref[0] == 0
    keep_ref[:, win : 2 * win] = jnp.where(mine_low, unit[:, :win], unit[:, width - win :])
    factor = affine_ref[1:2]
    mod_ref[...] = (unit * factor + affine_ref[0:1]).astype(BF)
    mod = mod_ref[...]
    ident = eye(tokens)
    cot_t = mm(eye(hw), x_ref[:, width:], NT)

    def project(part):
        copies[2 + part].wait()
        rows = mm(wt_s[part * hw : (part + 1) * hw, :], mod, NT)
        return rows.astype(BF).astype(F32)

    def norm(rows):
        inv = lax.rsqrt(jnp.sum(rows * rows, axis=0, keepdims=True) * (1.0 / hd) + EPS)
        return rows * inv, inv

    root = 1.0 / math.sqrt(hd)
    q_gain = qg_ref[...] * (root * LOG2E)
    k_gain = kg_ref[...]
    q_back = qg_ref[...] * root
    k_back = kg_ref[...] * (1.0 / LOG2E)
    q_all, k_all, v_all = project(0), project(1), project(2)

    spot = lax.broadcasted_iota(jnp.int32, (patches, tokens), 0)
    token = lax.broadcasted_iota(jnp.int32, (patches, tokens), 1)
    spots = jnp.where(lax.rem(token, patches) == spot, 16.0, 0.0)
    top = lax.broadcasted_iota(jnp.int32, (8, tokens), 0) == 0
    spare = -(hd + patches + 8) % LANES
    zeros = jnp.zeros((spare, tokens), F32)
    q_tail = [spots, jnp.where(top, 16.0, 0.0), zeros]
    k_tail = [spots, jnp.where(top, -16.0, 0.0), zeros]
    ones = jnp.where(top, 1.0, 0.0)
    blank = jnp.zeros((-hd % LANES, tokens), F32)

    def back(hat, inv, gain, grad):
        weighted = grad * gain
        mean = jnp.sum(hat * weighted, axis=0, keepdims=True) * (1.0 / hd)
        return inv * (weighted - hat * mean)

    def put(part, h, rows):
        start = part * hw + h * hd
        rows_s[start : start + hd, :] = rows

    for pair in range(heads // 2):
        hats, tall = [], []
        for h in (2 * pair, 2 * pair + 1):
            at = slice(h * hd, (h + 1) * hd)
            hats.append((norm(q_all[at]), norm(k_all[at])))
            kn = hats[-1][1][0] * k_gain
            tall.append((jnp.concatenate([kn] + k_tail), jnp.concatenate([v_all[at], blank])))
        k_rows = mm(ident, jnp.concatenate([t[0] for t in tall]).astype(BF), NT).astype(BF)
        v_rows = mm(ident, jnp.concatenate([t[1] for t in tall]).astype(BF), NT).astype(BF)
        for i, h in enumerate((2 * pair, 2 * pair + 1)):
            at = slice(h * hd, (h + 1) * hd)
            lanes = slice(i * LANES, (i + 1) * LANES)
            (q_hat, q_inv), (k_hat, k_inv) = hats[i]
            q_b = jnp.concatenate([q_hat * q_gain] + q_tail).astype(BF)
            k_b = (k_hat * k_gain).astype(BF)
            weights = jnp.exp2(mm(k_rows[:, lanes], q_b, NN))
            w_b = weights.astype(BF)
            v_b = jnp.concatenate([v_all[at], ones]).astype(BF)
            summed = mm(v_b, w_b, NN)
            share = 1.0 / summed[hd : hd + 1]
            out = summed[:hd] * share
            ot_s[at, :] = out
            cot = cot_t[at]
            cot_share = cot * share
            cot_b = jnp.concatenate([cot_share, blank]).astype(BF)
            delta = jnp.sum(out * cot_share, axis=0, keepdims=True)
            grad_s = (weights * (mm(v_rows[:, lanes], cot_b, NN) - delta)).astype(BF)
            put(2, h, mm(cot_b, w_b, NT)[:hd])
            put(0, h, back(q_hat, q_inv, q_back, mm(k_b, grad_s, NN)))
            put(1, h, back(k_hat, k_inv, k_back, mm(q_b, grad_s, NT)[:hd]))

    grad = jnp.zeros((tokens, width), F32)
    size = gp_keep_ref.shape[0]
    for part in range(3):
        at = slice(part * hw, (part + 1) * hw)
        block = rows_s[at, :].astype(BF)
        gp_s[at, :] = block
        grad = grad + mm(mm(ident, block, NT).astype(BF), wt_s[at, :], NN)
    scaled = grad * factor
    first = jnp.sum(scaled, axis=1, keepdims=True)
    second = jnp.sum(scaled * unit, axis=1, keepdims=True)
    col = lax.broadcasted_iota(jnp.int32, (tokens, win), 1)
    here = jnp.where(mine_low, half, 0)
    there = jnp.where(mine_low, 0, half)
    low, high = scaled[:, :win], scaled[:, width - win :]
    send = jnp.where(mine_low, high, low)
    keep = jnp.where(mine_low, low, high)
    for place, term in enumerate((first, second)):
        coarse = term.astype(BF).astype(F32)
        send = jnp.where(col == there + 2 * place, coarse, send)
        send = jnp.where(col == there + 2 * place + 1, term - coarse, send)
    for place, term in enumerate((first, second, inverse)):
        keep = jnp.where(col == here + place, term, keep)
    send_ref[...] = send.astype(BF)
    keep_ref[:, :win] = keep
    outs = []
    keep_ref[:, 2 * win : 2 * win + hw] = mm(ident, ot_s[...].astype(BF), NT)
    for i, (src, dst) in enumerate(((send_ref, send_hbm), (keep_ref, keep_hbm))):
        outs.append(pltpu.make_async_copy(src, dst, out_sems.at[i]))
        outs[-1].start()
    gp_keep_ref[...] = gp_s[pl.ds(pl.multiple_of(core_ref[0] * size, ROWS), size), :]
    gp_send_ref[...] = gp_s[pl.ds(pl.multiple_of((1 - core_ref[0]) * size, ROWS), size), :]
    for out in outs:
        out.wait()


def attend(core, which, x, affine, wt, qg, kg, patches, heads, hd):
    tokens = x.shape[0]
    width = wt.shape[1]
    hw = heads * hd
    win = window_of(width // 2)
    smem = pl.BlockSpec(memory_space=pltpu.SMEM)
    vmem = pl.BlockSpec(memory_space=pltpu.VMEM)
    hbm = pl.BlockSpec(memory_space=pltpu.HBM)
    outs = [((tokens, win), BF), ((tokens, 2 * win + window_of(hw)), F32)]
    half = jax.ShapeDtypeStruct((3 * hw // 2, tokens), BF)
    return pl.pallas_call(
        functools.partial(attend_kernel, patches=patches, heads=heads, hd=hd),
        in_specs=[smem, smem] + [hbm] * 3 + [vmem, vmem],
        out_specs=(vmem,) * 3 + (hbm,) * 2,
        out_shape=(jax.ShapeDtypeStruct((tokens, width), BF), half, half)
        + tuple(jax.ShapeDtypeStruct(*out) for out in outs),
        scratch_shapes=[
            pltpu.VMEM(x.shape, BF),
            pltpu.VMEM(affine.shape, F32),
            pltpu.VMEM((3 * hw, width), BF),
            pltpu.VMEM((3 * hw, tokens), BF),
            pltpu.VMEM((hw, tokens), F32),
            pltpu.VMEM((3 * hw, tokens), F32),
        ]
        + [pltpu.VMEM(*out) for out in outs]
        + [pltpu.SemaphoreType.DMA((5,)), pltpu.SemaphoreType.DMA((2,))],
        compiler_params=pltpu.CompilerParams(vmem_limit_bytes=50 * 2**20),
        name="attend",
    )(core, which, x, affine, wt, qg, kg)


def outer_kernel(where_ref, gp_a, gp_b, mod_a, mod_b, *refs):
    out_refs, tiles_s = refs[:-1], refs[-1]
    rows, width = gp_a.shape[0], mod_a.shape[1]
    tiles = rows // ROWS
    used = tiles * (width // LANES)
    tiles_s[used:] = jnp.zeros((tiles_s.shape[0] - used, ROWS, LANES), BF)
    gp = jnp.concatenate([gp_a[...], gp_b[...]], axis=1)
    for start in range(0, width, 2 * LANES):
        stop = min(start + 2 * LANES, width)
        mod = jnp.concatenate([mod_a[:, start:stop], mod_b[:, start:stop]], axis=0)
        found = mm(gp, mod, NN).astype(BF)
        for at in range(0, stop - start, LANES):
            j = (start + at) // LANES
            tiles_s[j * tiles : (j + 1) * tiles] = found[:, at : at + LANES].reshape(tiles, ROWS, LANES)
    size = tiles_s.shape[0] // 8
    for (lo, hi), order, send_ref, keep_ref in zip(bounds(size), ORDERS, out_refs[::2], out_refs[1::2]):
        for q in range(4):
            k = picked(q, order[1:])
            at = (where_ref[0] ^ k) * size + lo
            keep_ref[q] = tiles_s[pl.ds(at, hi - lo)]
            at = (where_ref[0] ^ (k ^ order[0])) * size + lo
            send_ref[q] = tiles_s[pl.ds(at, hi - lo)]


def outer(where, gp_a, gp_b, mod_a, mod_b, padded):
    smem = pl.BlockSpec(memory_space=pltpu.SMEM)
    vmem = pl.BlockSpec(memory_space=pltpu.VMEM)
    shapes = [jax.ShapeDtypeStruct((4, hi - lo, ROWS, LANES), BF) for lo, hi in bounds(padded // 8)]
    return pl.pallas_call(
        outer_kernel,
        in_specs=[smem] + [vmem] * 4,
        out_shape=tuple(shape for shape in shapes for _ in range(2)),
        scratch_shapes=[pltpu.VMEM((padded, ROWS, LANES), BF)],
        compiler_params=pltpu.CompilerParams(vmem_limit_bytes=16 * 2**20),
        name="outer",
    )(where, gp_a, gp_b, mod_a, mod_b)


ORDERS = ((1, 3, 4), (3, 4, 1), (4, 1, 3))


def bounds(size):
    cuts = [0, -(-size // 3), -(-2 * size // 3), size]
    return list(zip(cuts[:-1], cuts[1:]))


def picked(q, masks):
    return (masks[0] if q % 2 else 0) ^ (masks[1] if q // 2 else 0)


def window_of(half):
    return -(-half // LANES) * LANES


def finish_kernel(which_ref, recv_ref, keep_ref, out_ref, *, width):
    half = width // 2
    win = recv_ref.shape[1]
    mine_low = which_ref[0] == 0
    recv = recv_ref[...].astype(F32)
    keep = keep_ref[:, :win]
    unit = keep_ref[:, win : 2 * win]

    def column(block, place):
        return jnp.where(mine_low, block[:, half + place : half + place + 1], block[:, place : place + 1])

    first = column(keep, 0) + (column(recv, 0) + column(recv, 1))
    second = column(keep, 1) + (column(recv, 2) + column(recv, 3))
    inverse = column(keep, 2)
    grad = keep + recv
    out = inverse * (grad - first * (1.0 / width) - unit * (second * (1.0 / width)))
    moved = pltpu.roll(out, win - (win - half), 1)
    out_ref[:, :half] = jnp.where(mine_low, out, moved)[:, :half].astype(BF)
    out_ref[:, half:] = keep_ref[:, 2 * win : 2 * win + width - half].astype(BF)


def finish(which, recv, keep, width):
    tokens = recv.shape[0]
    smem = pl.BlockSpec(memory_space=pltpu.SMEM)
    vmem = pl.BlockSpec(memory_space=pltpu.VMEM)
    return pl.pallas_call(
        functools.partial(finish_kernel, width=width),
        in_specs=[smem, vmem, vmem],
        out_shape=jax.ShapeDtypeStruct((tokens, width), BF),
        compiler_params=pltpu.CompilerParams(vmem_limit_bytes=24 * 2**20),
        name="finish",
    )(which, recv, keep)


def fold_kernel(*refs):
    count = len(refs) // 4
    for i in range(count):
        keep_ref, got_ref = refs[2 * i : 2 * i + 2]
        send_ref, left_ref = refs[2 * count + 2 * i : 2 * count + 2 * i + 2]
        for q in range(keep_ref.shape[0]):
            total = (keep_ref[q].astype(F32) + got_ref[q].astype(F32)).astype(BF)
            if q % 2:
                send_ref[q // 2] = total
            else:
                left_ref[q // 2] = total


def fold(pairs):
    shapes = []
    for keep, _ in pairs:
        shapes += [jax.ShapeDtypeStruct((keep.shape[0] // 2,) + keep.shape[1:], BF)] * 2
    found = pl.pallas_call(
        fold_kernel,
        out_shape=tuple(shapes),
        compiler_params=pltpu.CompilerParams(vmem_limit_bytes=8 * 2**20),
        name="fold",
    )(*[x for pair in pairs for x in pair])
    return found[::2], found[1::2]


def close_kernel(*refs):
    out_ref, at = refs[-1], 0
    for keep_ref, got_ref in zip(refs[:-1:2], refs[1:-1:2]):
        count = keep_ref.shape[1]
        out_ref[at : at + count] = (keep_ref[0].astype(F32) + got_ref[0].astype(F32)).astype(BF)
        at += count


def close(pairs):
    count = sum(keep.shape[1] for keep, _ in pairs)
    return pl.pallas_call(
        close_kernel,
        out_shape=jax.ShapeDtypeStruct((count, ROWS, LANES), BF),
        compiler_params=pltpu.CompilerParams(vmem_limit_bytes=8 * 2**20),
        name="close",
    )(*[x for pair in pairs for x in pair])


def join_kernel(*refs):
    count = len(refs) // 3
    for i in range(count):
        have_ref, got_ref, out_ref = refs[2 * i], refs[2 * i + 1], refs[2 * count + i]
        size = have_ref.shape[0]
        out_ref[:size] = have_ref[...]
        out_ref[size:] = got_ref[...]


def join(pairs):
    shapes = [jax.ShapeDtypeStruct((2 * have.shape[0],) + have.shape[1:], BF) for have, _ in pairs]
    return pl.pallas_call(
        join_kernel,
        out_shape=tuple(shapes),
        compiler_params=pltpu.CompilerParams(vmem_limit_bytes=8 * 2**20),
        name="join",
    )(*[x for pair in pairs for x in pair])


def reduce_kernel(parts_ref, out_ref, *, factor):
    out_ref[...] = (jnp.sum(parts_ref[...].astype(F32), axis=0) * factor).astype(BF)


def reduce(parts, factor):
    return pl.pallas_call(
        functools.partial(reduce_kernel, factor=factor),
        out_shape=jax.ShapeDtypeStruct(parts.shape[1:], BF),
        compiler_params=pltpu.CompilerParams(vmem_limit_bytes=4 * 2**20),
        name="reduce",
    )(parts)


def place_kernel(clip_ref, *refs):
    clips = len(refs) - 4
    pieces, out_refs, all_s = refs[:clips], refs[clips:-1], refs[-1]
    size = pieces[0].shape[0]
    for shift, piece in enumerate(pieces):
        all_s[pl.ds(lax.rem(clip_ref[0] + shift, clips) * size, size)] = piece[...]
    for (lo, hi), out_ref in zip(bounds(clips * size), out_refs):
        out_ref[0] = all_s[lo:hi]


def place(clip, pieces):
    total = len(pieces) * pieces[0].shape[0]
    smem = pl.BlockSpec(memory_space=pltpu.SMEM)
    vmem = pl.BlockSpec(memory_space=pltpu.VMEM)
    return pl.pallas_call(
        place_kernel,
        in_specs=[smem] + [vmem] * len(pieces),
        out_shape=tuple(jax.ShapeDtypeStruct((1, hi - lo, ROWS, LANES), BF) for lo, hi in bounds(total)),
        scratch_shapes=[pltpu.VMEM((total, ROWS, LANES), BF)],
        compiler_params=pltpu.CompilerParams(vmem_limit_bytes=4 * 2**20),
        name="place",
    )(clip, *pieces)


def untile_kernel(where_ref, half_ref, *refs):
    pieces, (out_ref, tiles_s) = refs[:-2], refs[-2:]
    size = tiles_s.shape[0] // 16
    pieces = iter(pieces)
    for side in range(2):
        half = half_ref[0] ^ side
        for far in range(2):
            for (lo, hi), order in zip(bounds(size), ORDERS):
                piece = next(pieces)
                for q in range(4):
                    k = picked(q, (order[2], order[1])) ^ (order[0] * far)
                    at = (half * 8 + (where_ref[0] ^ k)) * size + lo
                    tiles_s[pl.ds(at, hi - lo)] = piece[q]
    rows = out_ref.shape[0] // 2
    tiles = rows // ROWS
    for half in range(2):
        for j in range(out_ref.shape[1] // LANES):
            start = half * 8 * size + j * tiles
            block = tiles_s[start : start + tiles].reshape(rows, LANES)
            out_ref[half * rows : (half + 1) * rows, j * LANES : (j + 1) * LANES] = block


def untile(where, half, pieces, rows, width):
    smem = pl.BlockSpec(memory_space=pltpu.SMEM)
    vmem = pl.BlockSpec(memory_space=pltpu.VMEM)
    tiles = sum(4 * piece.shape[1] for piece in pieces)
    return pl.pallas_call(
        untile_kernel,
        in_specs=[smem, smem] + [vmem] * len(pieces),
        out_shape=jax.ShapeDtypeStruct((rows, width), BF),
        scratch_shapes=[pltpu.VMEM((tiles, ROWS, LANES), BF)],
        compiler_params=pltpu.CompilerParams(vmem_limit_bytes=16 * 2**20),
        name="untile",
    )(where, half, *pieces)


def swap(x, axes, k):
    count = math.prod(lax.axis_size(a) for a in axes)
    return lax.ppermute(x, axes, [(i, i ^ k) for i in range(count)])


def exchange(x, axis):
    parts = x.reshape((-1,) + x.shape[-3:])
    return lax.all_to_all(parts, axis, split_axis=0, concat_axis=0, tiled=True)


def meet(blocks, level):
    return [swap(block, PLANE, order[level]) for block, order in zip(blocks, ORDERS)]


def sum_plane(found):
    send, keep = found[::2], found[1::2]
    send, keep = fold(list(zip(keep, meet(send, 0))))
    send, keep = fold(list(zip(keep, meet(send, 1))))
    return close(list(zip(keep, meet(send, 2))))


def ring(own, axis, home):
    count = lax.axis_size(axis)
    pieces = [own] * count
    up = down = own
    for step in range(1, count // 2 + 1):
        if step == 2:
            up, down, home = lax.optimization_barrier((up, down, home))
        up = lax.ppermute(up, axis, [(i, (i + 1) % count) for i in range(count)])
        pieces[count - step] = up
        if step < count - step:
            down = lax.ppermute(down, axis, [(i, (i - 1) % count) for i in range(count)])
            pieces[step] = down
    return pieces, home


def gather_plane(have, where, half, rows, width):
    have = join(list(zip(have, meet(have, 2))))
    have = join(list(zip(have, meet(have, 1))))
    pieces = list(have) + meet(have, 0)
    pieces = pieces + [swap(piece, ("core",), 1) for piece in pieces]
    return untile(where, half, pieces, rows, width)


def body(latent, mod_shift, mod_scale, w_qkv, q_gain, k_gain, cotangent):
    _, _, patches, width = latent.shape
    hw = w_qkv.shape[2]
    hd = q_gain.shape[0]
    heads = hw // hd
    frames = 1
    for a in SEQ:
        frames *= lax.axis_size(a)
    own_patches = patches // frames
    clips = lax.axis_size("dp")
    wt = w_qkv.transpose(1, 2, 0).reshape(3 * hw, width)
    x = pack(latent[0, 0], cotangent[0, 0].T).reshape(frames, own_patches, width + hw)
    x = lax.all_to_all(x, SEQ, split_axis=0, concat_axis=0, tiled=True).reshape(patches, width + hw)
    affine = jnp.concatenate([mod_shift, 1.0 + mod_scale])
    core = lax.axis_index("core").astype(jnp.int32).reshape(1)
    which = lax.axis_index("tensor").astype(jnp.int32).reshape(1)
    where = lax.axis_index(PLANE).astype(jnp.int32).reshape(1)
    mod, gp_keep, gp_send, send, keep = attend(
        core, which, x, affine, wt, q_gain[:, None], k_gain[:, None], own_patches, heads, hd
    )
    used = (3 * hw // 2 // ROWS) * (width // LANES)
    group = 8 * clips
    padded = -(-used // group) * group
    gp_other, mod_other = swap(gp_send, ("core",), 1), swap(mod, ("core",), 1)
    recv = lax.ppermute(send, "tensor", [(0, 1), (1, 0)])
    own = sum_plane(outer(where, gp_keep, gp_other, mod, mod_other, padded))
    home = finish(which, recv, keep, width).reshape(frames, own_patches, width)
    own, home = lax.optimization_barrier((own, home))
    own = exchange(own.reshape((clips, own.shape[0] // clips) + own.shape[1:]), "dp")
    own = reduce(own, 1.0 / math.sqrt(clips * frames * patches))
    pieces, home = ring(own, "dp", home)
    home = lax.all_to_all(home, SEQ, split_axis=0, concat_axis=0, tiled=True)
    pieces, home = lax.optimization_barrier((pieces, home))
    grad_t, att_t = unpack(home.reshape(patches, width))
    have = place(lax.axis_index("dp").astype(jnp.int32).reshape(1), pieces)
    grad_qkv = gather_plane(have, where, core, 3 * hw, width)
    grad_qkv = grad_qkv.reshape(3, hw, width).transpose(2, 0, 1)
    return (att_t.T[None, None], grad_t.T[None, None], grad_qkv)


def solution(mesh):
    fine = Mesh(mesh.devices.reshape(mesh.shape["dp"], 2, 4, 2, 2), ("dp",) + SEQ + ("tensor",))
    in_specs = (
        P("dp", SEQ, None, None),
        P("dp", None),
        P("dp", None),
        P(None, None, "tensor"),
        P(),
        P(),
        P("dp", SEQ, None, "tensor"),
    )
    out_specs = (
        P("dp", SEQ, None, "tensor"),
        P("dp", SEQ, None, "tensor"),
        P(None, None, "tensor"),
    )
    return jax.shard_map(body, mesh=fine, in_specs=in_specs, out_specs=out_specs, check_vma=False)
```

```python
import functools
import math

import jax
import jax.numpy as jnp
from jax import lax
from jax.experimental import pallas as pl
from jax.experimental.pallas import tpu as pltpu
from jax.sharding import Mesh, PartitionSpec as P

BF = jnp.bfloat16
F32 = jnp.float32
EPS = 1e-06
NN = (((1,), (0,)), ((), ()))
NT = (((1,), (1,)), ((), ()))
LOG2E = math.log2(math.e)
ROWS, LANES = 16, 128
PLANE = ("xlo", "y")
SEQ = PLANE + ("core",)


def mm(a, b, dims):
    return lax.dot_general(a, b, dims, preferred_element_type=F32)


def eye(n):
    rows = lax.broadcasted_iota(jnp.int32, (n, n), 0)
    cols = lax.broadcasted_iota(jnp.int32, (n, n), 1)
    return jnp.where(rows == cols, 1.0, 0.0).astype(BF)


def fetch(pairs, sems):
    copies = [pltpu.make_async_copy(src, dst, sems.at[i]) for i, (src, dst) in enumerate(pairs)]
    for copy in copies:
        copy.start()
    return copies


def pack_kernel(latent_hbm, cot_hbm, out_ref, latent_s, cot_s, sems):
    width = latent_s.shape[1]
    first, second = fetch([(cot_hbm, cot_s), (latent_hbm, latent_s)], sems)
    ident = eye(latent_s.shape[0])
    first.wait()
    out_ref[:, width:] = mm(ident, cot_s[...], NT).astype(BF)
    second.wait()
    out_ref[:, :width] = latent_s[...]


def pack(latent, cot_t):
    tokens, width = latent.shape
    hbm = pl.BlockSpec(memory_space=pltpu.HBM)
    return pl.pallas_call(
        pack_kernel,
        in_specs=[hbm, hbm],
        out_shape=jax.ShapeDtypeStruct((tokens, width + cot_t.shape[0]), BF),
        scratch_shapes=[
            pltpu.VMEM(latent.shape, BF),
            pltpu.VMEM(cot_t.shape, BF),
            pltpu.SemaphoreType.DMA((2,)),
        ],
        compiler_params=pltpu.CompilerParams(vmem_limit_bytes=60 * 2**20),
        name="pack",
    )(latent, cot_t)


def unpack_kernel(rows_ref, first_ref, second_ref):
    ident = eye(LANES)
    half = first_ref.shape[0]
    for start in range(0, 2 * half, LANES):
        found = mm(ident, rows_ref[:, start : start + LANES], NT).astype(BF)
        cut = min(max(half - start, 0), LANES)
        if cut:
            first_ref[start : start + cut] = found[:cut]
        if cut < LANES:
            second_ref[start + cut - half : start + LANES - half] = found[cut:]


def unpack(rows):
    tokens, width = rows.shape
    shape = jax.ShapeDtypeStruct((width // 2, tokens), BF)
    return pl.pallas_call(
        unpack_kernel,
        out_shape=(shape, shape),
        compiler_params=pltpu.CompilerParams(vmem_limit_bytes=8 * 2**20),
        name="unpack",
    )(rows)


def unit_of(values):
    width = values.shape[1]
    centred = values - jnp.sum(values, axis=1, keepdims=True) * (1.0 / width)
    inverse = lax.rsqrt(jnp.sum(centred * centred, axis=1, keepdims=True) * (1.0 / width) + EPS)
    return centred * inverse, inverse


def attend_kernel(core_ref, x_ref, affine_ref, wt_hbm, qg_ref, kg_ref,
                  mod_ref, gp_keep_ref, gp_send_ref, att_ref,
                  wt_s, rows_s, weights_s, w_s, grad_s, q_s, k_s, v_s, cot_s, sems, *, patches, heads, hd):
    tokens, _ = x_ref.shape
    width = affine_ref.shape[1]
    hw = heads * hd
    parts = [pl.ds(part * hw, hw) for part in range(3)]
    copies = fetch([(wt_hbm.at[rows], wt_s.at[rows]) for rows in parts], sems)
    unit, _ = unit_of(x_ref[:, :width].astype(F32))
    mod_ref[...] = (unit * affine_ref[1:2] + affine_ref[0:1]).astype(BF)
    mod = mod_ref[...]
    ident = eye(tokens)
    for start in range(0, hw, tokens):
        size = min(tokens, hw - start)
        block = x_ref[:, width + start : width + start + size]
        cot_s[start : start + size, :] = mm(ident[:size, :size], block, NT)

    def project(part):
        copies[part].wait()
        return mm(wt_s[part * hw : (part + 1) * hw, :], mod, NT).astype(BF).astype(F32)

    def norm(rows):
        inv = lax.rsqrt(jnp.sum(rows * rows, axis=0, keepdims=True) * (1.0 / hd) + EPS)
        return rows * inv, inv

    def back(hat, inv, gain, grad):
        weighted = grad * gain
        mean = jnp.sum(hat * weighted, axis=0, keepdims=True) * (1.0 / hd)
        return inv * (weighted - hat * mean)

    def put(part, h, rows):
        start = part * hw + h * hd
        rows_s[start : start + hd, :] = rows

    root = 1.0 / math.sqrt(hd)
    q_gain = qg_ref[...] * (root * LOG2E)
    k_gain = kg_ref[...]
    q_back = qg_ref[...] * root
    k_back = kg_ref[...] * (1.0 / LOG2E)
    each = [slice(h * hd, (h + 1) * hd) for h in range(heads)]

    spot = lax.broadcasted_iota(jnp.int32, (patches, tokens), 0)
    token = lax.broadcasted_iota(jnp.int32, (patches, tokens), 1)
    spots = jnp.where(lax.rem(token, patches) == spot, 16.0, 0.0)
    top = lax.broadcasted_iota(jnp.int32, (8, tokens), 0) == 0
    zeros = jnp.zeros((-(hd + patches + 8) % LANES, tokens), F32)
    q_tail = [spots, jnp.where(top, 16.0, 0.0), zeros]
    k_tail = [spots, jnp.where(top, -16.0, 0.0), zeros]
    v_tail = [jnp.where(top, 1.0, 0.0), jnp.zeros((-(hd + 8) % LANES, tokens), F32)]
    blank = jnp.zeros((-hd % LANES, tokens), F32)

    def rows_of(ref):
        found = []
        for h in range(0, heads, 2):
            both = mm(ident, ref[h : h + 2].reshape(2 * LANES, tokens), NT).astype(BF)
            found += [both[:, :LANES], both[:, LANES:]]
        return found

    q_all = project(0)
    q_inv = []
    for h, at in enumerate(each):
        hat, inv = norm(q_all[at])
        q_inv.append(inv)
        q_s[h] = jnp.concatenate([hat * q_gain] + q_tail).astype(BF)
    k_all = project(1)
    k_inv = []
    for h, at in enumerate(each):
        hat, inv = norm(k_all[at])
        k_inv.append(inv)
        k_s[h] = jnp.concatenate([hat * k_gain] + k_tail).astype(BF)
    v_all = project(2)
    for h, at in enumerate(each):
        v_s[h] = jnp.concatenate([v_all[at]] + v_tail).astype(BF)
    k_rows = rows_of(k_s)
    for h in range(heads):
        weights = jnp.exp2(mm(k_rows[h], q_s[h], NN))
        weights_s[h] = weights
        w_s[h] = weights.astype(BF)
    v_rows = rows_of(v_s)
    deltas, cots = [], []
    for h, at in enumerate(each):
        summed = mm(v_s[h], w_s[h], NN)
        share = 1.0 / summed[hd : hd + 1]
        out = summed[:hd] * share
        att_ref[at, :] = out.astype(BF)
        cot_share = cot_s[at, :] * share
        cots.append(jnp.concatenate([cot_share, blank]).astype(BF))
        deltas.append(jnp.sum(out * cot_share, axis=0, keepdims=True))
    for h in range(heads):
        grad_s[h] = (weights_s[h] * (mm(v_rows[h], cots[h], NN) - deltas[h])).astype(BF)
        put(2, h, mm(cots[h], w_s[h], NT)[:hd])
    for h, at in enumerate(each):
        put(0, h, back(q_all[at] * q_inv[h], q_inv[h], q_back, mm(k_s[h], grad_s[h], NN)[:hd]))
        put(1, h, back(k_all[at] * k_inv[h], k_inv[h], k_back, mm(q_s[h], grad_s[h], NT)[:hd]))
    size = gp_keep_ref.shape[0]
    gp_keep_ref[...] = rows_s[pl.ds(pl.multiple_of(core_ref[0] * size, ROWS), size), :].astype(BF)
    gp_send_ref[...] = rows_s[pl.ds(pl.multiple_of((1 - core_ref[0]) * size, ROWS), size), :].astype(BF)


def attend(core, x, affine, wt, qg, kg, patches, heads, hd):
    tokens = x.shape[0]
    width = wt.shape[1]
    hw = heads * hd
    smem = pl.BlockSpec(memory_space=pltpu.SMEM)
    vmem = pl.BlockSpec(memory_space=pltpu.VMEM)
    half = jax.ShapeDtypeStruct((3 * hw // 2, tokens), BF)
    tall = pltpu.VMEM((heads, LANES, tokens), BF)
    return pl.pallas_call(
        functools.partial(attend_kernel, patches=patches, heads=heads, hd=hd),
        in_specs=[smem, vmem, vmem, pl.BlockSpec(memory_space=pltpu.HBM), vmem, vmem],
        out_shape=(
            jax.ShapeDtypeStruct((tokens, width), BF),
            half,
            half,
            jax.ShapeDtypeStruct((hw, tokens), BF),
        ),
        scratch_shapes=[
            pltpu.VMEM((3 * hw, width), BF),
            pltpu.VMEM((3 * hw, tokens), F32),
            pltpu.VMEM((heads, tokens, tokens), F32),
            pltpu.VMEM((heads, tokens, tokens), BF),
            pltpu.VMEM((heads, tokens, tokens), BF),
            tall,
            tall,
            tall,
            pltpu.VMEM((hw, tokens), F32),
            pltpu.SemaphoreType.DMA((3,)),
        ],
        compiler_params=pltpu.CompilerParams(vmem_limit_bytes=50 * 2**20),
        name="attend",
    )(core, x, affine, wt, qg, kg)


def split_kernel(core_ref, which_ref, x_ref, affine_ref, wt_hbm, gp_keep_ref, gp_send_ref, att_ref,
                 send_ref, keep_ref, wt_s, gp_s, sems):
    tokens, _ = x_ref.shape
    width = affine_ref.shape[1]
    hw = att_ref.shape[0]
    parts = [pl.ds(part * hw, hw) for part in range(3)]
    copies = fetch([(wt_hbm.at[rows], wt_s.at[rows]) for rows in parts], sems)
    unit, inverse = unit_of(x_ref[:, :width].astype(F32))
    ident = eye(tokens)
    size = gp_keep_ref.shape[0]
    gp_s[pl.ds(pl.multiple_of(core_ref[0] * size, ROWS), size), :] = gp_keep_ref[...]
    gp_s[pl.ds(pl.multiple_of((1 - core_ref[0]) * size, ROWS), size), :] = gp_send_ref[...]
    grad = jnp.zeros((tokens, width), F32)
    for part in range(3):
        at = slice(part * hw, (part + 1) * hw)
        rows = mm(ident, gp_s[at, :], NT).astype(BF)
        copies[part].wait()
        grad = grad + mm(rows, wt_s[at, :], NN)
    half = width // 2
    win = send_ref.shape[1]
    mine_low = which_ref[0] == 0
    scaled = grad * affine_ref[1:2]
    first = jnp.sum(scaled, axis=1, keepdims=True)
    second = jnp.sum(scaled * unit, axis=1, keepdims=True)
    col = lax.broadcasted_iota(jnp.int32, (tokens, win), 1)
    here = jnp.where(mine_low, half, 0)
    there = jnp.where(mine_low, 0, half)
    low, high = scaled[:, :win], scaled[:, width - win :]
    send = jnp.where(mine_low, high, low)
    keep = jnp.where(mine_low, low, high)
    for place, term in enumerate((first, second)):
        coarse = term.astype(BF).astype(F32)
        send = jnp.where(col == there + 2 * place, coarse, send)
        send = jnp.where(col == there + 2 * place + 1, term - coarse, send)
    for place, term in enumerate((first, second, inverse)):
        keep = jnp.where(col == here + place, term, keep)
    send_ref[...] = send.astype(BF)
    keep_ref[:, :win] = keep
    keep_ref[:, win : 2 * win] = jnp.where(mine_low, unit[:, :win], unit[:, width - win :])
    keep_ref[:, 2 * win : 2 * win + hw] = mm(ident, att_ref[...], NT)


def split(core, which, x, affine, wt, gp_keep, gp_send, att):
    tokens = x.shape[0]
    hw = att.shape[0]
    win = window_of(wt.shape[1] // 2)
    smem = pl.BlockSpec(memory_space=pltpu.SMEM)
    vmem = pl.BlockSpec(memory_space=pltpu.VMEM)
    return pl.pallas_call(
        split_kernel,
        in_specs=[smem, smem, vmem, vmem, pl.BlockSpec(memory_space=pltpu.HBM), vmem, vmem, vmem],
        out_shape=(
            jax.ShapeDtypeStruct((tokens, win), BF),
            jax.ShapeDtypeStruct((tokens, 2 * win + window_of(hw)), F32),
        ),
        scratch_shapes=[
            pltpu.VMEM(wt.shape, BF),
            pltpu.VMEM((wt.shape[0], tokens), BF),
            pltpu.SemaphoreType.DMA((3,)),
        ],
        compiler_params=pltpu.CompilerParams(vmem_limit_bytes=18 * 2**20),
        name="split",
    )(core, which, x, affine, wt, gp_keep, gp_send, att)


def outer_kernel(where_ref, gp_a, gp_b, mod_a, mod_b, *refs):
    out_refs, tiles_s = refs[:-1], refs[-1]
    rows, width = gp_a.shape[0], mod_a.shape[1]
    tiles = rows // ROWS
    used = tiles * (width // LANES)
    tiles_s[used:] = jnp.zeros((tiles_s.shape[0] - used, ROWS, LANES), BF)
    gp = jnp.concatenate([gp_a[...], gp_b[...]], axis=1)
    for start in range(0, width, 2 * LANES):
        stop = min(start + 2 * LANES, width)
        mod = jnp.concatenate([mod_a[:, start:stop], mod_b[:, start:stop]], axis=0)
        found = mm(gp, mod, NN).astype(BF)
        for at in range(0, stop - start, LANES):
            j = (start + at) // LANES
            tiles_s[j * tiles : (j + 1) * tiles] = found[:, at : at + LANES].reshape(tiles, ROWS, LANES)
    size = tiles_s.shape[0] // 8
    keep_ref = out_refs[-1]
    for (lo, hi), order, send_ref in zip(bounds(size), ORDERS, out_refs):
        for q in range(4):
            k = picked(q, order[1:])
            at = (where_ref[0] ^ k) * size + lo
            keep_ref[q, lo:hi] = tiles_s[pl.ds(at, hi - lo)]
            at = (where_ref[0] ^ (k ^ order[0])) * size + lo
            send_ref[q] = tiles_s[pl.ds(at, hi - lo)]


def outer(where, gp_a, gp_b, mod_a, mod_b, padded):
    smem = pl.BlockSpec(memory_space=pltpu.SMEM)
    vmem = pl.BlockSpec(memory_space=pltpu.VMEM)
    size = padded // 8
    shapes = [jax.ShapeDtypeStruct((4, n, ROWS, LANES), BF) for n in [hi - lo for lo, hi in bounds(size)] + [size]]
    return pl.pallas_call(
        outer_kernel,
        in_specs=[smem] + [vmem] * 4,
        out_shape=tuple(shapes),
        scratch_shapes=[pltpu.VMEM((padded, ROWS, LANES), BF)],
        compiler_params=pltpu.CompilerParams(vmem_limit_bytes=16 * 2**20),
        name="outer",
    )(where, gp_a, gp_b, mod_a, mod_b)


ORDERS = ((1, 3, 4), (3, 4, 1), (4, 1, 3))


def bounds(size):
    cuts = [0, -(-size // 3), -(-2 * size // 3), size]
    return list(zip(cuts[:-1], cuts[1:]))


def picked(q, masks):
    return (masks[0] if q % 2 else 0) ^ (masks[1] if q // 2 else 0)


def window_of(half):
    return -(-half // LANES) * LANES


def finish_kernel(which_ref, recv_ref, keep_ref, out_ref, *, width):
    half = width // 2
    win = recv_ref.shape[1]
    mine_low = which_ref[0] == 0
    recv = recv_ref[...].astype(F32)
    keep = keep_ref[:, :win]
    unit = keep_ref[:, win : 2 * win]

    def column(block, place):
        return jnp.where(mine_low, block[:, half + place : half + place + 1], block[:, place : place + 1])

    first = column(keep, 0) + (column(recv, 0) + column(recv, 1))
    second = column(keep, 1) + (column(recv, 2) + column(recv, 3))
    inverse = column(keep, 2)
    grad = keep + recv
    out = inverse * (grad - first * (1.0 / width) - unit * (second * (1.0 / width)))
    moved = pltpu.roll(out, win - (win - half), 1)
    out_ref[:, :half] = jnp.where(mine_low, out, moved)[:, :half].astype(BF)
    out_ref[:, half:] = keep_ref[:, 2 * win : 2 * win + width - half].astype(BF)


def finish(which, recv, keep, width):
    tokens = recv.shape[0]
    smem = pl.BlockSpec(memory_space=pltpu.SMEM)
    vmem = pl.BlockSpec(memory_space=pltpu.VMEM)
    return pl.pallas_call(
        functools.partial(finish_kernel, width=width),
        in_specs=[smem, vmem, vmem],
        out_shape=jax.ShapeDtypeStruct((tokens, width), BF),
        compiler_params=pltpu.CompilerParams(vmem_limit_bytes=24 * 2**20),
        name="finish",
    )(which, recv, keep)


def fold_kernel(keep_ref, *refs):
    count = (len(refs) - 1) // 2
    got_refs, send_refs, left_ref = refs[:count], refs[count:-1], refs[-1]
    for (lo, hi), got_ref, send_ref in zip(bounds(keep_ref.shape[1]), got_refs, send_refs):
        for q in range(keep_ref.shape[0]):
            total = (keep_ref[q, lo:hi].astype(F32) + got_ref[q].astype(F32)).astype(BF)
            if q % 2:
                send_ref[q // 2] = total
            else:
                left_ref[q // 2, lo:hi] = total


def fold(keep, got):
    shapes = [jax.ShapeDtypeStruct((x.shape[0] // 2,) + x.shape[1:], BF) for x in (*got, keep)]
    found = pl.pallas_call(
        fold_kernel,
        out_shape=tuple(shapes),
        compiler_params=pltpu.CompilerParams(vmem_limit_bytes=8 * 2**20),
        name="fold",
    )(keep, *got)
    return found[:-1], found[-1]


def close_kernel(keep_ref, *refs):
    out_ref = refs[-1]
    for (lo, hi), got_ref in zip(bounds(keep_ref.shape[1]), refs):
        out_ref[lo:hi] = (keep_ref[0, lo:hi].astype(F32) + got_ref[0].astype(F32)).astype(BF)


def close(keep, got):
    return pl.pallas_call(
        close_kernel,
        out_shape=jax.ShapeDtypeStruct(keep.shape[1:], BF),
        compiler_params=pltpu.CompilerParams(vmem_limit_bytes=8 * 2**20),
        name="close",
    )(keep, *got)


def join_kernel(*refs):
    count = len(refs) // 3
    for i in range(count):
        have_ref, got_ref, out_ref = refs[2 * i], refs[2 * i + 1], refs[2 * count + i]
        size = have_ref.shape[0]
        out_ref[:size] = have_ref[...]
        out_ref[size:] = got_ref[...]


def join(pairs):
    shapes = [jax.ShapeDtypeStruct((2 * have.shape[0],) + have.shape[1:], BF) for have, _ in pairs]
    return pl.pallas_call(
        join_kernel,
        out_shape=tuple(shapes),
        compiler_params=pltpu.CompilerParams(vmem_limit_bytes=8 * 2**20),
        name="join",
    )(*[x for pair in pairs for x in pair])


def reduce_kernel(parts_ref, out_ref, *, factor):
    out_ref[...] = (jnp.sum(parts_ref[...].astype(F32), axis=0) * factor).astype(BF)


def reduce(parts, factor):
    return pl.pallas_call(
        functools.partial(reduce_kernel, factor=factor),
        out_shape=jax.ShapeDtypeStruct(parts.shape[1:], BF),
        compiler_params=pltpu.CompilerParams(vmem_limit_bytes=4 * 2**20),
        name="reduce",
    )(parts)


def place_kernel(clip_ref, *refs):
    clips = len(refs) - 4
    pieces, out_refs, all_s = refs[:clips], refs[clips:-1], refs[-1]
    size = pieces[0].shape[0]
    for shift, piece in enumerate(pieces):
        all_s[pl.ds(lax.rem(clip_ref[0] + shift, clips) * size, size)] = piece[...]
    for (lo, hi), out_ref in zip(bounds(clips * size), out_refs):
        out_ref[0] = all_s[lo:hi]


def place(clip, pieces):
    total = len(pieces) * pieces[0].shape[0]
    smem = pl.BlockSpec(memory_space=pltpu.SMEM)
    vmem = pl.BlockSpec(memory_space=pltpu.VMEM)
    return pl.pallas_call(
        place_kernel,
        in_specs=[smem] + [vmem] * len(pieces),
        out_shape=tuple(jax.ShapeDtypeStruct((1, hi - lo, ROWS, LANES), BF) for lo, hi in bounds(total)),
        scratch_shapes=[pltpu.VMEM((total, ROWS, LANES), BF)],
        compiler_params=pltpu.CompilerParams(vmem_limit_bytes=4 * 2**20),
        name="place",
    )(clip, *pieces)


def untile_kernel(where_ref, half_ref, *refs):
    pieces, (out_ref, tiles_s) = refs[:-2], refs[-2:]
    size = tiles_s.shape[0] // 16
    pieces = iter(pieces)
    for side in range(2):
        half = half_ref[0] ^ side
        for far in range(2):
            for (lo, hi), order in zip(bounds(size), ORDERS):
                piece = next(pieces)
                for q in range(4):
                    k = picked(q, (order[2], order[1])) ^ (order[0] * far)
                    at = (half * 8 + (where_ref[0] ^ k)) * size + lo
                    tiles_s[pl.ds(at, hi - lo)] = piece[q]
    rows = out_ref.shape[0] // 2
    tiles = rows // ROWS
    for half in range(2):
        for j in range(out_ref.shape[1] // LANES):
            start = half * 8 * size + j * tiles
            block = tiles_s[start : start + tiles].reshape(rows, LANES)
            out_ref[half * rows : (half + 1) * rows, j * LANES : (j + 1) * LANES] = block


def untile(where, half, pieces, rows, width):
    smem = pl.BlockSpec(memory_space=pltpu.SMEM)
    vmem = pl.BlockSpec(memory_space=pltpu.VMEM)
    tiles = sum(4 * piece.shape[1] for piece in pieces)
    return pl.pallas_call(
        untile_kernel,
        in_specs=[smem, smem] + [vmem] * len(pieces),
        out_shape=jax.ShapeDtypeStruct((rows, width), BF),
        scratch_shapes=[pltpu.VMEM((tiles, ROWS, LANES), BF)],
        compiler_params=pltpu.CompilerParams(vmem_limit_bytes=16 * 2**20),
        name="untile",
    )(where, half, *pieces)


def swap(x, axes, k):
    count = math.prod(lax.axis_size(a) for a in axes)
    return lax.ppermute(x, axes, [(i, i ^ k) for i in range(count)])


def exchange(x, axis):
    parts = x.reshape((-1,) + x.shape[-3:])
    return lax.all_to_all(parts, axis, split_axis=0, concat_axis=0, tiled=True)


def meet(blocks, level):
    return [swap(block, PLANE, order[level]) for block, order in zip(blocks, ORDERS)]


def sum_plane(found, beside):
    send, keep = found[:-1], found[-1]
    got, beside = lax.optimization_barrier((meet(send, 0), beside))
    send, keep = fold(keep, got)
    send, keep = fold(keep, meet(send, 1))
    return close(keep, meet(send, 2)), beside


def ring(own, axis, home):
    count = lax.axis_size(axis)
    pieces = [own] * count
    up = down = own
    for step in range(1, count // 2 + 1):
        if step == 2:
            up, down, home = lax.optimization_barrier((up, down, home))
        up = lax.ppermute(up, axis, [(i, (i + 1) % count) for i in range(count)])
        pieces[count - step] = up
        if step < count - step:
            down = lax.ppermute(down, axis, [(i, (i - 1) % count) for i in range(count)])
            pieces[step] = down
    return pieces, home


def gather_plane(have, where, half, rows, width):
    have = join(list(zip(have, meet(have, 2))))
    have = join(list(zip(have, meet(have, 1))))
    pieces = list(have) + meet(have, 0)
    pieces = pieces + [swap(piece, ("core",), 1) for piece in pieces]
    return untile(where, half, pieces, rows, width)


def body(latent, mod_shift, mod_scale, w_qkv, q_gain, k_gain, cotangent):
    _, _, patches, width = latent.shape
    hw = w_qkv.shape[2]
    hd = q_gain.shape[0]
    heads = hw // hd
    frames = 1
    for a in SEQ:
        frames *= lax.axis_size(a)
    own_patches = patches // frames
    clips = lax.axis_size("dp")
    wt = w_qkv.transpose(1, 2, 0).reshape(3 * hw, width)
    x = pack(latent[0, 0], cotangent[0, 0].T).reshape(frames, own_patches, width + hw)
    x = lax.all_to_all(x, SEQ, split_axis=0, concat_axis=0, tiled=True).reshape(patches, width + hw)
    affine = jnp.concatenate([mod_shift, 1.0 + mod_scale])
    core = lax.axis_index("core").astype(jnp.int32).reshape(1)
    which = lax.axis_index("tensor").astype(jnp.int32).reshape(1)
    where = lax.axis_index(PLANE).astype(jnp.int32).reshape(1)
    mod, gp_keep, gp_send, att_t = attend(
        core, x, affine, wt, q_gain[:, None], k_gain[:, None], own_patches, heads, hd
    )
    used = (3 * hw // 2 // ROWS) * (width // LANES)
    group = 8 * clips
    padded = -(-used // group) * group
    gp_other, mod_other = swap(gp_send, ("core",), 1), swap(mod, ("core",), 1)
    found = outer(where, gp_keep, gp_other, mod, mod_other, padded)
    send, keep = split(core, which, x, affine, wt, gp_keep, gp_send, att_t)
    own, send = sum_plane(found, send)
    recv = lax.ppermute(send, "tensor", [(0, 1), (1, 0)])
    home = finish(which, recv, keep, width).reshape(frames, own_patches, width)
    own, home = lax.optimization_barrier((own, home))
    own = exchange(own.reshape((clips, own.shape[0] // clips) + own.shape[1:]), "dp")
    own = reduce(own, 1.0 / math.sqrt(clips * frames * patches))
    pieces, home = ring(own, "dp", home)
    home = lax.all_to_all(home, SEQ, split_axis=0, concat_axis=0, tiled=True)
    pieces, home = lax.optimization_barrier((pieces, home))
    grad_t, att_t = unpack(home.reshape(patches, width))
    have = place(lax.axis_index("dp").astype(jnp.int32).reshape(1), pieces)
    grad_qkv = gather_plane(have, where, core, 3 * hw, width)
    grad_qkv = grad_qkv.reshape(3, hw, width).transpose(2, 0, 1)
    return (att_t.T[None, None], grad_t.T[None, None], grad_qkv)


def solution(mesh):
    fine = Mesh(mesh.devices.reshape(mesh.shape["dp"], 2, 4, 2, 2), ("dp",) + SEQ + ("tensor",))
    in_specs = (
        P("dp", SEQ, None, None),
        P("dp", None),
        P("dp", None),
        P(None, None, "tensor"),
        P(),
        P(),
        P("dp", SEQ, None, "tensor"),
    )
    out_specs = (
        P("dp", SEQ, None, "tensor"),
        P("dp", SEQ, None, "tensor"),
        P(None, None, "tensor"),
    )
    return jax.shard_map(body, mesh=fine, in_specs=in_specs, out_specs=out_specs, check_vma=False)
```

```python
import functools
import math

import jax
import jax.numpy as jnp
from jax import lax
from jax.experimental import pallas as pl
from jax.experimental.pallas import tpu as pltpu
from jax.sharding import Mesh, PartitionSpec as P

BF = jnp.bfloat16
F32 = jnp.float32
EPS = 1e-06
NN = (((1,), (0,)), ((), ()))
NT = (((1,), (1,)), ((), ()))
LOG2E = math.log2(math.e)
ROWS, LANES = 16, 128
PLANE = ("xlo", "y")
SEQ = PLANE + ("core",)


def mm(a, b, dims):
    return lax.dot_general(a, b, dims, preferred_element_type=F32)


def eye(n):
    rows = lax.broadcasted_iota(jnp.int32, (n, n), 0)
    cols = lax.broadcasted_iota(jnp.int32, (n, n), 1)
    return jnp.where(rows == cols, 1.0, 0.0).astype(BF)


def fetch(pairs, sems):
    copies = [pltpu.make_async_copy(src, dst, sems.at[i]) for i, (src, dst) in enumerate(pairs)]
    for copy in copies:
        copy.start()
    return copies


def pack_kernel(latent_hbm, cot_hbm, out_ref, latent_s, cot_s, sems):
    width = latent_s.shape[1]
    first, second = fetch([(cot_hbm, cot_s), (latent_hbm, latent_s)], sems)
    ident = eye(latent_s.shape[0])
    first.wait()
    out_ref[:, width:] = mm(ident, cot_s[...], NT).astype(BF)
    second.wait()
    out_ref[:, :width] = latent_s[...]


def pack(latent, cot_t):
    tokens, width = latent.shape
    hbm = pl.BlockSpec(memory_space=pltpu.HBM)
    return pl.pallas_call(
        pack_kernel,
        in_specs=[hbm, hbm],
        out_shape=jax.ShapeDtypeStruct((tokens, width + cot_t.shape[0]), BF),
        scratch_shapes=[
            pltpu.VMEM(latent.shape, BF),
            pltpu.VMEM(cot_t.shape, BF),
            pltpu.SemaphoreType.DMA((2,)),
        ],
        compiler_params=pltpu.CompilerParams(vmem_limit_bytes=60 * 2**20),
        name="pack",
    )(latent, cot_t)


def unpack_kernel(rows_ref, first_ref, second_ref):
    ident = eye(LANES)
    half = first_ref.shape[0]
    for start in range(0, 2 * half, LANES):
        found = mm(ident, rows_ref[:, start : start + LANES], NT).astype(BF)
        cut = min(max(half - start, 0), LANES)
        if cut:
            first_ref[start : start + cut] = found[:cut]
        if cut < LANES:
            second_ref[start + cut - half : start + LANES - half] = found[cut:]


def unpack(rows):
    tokens, width = rows.shape
    shape = jax.ShapeDtypeStruct((width // 2, tokens), BF)
    return pl.pallas_call(
        unpack_kernel,
        out_shape=(shape, shape),
        compiler_params=pltpu.CompilerParams(vmem_limit_bytes=8 * 2**20),
        name="unpack",
    )(rows)


def unit_of(values):
    width = values.shape[1]
    centred = values - jnp.sum(values, axis=1, keepdims=True) * (1.0 / width)
    inverse = lax.rsqrt(jnp.sum(centred * centred, axis=1, keepdims=True) * (1.0 / width) + EPS)
    return centred * inverse, inverse


def attend_kernel(core_ref, x_ref, affine_ref, wt_hbm, qg_ref, kg_ref,
                  mod_ref, gp_keep_ref, gp_send_ref, att_ref,
                  wt_s, rows_s, weights_s, w_s, grad_s, q_s, k_s, v_s, cot_s, sems, *, patches, heads, hd):
    tokens, _ = x_ref.shape
    width = affine_ref.shape[1]
    hw = heads * hd
    parts = [pl.ds(part * hw, hw) for part in range(3)]
    copies = fetch([(wt_hbm.at[rows], wt_s.at[rows]) for rows in parts], sems)
    unit, _ = unit_of(x_ref[:, :width].astype(F32))
    mod_ref[...] = (unit * affine_ref[1:2] + affine_ref[0:1]).astype(BF)
    mod = mod_ref[...]
    ident = eye(tokens)
    for start in range(0, hw, tokens):
        size = min(tokens, hw - start)
        block = x_ref[:, width + start : width + start + size]
        cot_s[start : start + size, :] = mm(ident[:size, :size], block, NT)

    def project(part):
        copies[part].wait()
        return mm(wt_s[part * hw : (part + 1) * hw, :], mod, NT).astype(BF).astype(F32)

    def norm(rows):
        inv = lax.rsqrt(jnp.sum(rows * rows, axis=0, keepdims=True) * (1.0 / hd) + EPS)
        return rows * inv, inv

    def back(hat, inv, gain, grad):
        weighted = grad * gain
        mean = jnp.sum(hat * weighted, axis=0, keepdims=True) * (1.0 / hd)
        return inv * (weighted - hat * mean)

    def put(part, h, rows):
        start = part * hw + h * hd
        rows_s[start : start + hd, :] = rows

    root = 1.0 / math.sqrt(hd)
    q_gain = qg_ref[...] * (root * LOG2E)
    k_gain = kg_ref[...]
    q_back = qg_ref[...] * root
    k_back = kg_ref[...] * (1.0 / LOG2E)
    each = [slice(h * hd, (h + 1) * hd) for h in range(heads)]

    spot = lax.broadcasted_iota(jnp.int32, (patches, tokens), 0)
    token = lax.broadcasted_iota(jnp.int32, (patches, tokens), 1)
    spots = jnp.where(lax.rem(token, patches) == spot, 16.0, 0.0)
    top = lax.broadcasted_iota(jnp.int32, (8, tokens), 0) == 0
    zeros = jnp.zeros((-(hd + patches + 8) % LANES, tokens), F32)
    q_tail = [spots, jnp.where(top, 16.0, 0.0), zeros]
    k_tail = [spots, jnp.where(top, -16.0, 0.0), zeros]
    v_tail = [jnp.where(top, 1.0, 0.0), jnp.zeros((-(hd + 8) % LANES, tokens), F32)]
    blank = jnp.zeros((-hd % LANES, tokens), F32)

    def rows_of(ref):
        found = []
        for h in range(0, heads, 2):
            both = mm(ident, ref[h : h + 2].reshape(2 * LANES, tokens), NT).astype(BF)
            found += [both[:, :LANES], both[:, LANES:]]
        return found

    q_all = project(0)
    q_inv = []
    for h, at in enumerate(each):
        hat, inv = norm(q_all[at])
        q_inv.append(inv)
        q_s[h] = jnp.concatenate([hat * q_gain] + q_tail).astype(BF)
    k_all = project(1)
    k_inv = []
    for h, at in enumerate(each):
        hat, inv = norm(k_all[at])
        k_inv.append(inv)
        k_s[h] = jnp.concatenate([hat * k_gain] + k_tail).astype(BF)
    v_all = project(2)
    for h, at in enumerate(each):
        v_s[h] = jnp.concatenate([v_all[at]] + v_tail).astype(BF)
    k_rows = rows_of(k_s)
    for h in range(heads):
        weights = jnp.exp2(mm(k_rows[h], q_s[h], NN))
        weights_s[h] = weights
        w_s[h] = weights.astype(BF)
    v_rows = rows_of(v_s)
    deltas, cots = [], []
    for h, at in enumerate(each):
        summed = mm(v_s[h], w_s[h], NN)
        share = 1.0 / summed[hd : hd + 1]
        out = summed[:hd] * share
        att_ref[at, :] = out.astype(BF)
        cot_share = cot_s[at, :] * share
        cots.append(jnp.concatenate([cot_share, blank]).astype(BF))
        deltas.append(jnp.sum(out * cot_share, axis=0, keepdims=True))
    for h in range(heads):
        grad_s[h] = (weights_s[h] * (mm(v_rows[h], cots[h], NN) - deltas[h])).astype(BF)
        put(2, h, mm(cots[h], w_s[h], NT)[:hd])
    for h, at in enumerate(each):
        put(0, h, back(q_all[at] * q_inv[h], q_inv[h], q_back, mm(k_s[h], grad_s[h], NN)[:hd]))
        put(1, h, back(k_all[at] * k_inv[h], k_inv[h], k_back, mm(q_s[h], grad_s[h], NT)[:hd]))
    size = gp_keep_ref.shape[0]
    gp_keep_ref[...] = rows_s[pl.ds(pl.multiple_of(core_ref[0] * size, ROWS), size), :].astype(BF)
    gp_send_ref[...] = rows_s[pl.ds(pl.multiple_of((1 - core_ref[0]) * size, ROWS), size), :].astype(BF)


def attend(core, x, affine, wt, qg, kg, patches, heads, hd):
    tokens = x.shape[0]
    width = wt.shape[1]
    hw = heads * hd
    smem = pl.BlockSpec(memory_space=pltpu.SMEM)
    vmem = pl.BlockSpec(memory_space=pltpu.VMEM)
    half = jax.ShapeDtypeStruct((3 * hw // 2, tokens), BF)
    tall = pltpu.VMEM((heads, LANES, tokens), BF)
    return pl.pallas_call(
        functools.partial(attend_kernel, patches=patches, heads=heads, hd=hd),
        in_specs=[smem, vmem, vmem, pl.BlockSpec(memory_space=pltpu.HBM), vmem, vmem],
        out_shape=(
            jax.ShapeDtypeStruct((tokens, width), BF),
            half,
            half,
            jax.ShapeDtypeStruct((hw, tokens), BF),
        ),
        scratch_shapes=[
            pltpu.VMEM((3 * hw, width), BF),
            pltpu.VMEM((3 * hw, tokens), F32),
            pltpu.VMEM((heads, tokens, tokens), F32),
            pltpu.VMEM((heads, tokens, tokens), BF),
            pltpu.VMEM((heads, tokens, tokens), BF),
            tall,
            tall,
            tall,
            pltpu.VMEM((hw, tokens), F32),
            pltpu.SemaphoreType.DMA((3,)),
        ],
        compiler_params=pltpu.CompilerParams(vmem_limit_bytes=52 * 2**20),
        name="attend",
    )(core, x, affine, wt, qg, kg)


def split_kernel(core_ref, which_ref, x_ref, affine_ref, wt_hbm, gp_keep_ref, gp_send_ref, att_ref,
                 send_ref, keep_ref, wt_s, gp_s, sems):
    tokens, _ = x_ref.shape
    width = affine_ref.shape[1]
    hw = att_ref.shape[0]
    parts = [pl.ds(part * hw, hw) for part in range(3)]
    copies = fetch([(wt_hbm.at[rows], wt_s.at[rows]) for rows in parts], sems)
    unit, inverse = unit_of(x_ref[:, :width].astype(F32))
    ident = eye(tokens)
    size = gp_keep_ref.shape[0]
    gp_s[pl.ds(pl.multiple_of(core_ref[0] * size, ROWS), size), :] = gp_keep_ref[...]
    gp_s[pl.ds(pl.multiple_of((1 - core_ref[0]) * size, ROWS), size), :] = gp_send_ref[...]
    grad = jnp.zeros((tokens, width), F32)
    for part in range(3):
        at = slice(part * hw, (part + 1) * hw)
        rows = mm(ident, gp_s[at, :], NT).astype(BF)
        copies[part].wait()
        grad = grad + mm(rows, wt_s[at, :], NN)
    half = width // 2
    win = send_ref.shape[1]
    mine_low = which_ref[0] == 0
    scaled = grad * affine_ref[1:2]
    first = jnp.sum(scaled, axis=1, keepdims=True)
    second = jnp.sum(scaled * unit, axis=1, keepdims=True)
    col = lax.broadcasted_iota(jnp.int32, (tokens, win), 1)
    here = jnp.where(mine_low, half, 0)
    there = jnp.where(mine_low, 0, half)
    low, high = scaled[:, :win], scaled[:, width - win :]
    send = jnp.where(mine_low, high, low)
    keep = jnp.where(mine_low, low, high)
    for place, term in enumerate((first, second)):
        coarse = term.astype(BF).astype(F32)
        send = jnp.where(col == there + 2 * place, coarse, send)
        send = jnp.where(col == there + 2 * place + 1, term - coarse, send)
    for place, term in enumerate((first, second, inverse)):
        keep = jnp.where(col == here + place, term, keep)
    send_ref[...] = send.astype(BF)
    keep_ref[:, :win] = keep
    keep_ref[:, win : 2 * win] = jnp.where(mine_low, unit[:, :win], unit[:, width - win :])
    keep_ref[:, 2 * win : 2 * win + hw] = mm(ident, att_ref[...], NT)


def split(core, which, x, affine, wt, gp_keep, gp_send, att):
    tokens = x.shape[0]
    hw = att.shape[0]
    win = window_of(wt.shape[1] // 2)
    smem = pl.BlockSpec(memory_space=pltpu.SMEM)
    vmem = pl.BlockSpec(memory_space=pltpu.VMEM)
    return pl.pallas_call(
        split_kernel,
        in_specs=[smem, smem, vmem, vmem, pl.BlockSpec(memory_space=pltpu.HBM), vmem, vmem, vmem],
        out_shape=(
            jax.ShapeDtypeStruct((tokens, win), BF),
            jax.ShapeDtypeStruct((tokens, 2 * win + window_of(hw)), F32),
        ),
        scratch_shapes=[
            pltpu.VMEM(wt.shape, BF),
            pltpu.VMEM((wt.shape[0], tokens), BF),
            pltpu.SemaphoreType.DMA((3,)),
        ],
        compiler_params=pltpu.CompilerParams(vmem_limit_bytes=30 * 2**20),
        name="split",
    )(core, which, x, affine, wt, gp_keep, gp_send, att)


def outer_kernel(where_ref, gp_a, gp_b, mod_a, mod_b, *refs):
    out_refs, tiles_s = refs[:-1], refs[-1]
    rows, width = gp_a.shape[0], mod_a.shape[1]
    tiles = rows // ROWS
    used = tiles * (width // LANES)
    tiles_s[used:] = jnp.zeros((tiles_s.shape[0] - used, ROWS, LANES), BF)
    gp = jnp.concatenate([gp_a[...], gp_b[...]], axis=1)
    for start in range(0, width, 2 * LANES):
        stop = min(start + 2 * LANES, width)
        mod = jnp.concatenate([mod_a[:, start:stop], mod_b[:, start:stop]], axis=0)
        found = mm(gp, mod, NN).astype(BF)
        for at in range(0, stop - start, LANES):
            j = (start + at) // LANES
            tiles_s[j * tiles : (j + 1) * tiles] = found[:, at : at + LANES].reshape(tiles, ROWS, LANES)
    size = tiles_s.shape[0] // 8
    keep_ref = out_refs[-1]
    for (lo, hi), order, send_ref in zip(bounds(size), ORDERS, out_refs):
        for q in range(4):
            k = picked(q, order[1:])
            at = (where_ref[0] ^ k) * size + lo
            keep_ref[q, lo:hi] = tiles_s[pl.ds(at, hi - lo)]
            at = (where_ref[0] ^ (k ^ order[0])) * size + lo
            send_ref[q] = tiles_s[pl.ds(at, hi - lo)]


def outer(where, gp_a, gp_b, mod_a, mod_b, padded):
    smem = pl.BlockSpec(memory_space=pltpu.SMEM)
    vmem = pl.BlockSpec(memory_space=pltpu.VMEM)
    size = padded // 8
    shapes = [jax.ShapeDtypeStruct((4, n, ROWS, LANES), BF) for n in [hi - lo for lo, hi in bounds(size)] + [size]]
    return pl.pallas_call(
        outer_kernel,
        in_specs=[smem] + [vmem] * 4,
        out_shape=tuple(shapes),
        scratch_shapes=[pltpu.VMEM((padded, ROWS, LANES), BF)],
        compiler_params=pltpu.CompilerParams(vmem_limit_bytes=16 * 2**20),
        name="outer",
    )(where, gp_a, gp_b, mod_a, mod_b)


ORDERS = ((1, 3, 4), (3, 4, 1), (4, 1, 3))


def bounds(size):
    cuts = [0, -(-size // 3), -(-2 * size // 3), size]
    return list(zip(cuts[:-1], cuts[1:]))


def picked(q, masks):
    return (masks[0] if q % 2 else 0) ^ (masks[1] if q // 2 else 0)


def window_of(half):
    return -(-half // LANES) * LANES


def finish_kernel(which_ref, recv_ref, keep_ref, out_ref, *, width):
    half = width // 2
    win = recv_ref.shape[1]
    mine_low = which_ref[0] == 0
    recv = recv_ref[...].astype(F32)
    keep = keep_ref[:, :win]
    unit = keep_ref[:, win : 2 * win]

    def column(block, place):
        return jnp.where(mine_low, block[:, half + place : half + place + 1], block[:, place : place + 1])

    first = column(keep, 0) + (column(recv, 0) + column(recv, 1))
    second = column(keep, 1) + (column(recv, 2) + column(recv, 3))
    inverse = column(keep, 2)
    grad = keep + recv
    out = inverse * (grad - first * (1.0 / width) - unit * (second * (1.0 / width)))
    moved = pltpu.roll(out, win - (win - half), 1)
    out_ref[:, :half] = jnp.where(mine_low, out, moved)[:, :half].astype(BF)
    out_ref[:, half:] = keep_ref[:, 2 * win : 2 * win + width - half].astype(BF)


def finish(which, recv, keep, width):
    tokens = recv.shape[0]
    smem = pl.BlockSpec(memory_space=pltpu.SMEM)
    vmem = pl.BlockSpec(memory_space=pltpu.VMEM)
    return pl.pallas_call(
        functools.partial(finish_kernel, width=width),
        in_specs=[smem, vmem, vmem],
        out_shape=jax.ShapeDtypeStruct((tokens, width), BF),
        compiler_params=pltpu.CompilerParams(vmem_limit_bytes=24 * 2**20),
        name="finish",
    )(which, recv, keep)


def fold_kernel(keep_ref, *refs):
    count = (len(refs) - 1) // 2
    got_refs, send_refs, left_ref = refs[:count], refs[count:-1], refs[-1]
    for (lo, hi), got_ref, send_ref in zip(bounds(keep_ref.shape[1]), got_refs, send_refs):
        for q in range(keep_ref.shape[0]):
            total = (keep_ref[q, lo:hi].astype(F32) + got_ref[q].astype(F32)).astype(BF)
            if q % 2:
                send_ref[q // 2] = total
            else:
                left_ref[q // 2, lo:hi] = total


def fold(keep, got):
    shapes = [jax.ShapeDtypeStruct((x.shape[0] // 2,) + x.shape[1:], BF) for x in (*got, keep)]
    found = pl.pallas_call(
        fold_kernel,
        out_shape=tuple(shapes),
        compiler_params=pltpu.CompilerParams(vmem_limit_bytes=8 * 2**20),
        name="fold",
    )(keep, *got)
    return found[:-1], found[-1]


def close_kernel(keep_ref, *refs):
    out_ref = refs[-1]
    for (lo, hi), got_ref in zip(bounds(keep_ref.shape[1]), refs):
        out_ref[lo:hi] = (keep_ref[0, lo:hi].astype(F32) + got_ref[0].astype(F32)).astype(BF)


def close(keep, got):
    return pl.pallas_call(
        close_kernel,
        out_shape=jax.ShapeDtypeStruct(keep.shape[1:], BF),
        compiler_params=pltpu.CompilerParams(vmem_limit_bytes=8 * 2**20),
        name="close",
    )(keep, *got)


def join_kernel(*refs):
    count = len(refs) // 3
    for i in range(count):
        have_ref, got_ref, out_ref = refs[2 * i], refs[2 * i + 1], refs[2 * count + i]
        size = have_ref.shape[0]
        out_ref[:size] = have_ref[...]
        out_ref[size:] = got_ref[...]


def join(pairs):
    shapes = [jax.ShapeDtypeStruct((2 * have.shape[0],) + have.shape[1:], BF) for have, _ in pairs]
    return pl.pallas_call(
        join_kernel,
        out_shape=tuple(shapes),
        compiler_params=pltpu.CompilerParams(vmem_limit_bytes=8 * 2**20),
        name="join",
    )(*[x for pair in pairs for x in pair])


def reduce_kernel(parts_ref, out_ref, *, factor):
    out_ref[...] = (jnp.sum(parts_ref[...].astype(F32), axis=0) * factor).astype(BF)


def reduce(parts, factor):
    return pl.pallas_call(
        functools.partial(reduce_kernel, factor=factor),
        out_shape=jax.ShapeDtypeStruct(parts.shape[1:], BF),
        compiler_params=pltpu.CompilerParams(vmem_limit_bytes=4 * 2**20),
        name="reduce",
    )(parts)


def trio_kernel(own_ref, below_ref, above_ref, all_ref, two_ref):
    size = own_ref.shape[0]
    for i, ref in enumerate((below_ref, own_ref, above_ref)):
        all_ref[i * size : (i + 1) * size] = ref[...]
        if i < 2:
            two_ref[i * size : (i + 1) * size] = ref[...]


def trio(own, below, above):
    size = own.shape[0]
    return pl.pallas_call(
        trio_kernel,
        out_shape=tuple(jax.ShapeDtypeStruct((n * size,) + own.shape[1:], BF) for n in (3, 2)),
        compiler_params=pltpu.CompilerParams(vmem_limit_bytes=4 * 2**20),
        name="trio",
    )(own, below, above)


def place_kernel(clip_ref, near_ref, below_ref, above_ref, *refs, clips):
    out_refs, all_s = refs[:-1], refs[-1]
    size = all_s.shape[0] // clips
    for ref, first in ((near_ref, -1), (below_ref, -4), (above_ref, 2)):
        for i in range(ref.shape[0] // size):
            at = lax.rem(clip_ref[0] + (first + i + clips), clips) * size
            all_s[pl.ds(at, size)] = ref[i * size : (i + 1) * size]
    for (lo, hi), out_ref in zip(bounds(clips * size), out_refs):
        out_ref[0] = all_s[lo:hi]


def place(clip, near, below, above, clips):
    total = near.shape[0] // 3 * clips
    smem = pl.BlockSpec(memory_space=pltpu.SMEM)
    vmem = pl.BlockSpec(memory_space=pltpu.VMEM)
    return pl.pallas_call(
        functools.partial(place_kernel, clips=clips),
        in_specs=[smem, vmem, vmem, vmem],
        out_shape=tuple(jax.ShapeDtypeStruct((1, hi - lo, ROWS, LANES), BF) for lo, hi in bounds(total)),
        scratch_shapes=[pltpu.VMEM((total, ROWS, LANES), BF)],
        compiler_params=pltpu.CompilerParams(vmem_limit_bytes=4 * 2**20),
        name="place",
    )(clip, near, below, above)


def untile_kernel(where_ref, half_ref, *refs):
    pieces, (out_ref, tiles_s) = refs[:-2], refs[-2:]
    size = tiles_s.shape[0] // 16
    pieces = iter(pieces)
    for side in range(2):
        half = half_ref[0] ^ side
        for far in range(2):
            for (lo, hi), order in zip(bounds(size), ORDERS):
                piece = next(pieces)
                for q in range(4):
                    k = picked(q, (order[2], order[1])) ^ (order[0] * far)
                    at = (half * 8 + (where_ref[0] ^ k)) * size + lo
                    tiles_s[pl.ds(at, hi - lo)] = piece[q]
    rows = out_ref.shape[0] // 2
    tiles = rows // ROWS
    for half in range(2):
        for j in range(out_ref.shape[1] // LANES):
            start = half * 8 * size + j * tiles
            block = tiles_s[start : start + tiles].reshape(rows, LANES)
            out_ref[half * rows : (half + 1) * rows, j * LANES : (j + 1) * LANES] = block


def untile(where, half, pieces, rows, width):
    smem = pl.BlockSpec(memory_space=pltpu.SMEM)
    vmem = pl.BlockSpec(memory_space=pltpu.VMEM)
    tiles = sum(4 * piece.shape[1] for piece in pieces)
    return pl.pallas_call(
        untile_kernel,
        in_specs=[smem, smem] + [vmem] * len(pieces),
        out_shape=jax.ShapeDtypeStruct((rows, width), BF),
        scratch_shapes=[pltpu.VMEM((tiles, ROWS, LANES), BF)],
        compiler_params=pltpu.CompilerParams(vmem_limit_bytes=16 * 2**20),
        name="untile",
    )(where, half, *pieces)


def swap(x, axes, k):
    count = math.prod(lax.axis_size(a) for a in axes)
    return lax.ppermute(x, axes, [(i, i ^ k) for i in range(count)])


def exchange(x, axis):
    parts = x.reshape((-1,) + x.shape[-3:])
    return lax.all_to_all(parts, axis, split_axis=0, concat_axis=0, tiled=True)


def meet(blocks, level):
    return [swap(block, PLANE, order[level]) for block, order in zip(blocks, ORDERS)]


def sum_plane(found, beside):
    send, keep = found[:-1], found[-1]
    got, beside = lax.optimization_barrier((meet(send, 0), beside))
    send, keep = fold(keep, got)
    send, keep = fold(keep, meet(send, 1))
    return close(keep, meet(send, 2)), beside


def shift(x, axis, step):
    count = lax.axis_size(axis)
    return lax.ppermute(x, axis, [(i, (i + step) % count) for i in range(count)])


def gather_clips(own, home):
    near, two = trio(own, shift(own, "dp", 1), shift(own, "dp", -1))
    near, two, home = lax.optimization_barrier((near, two, home))
    return near, shift(near, "dp", 3), shift(two, "dp", -3), home


def gather_plane(have, where, half, rows, width):
    have = join(list(zip(have, meet(have, 2))))
    have = join(list(zip(have, meet(have, 1))))
    pieces = list(have) + meet(have, 0)
    pieces = pieces + [swap(piece, ("core",), 1) for piece in pieces]
    return untile(where, half, pieces, rows, width)


def body(latent, mod_shift, mod_scale, w_qkv, q_gain, k_gain, cotangent):
    _, _, patches, width = latent.shape
    hw = w_qkv.shape[2]
    hd = q_gain.shape[0]
    heads = hw // hd
    frames = 1
    for a in SEQ:
        frames *= lax.axis_size(a)
    own_patches = patches // frames
    clips = lax.axis_size("dp")
    wt = w_qkv.transpose(1, 2, 0).reshape(3 * hw, width)
    x = pack(latent[0, 0], cotangent[0, 0].T).reshape(frames, own_patches, width + hw)
    x = lax.all_to_all(x, SEQ, split_axis=0, concat_axis=0, tiled=True).reshape(patches, width + hw)
    affine = jnp.concatenate([mod_shift, 1.0 + mod_scale])
    core = lax.axis_index("core").astype(jnp.int32).reshape(1)
    which = lax.axis_index("tensor").astype(jnp.int32).reshape(1)
    where = lax.axis_index(PLANE).astype(jnp.int32).reshape(1)
    mod, gp_keep, gp_send, att_t = attend(
        core, x, affine, wt, q_gain[:, None], k_gain[:, None], own_patches, heads, hd
    )
    used = (3 * hw // 2 // ROWS) * (width // LANES)
    group = 8 * clips
    padded = -(-used // group) * group
    gp_other, mod_other = swap(gp_send, ("core",), 1), swap(mod, ("core",), 1)
    found = outer(where, gp_keep, gp_other, mod, mod_other, padded)
    send, keep = split(core, which, x, affine, wt, gp_keep, gp_send, att_t)
    own, send = sum_plane(found, send)
    own, send = lax.optimization_barrier((own, send))
    recv = lax.ppermute(send, "tensor", [(0, 1), (1, 0)])
    own = exchange(own.reshape((clips, own.shape[0] // clips) + own.shape[1:]), "dp")
    own, recv = lax.optimization_barrier((own, recv))
    own = reduce(own, 1.0 / math.sqrt(clips * frames * patches))
    home = finish(which, recv, keep, width).reshape(frames, own_patches, width)
    near, below, above, home = gather_clips(own, home)
    home = lax.all_to_all(home, SEQ, split_axis=0, concat_axis=0, tiled=True)
    below, home = lax.optimization_barrier((below, home))
    grad_t, att_t = unpack(home.reshape(patches, width))
    clip = lax.axis_index("dp").astype(jnp.int32).reshape(1)
    have = place(clip, near, below, above, clips)
    grad_qkv = gather_plane(have, where, core, 3 * hw, width)
    grad_qkv = grad_qkv.reshape(3, hw, width).transpose(2, 0, 1)
    return (att_t.T[None, None], grad_t.T[None, None], grad_qkv)


def solution(mesh):
    fine = Mesh(mesh.devices.reshape(mesh.shape["dp"], 2, 4, 2, 2), ("dp",) + SEQ + ("tensor",))
    in_specs = (
        P("dp", SEQ, None, None),
        P("dp", None),
        P("dp", None),
        P(None, None, "tensor"),
        P(),
        P(),
        P("dp", SEQ, None, "tensor"),
    )
    out_specs = (
        P("dp", SEQ, None, "tensor"),
        P("dp", SEQ, None, "tensor"),
        P(None, None, "tensor"),
    )
    return jax.shard_map(body, mesh=fine, in_specs=in_specs, out_specs=out_specs, check_vma=False)
```

```python
import functools
import math

import jax
import jax.numpy as jnp
from jax import lax
from jax.experimental import pallas as pl
from jax.experimental.pallas import tpu as pltpu
from jax.sharding import Mesh, PartitionSpec as P

BF = jnp.bfloat16
F32 = jnp.float32
EPS = 1e-06
NN = (((1,), (0,)), ((), ()))
NT = (((1,), (1,)), ((), ()))
LOG2E = math.log2(math.e)
ROWS, LANES = 16, 128
PLANE = ("xlo", "y")
SEQ = PLANE + ("core",)


def mm(a, b, dims):
    return lax.dot_general(a, b, dims, preferred_element_type=F32)


def eye(n):
    rows = lax.broadcasted_iota(jnp.int32, (n, n), 0)
    cols = lax.broadcasted_iota(jnp.int32, (n, n), 1)
    return jnp.where(rows == cols, 1.0, 0.0).astype(BF)


def fetch(pairs, sems):
    copies = [pltpu.make_async_copy(src, dst, sems.at[i]) for i, (src, dst) in enumerate(pairs)]
    for copy in copies:
        copy.start()
    return copies


def pack_kernel(latent_hbm, cot_hbm, out_ref, latent_s, cot_s, sems):
    width = latent_s.shape[1]
    first, second = fetch([(cot_hbm, cot_s), (latent_hbm, latent_s)], sems)
    ident = eye(latent_s.shape[0])
    first.wait()
    out_ref[:, width:] = mm(ident, cot_s[...], NT).astype(BF)
    second.wait()
    out_ref[:, :width] = latent_s[...]


def pack(latent, cot_t):
    tokens, width = latent.shape
    hbm = pl.BlockSpec(memory_space=pltpu.HBM)
    return pl.pallas_call(
        pack_kernel,
        in_specs=[hbm, hbm],
        out_shape=jax.ShapeDtypeStruct((tokens, width + cot_t.shape[0]), BF),
        scratch_shapes=[
            pltpu.VMEM(latent.shape, BF),
            pltpu.VMEM(cot_t.shape, BF),
            pltpu.SemaphoreType.DMA((2,)),
        ],
        compiler_params=pltpu.CompilerParams(vmem_limit_bytes=60 * 2**20),
        name="pack",
    )(latent, cot_t)


def unpack_kernel(rows_ref, first_ref, second_ref):
    ident = eye(LANES)
    half = first_ref.shape[0]
    for start in range(0, 2 * half, LANES):
        found = mm(ident, rows_ref[:, start : start + LANES], NT).astype(BF)
        cut = min(max(half - start, 0), LANES)
        if cut:
            first_ref[start : start + cut] = found[:cut]
        if cut < LANES:
            second_ref[start + cut - half : start + LANES - half] = found[cut:]


def unpack(rows):
    tokens, width = rows.shape
    shape = jax.ShapeDtypeStruct((width // 2, tokens), BF)
    return pl.pallas_call(
        unpack_kernel,
        out_shape=(shape, shape),
        compiler_params=pltpu.CompilerParams(vmem_limit_bytes=8 * 2**20),
        name="unpack",
    )(rows)


def unit_of(values):
    width = values.shape[1]
    centred = values - jnp.sum(values, axis=1, keepdims=True) * (1.0 / width)
    inverse = lax.rsqrt(jnp.sum(centred * centred, axis=1, keepdims=True) * (1.0 / width) + EPS)
    return centred * inverse, inverse


def attend_kernel(core_ref, x_ref, affine_ref, wt_hbm, qg_ref, kg_ref,
                  mod_ref, gp_keep_ref, gp_send_ref, att_ref,
                  wt_s, rows_s, weights_s, w_s, grad_s, q_s, k_s, v_s, cot_s, sems, *, patches, heads, hd):
    tokens, _ = x_ref.shape
    width = affine_ref.shape[1]
    hw = heads * hd
    parts = [pl.ds(part * hw, hw) for part in range(3)]
    copies = fetch([(wt_hbm.at[rows], wt_s.at[rows]) for rows in parts], sems)
    unit, _ = unit_of(x_ref[:, :width].astype(F32))
    mod_ref[...] = (unit * affine_ref[1:2] + affine_ref[0:1]).astype(BF)
    mod = mod_ref[...]
    ident = eye(tokens)
    for start in range(0, hw, tokens):
        size = min(tokens, hw - start)
        block = x_ref[:, width + start : width + start + size]
        cot_s[start : start + size, :] = mm(ident[:size, :size], block, NT)

    def project(part):
        copies[part].wait()
        return mm(wt_s[part * hw : (part + 1) * hw, :], mod, NT).astype(BF).astype(F32)

    def norm(rows):
        inv = lax.rsqrt(jnp.sum(rows * rows, axis=0, keepdims=True) * (1.0 / hd) + EPS)
        return rows * inv, inv

    def back(hat, inv, gain, grad):
        weighted = grad * gain
        mean = jnp.sum(hat * weighted, axis=0, keepdims=True) * (1.0 / hd)
        return inv * (weighted - hat * mean)

    def put(part, h, rows):
        start = part * hw + h * hd
        rows_s[start : start + hd, :] = rows

    root = 1.0 / math.sqrt(hd)
    q_gain = qg_ref[...] * (root * LOG2E)
    k_gain = kg_ref[...]
    q_back = qg_ref[...] * root
    k_back = kg_ref[...] * (1.0 / LOG2E)
    each = [slice(h * hd, (h + 1) * hd) for h in range(heads)]

    spot = lax.broadcasted_iota(jnp.int32, (patches, tokens), 0)
    token = lax.broadcasted_iota(jnp.int32, (patches, tokens), 1)
    spots = jnp.where(lax.rem(token, patches) == spot, 16.0, 0.0)
    top = lax.broadcasted_iota(jnp.int32, (8, tokens), 0) == 0
    zeros = jnp.zeros((-(hd + patches + 8) % LANES, tokens), F32)
    q_tail = [spots, jnp.where(top, 16.0, 0.0), zeros]
    k_tail = [spots, jnp.where(top, -16.0, 0.0), zeros]
    v_tail = [jnp.where(top, 1.0, 0.0), jnp.zeros((-(hd + 8) % LANES, tokens), F32)]
    blank = jnp.zeros((-hd % LANES, tokens), F32)

    def rows_of(ref):
        found = []
        for h in range(0, heads, 2):
            both = mm(ident, ref[h : h + 2].reshape(2 * LANES, tokens), NT).astype(BF)
            found += [both[:, :LANES], both[:, LANES:]]
        return found

    q_all = project(0)
    q_inv = []
    for h, at in enumerate(each):
        hat, inv = norm(q_all[at])
        q_inv.append(inv)
        q_s[h] = jnp.concatenate([hat * q_gain] + q_tail).astype(BF)
    k_all = project(1)
    k_inv = []
    for h, at in enumerate(each):
        hat, inv = norm(k_all[at])
        k_inv.append(inv)
        k_s[h] = jnp.concatenate([hat * k_gain] + k_tail).astype(BF)
    v_all = project(2)
    for h, at in enumerate(each):
        v_s[h] = jnp.concatenate([v_all[at]] + v_tail).astype(BF)
    k_rows = rows_of(k_s)
    for h in range(heads):
        weights = jnp.exp2(mm(k_rows[h], q_s[h], NN))
        weights_s[h] = weights
        w_s[h] = weights.astype(BF)
    v_rows = rows_of(v_s)
    deltas, cots = [], []
    for h, at in enumerate(each):
        summed = mm(v_s[h], w_s[h], NN)
        share = 1.0 / summed[hd : hd + 1]
        out = summed[:hd] * share
        att_ref[at, :] = out.astype(BF)
        cot_share = cot_s[at, :] * share
        cots.append(jnp.concatenate([cot_share, blank]).astype(BF))
        deltas.append(jnp.sum(out * cot_share, axis=0, keepdims=True))
    for h in range(heads):
        grad_s[h] = (weights_s[h] * (mm(v_rows[h], cots[h], NN) - deltas[h])).astype(BF)
        put(2, h, mm(cots[h], w_s[h], NT)[:hd])
    for h, at in enumerate(each):
        put(0, h, back(q_all[at] * q_inv[h], q_inv[h], q_back, mm(k_s[h], grad_s[h], NN)[:hd]))
        put(1, h, back(k_all[at] * k_inv[h], k_inv[h], k_back, mm(q_s[h], grad_s[h], NT)[:hd]))
    size = gp_keep_ref.shape[0]
    gp_keep_ref[...] = rows_s[pl.ds(pl.multiple_of(core_ref[0] * size, ROWS), size), :].astype(BF)
    gp_send_ref[...] = rows_s[pl.ds(pl.multiple_of((1 - core_ref[0]) * size, ROWS), size), :].astype(BF)


def attend(core, x, affine, wt, qg, kg, patches, heads, hd):
    tokens = x.shape[0]
    width = wt.shape[1]
    hw = heads * hd
    smem = pl.BlockSpec(memory_space=pltpu.SMEM)
    vmem = pl.BlockSpec(memory_space=pltpu.VMEM)
    half = jax.ShapeDtypeStruct((3 * hw // 2, tokens), BF)
    tall = pltpu.VMEM((heads, LANES, tokens), BF)
    return pl.pallas_call(
        functools.partial(attend_kernel, patches=patches, heads=heads, hd=hd),
        in_specs=[smem, vmem, vmem, pl.BlockSpec(memory_space=pltpu.HBM), vmem, vmem],
        out_shape=(
            jax.ShapeDtypeStruct((tokens, width), BF),
            half,
            half,
            jax.ShapeDtypeStruct((hw, tokens), BF),
        ),
        scratch_shapes=[
            pltpu.VMEM((3 * hw, width), BF),
            pltpu.VMEM((3 * hw, tokens), F32),
            pltpu.VMEM((heads, tokens, tokens), F32),
            pltpu.VMEM((heads, tokens, tokens), BF),
            pltpu.VMEM((heads, tokens, tokens), BF),
            tall,
            tall,
            tall,
            pltpu.VMEM((hw, tokens), F32),
            pltpu.SemaphoreType.DMA((3,)),
        ],
        compiler_params=pltpu.CompilerParams(vmem_limit_bytes=52 * 2**20),
        name="attend",
    )(core, x, affine, wt, qg, kg)


def split_kernel(core_ref, which_ref, x_hbm, affine_hbm, wt_hbm, gp_keep_hbm, gp_send_hbm, att_hbm,
                 send_ref, keep_ref, x_ref, affine_ref, wt_s, gp_keep_ref, gp_send_ref, att_ref, gp_s, sems):
    tokens, _ = x_ref.shape
    width = affine_ref.shape[1]
    hw = att_ref.shape[0]
    parts = [pl.ds(part * hw, hw) for part in range(3)]
    copies = fetch(
        [(x_hbm, x_ref), (gp_keep_hbm, gp_keep_ref), (gp_send_hbm, gp_send_ref)]
        + [(wt_hbm.at[rows], wt_s.at[rows]) for rows in parts]
        + [(affine_hbm, affine_ref), (att_hbm, att_ref)],
        sems,
    )
    for copy in copies[:3]:
        copy.wait()
    unit, inverse = unit_of(x_ref[:, :width].astype(F32))
    ident = eye(tokens)
    size = gp_keep_ref.shape[0]
    gp_s[pl.ds(pl.multiple_of(core_ref[0] * size, ROWS), size), :] = gp_keep_ref[...]
    gp_s[pl.ds(pl.multiple_of((1 - core_ref[0]) * size, ROWS), size), :] = gp_send_ref[...]
    grad = jnp.zeros((tokens, width), F32)
    for part in range(3):
        at = slice(part * hw, (part + 1) * hw)
        rows = mm(ident, gp_s[at, :], NT).astype(BF)
        copies[3 + part].wait()
        grad = grad + mm(rows, wt_s[at, :], NN)
    half = width // 2
    win = send_ref.shape[1]
    mine_low = which_ref[0] == 0
    for copy in copies[6:]:
        copy.wait()
    scaled = grad * affine_ref[1:2]
    first = jnp.sum(scaled, axis=1, keepdims=True)
    second = jnp.sum(scaled * unit, axis=1, keepdims=True)
    col = lax.broadcasted_iota(jnp.int32, (tokens, win), 1)
    here = jnp.where(mine_low, half, 0)
    there = jnp.where(mine_low, 0, half)
    low, high = scaled[:, :win], scaled[:, width - win :]
    send = jnp.where(mine_low, high, low)
    keep = jnp.where(mine_low, low, high)
    for place, term in enumerate((first, second)):
        coarse = term.astype(BF).astype(F32)
        send = jnp.where(col == there + 2 * place, coarse, send)
        send = jnp.where(col == there + 2 * place + 1, term - coarse, send)
    for place, term in enumerate((first, second, inverse)):
        keep = jnp.where(col == here + place, term, keep)
    send_ref[...] = send.astype(BF)
    keep_ref[:, :win] = keep
    keep_ref[:, win : 2 * win] = jnp.where(mine_low, unit[:, :win], unit[:, width - win :])
    keep_ref[:, 2 * win : 2 * win + hw] = mm(ident, att_ref[...], NT)


def split(core, which, x, affine, wt, gp_keep, gp_send, att):
    tokens = x.shape[0]
    hw = att.shape[0]
    win = window_of(wt.shape[1] // 2)
    smem = pl.BlockSpec(memory_space=pltpu.SMEM)
    vmem = pl.BlockSpec(memory_space=pltpu.VMEM)
    return pl.pallas_call(
        split_kernel,
        in_specs=[smem, smem] + [pl.BlockSpec(memory_space=pltpu.HBM)] * 6,
        out_shape=(
            jax.ShapeDtypeStruct((tokens, win), BF),
            jax.ShapeDtypeStruct((tokens, 2 * win + window_of(hw)), F32),
        ),
        scratch_shapes=[pltpu.VMEM(a.shape, a.dtype) for a in (x, affine, wt, gp_keep, gp_send, att)]
        + [pltpu.VMEM((wt.shape[0], tokens), BF), pltpu.SemaphoreType.DMA((8,))],
        compiler_params=pltpu.CompilerParams(vmem_limit_bytes=58 * 2**20),
        name="split",
    )(core, which, x, affine, wt, gp_keep, gp_send, att)


def outer_kernel(where_ref, gp_a, gp_b, mod_a, mod_b, *refs):
    out_refs, tiles_s = refs[:-1], refs[-1]
    rows, width = gp_a.shape[0], mod_a.shape[1]
    tiles = rows // ROWS
    used = tiles * (width // LANES)
    tiles_s[used:] = jnp.zeros((tiles_s.shape[0] - used, ROWS, LANES), BF)
    gp = jnp.concatenate([gp_a[...], gp_b[...]], axis=1)
    for start in range(0, width, 2 * LANES):
        stop = min(start + 2 * LANES, width)
        mod = jnp.concatenate([mod_a[:, start:stop], mod_b[:, start:stop]], axis=0)
        found = mm(gp, mod, NN).astype(BF)
        for at in range(0, stop - start, LANES):
            j = (start + at) // LANES
            tiles_s[j * tiles : (j + 1) * tiles] = found[:, at : at + LANES].reshape(tiles, ROWS, LANES)
    size = tiles_s.shape[0] // 8
    keep_ref = out_refs[-1]
    for (lo, hi), order, send_ref in zip(bounds(size), ORDERS, out_refs):
        for q in range(4):
            k = picked(q, order[1:])
            at = (where_ref[0] ^ k) * size + lo
            keep_ref[q, lo:hi] = tiles_s[pl.ds(at, hi - lo)]
            at = (where_ref[0] ^ (k ^ order[0])) * size + lo
            send_ref[q] = tiles_s[pl.ds(at, hi - lo)]


def outer(where, gp_a, gp_b, mod_a, mod_b, padded):
    smem = pl.BlockSpec(memory_space=pltpu.SMEM)
    vmem = pl.BlockSpec(memory_space=pltpu.VMEM)
    size = padded // 8
    shapes = [jax.ShapeDtypeStruct((4, n, ROWS, LANES), BF) for n in [hi - lo for lo, hi in bounds(size)] + [size]]
    return pl.pallas_call(
        outer_kernel,
        in_specs=[smem] + [vmem] * 4,
        out_shape=tuple(shapes),
        scratch_shapes=[pltpu.VMEM((padded, ROWS, LANES), BF)],
        compiler_params=pltpu.CompilerParams(vmem_limit_bytes=16 * 2**20),
        name="outer",
    )(where, gp_a, gp_b, mod_a, mod_b)


ORDERS = ((1, 3, 4), (3, 4, 1), (4, 1, 3))


def bounds(size):
    cuts = [0, -(-size // 3), -(-2 * size // 3), size]
    return list(zip(cuts[:-1], cuts[1:]))


def picked(q, masks):
    return (masks[0] if q % 2 else 0) ^ (masks[1] if q // 2 else 0)


def window_of(half):
    return -(-half // LANES) * LANES


def finish_kernel(which_ref, recv_ref, keep_ref, out_ref, *, width):
    half = width // 2
    win = recv_ref.shape[1]
    mine_low = which_ref[0] == 0
    recv = recv_ref[...].astype(F32)
    keep = keep_ref[:, :win]
    unit = keep_ref[:, win : 2 * win]

    def column(block, place):
        return jnp.where(mine_low, block[:, half + place : half + place + 1], block[:, place : place + 1])

    first = column(keep, 0) + (column(recv, 0) + column(recv, 1))
    second = column(keep, 1) + (column(recv, 2) + column(recv, 3))
    inverse = column(keep, 2)
    grad = keep + recv
    out = inverse * (grad - first * (1.0 / width) - unit * (second * (1.0 / width)))
    moved = pltpu.roll(out, win - (win - half), 1)
    out_ref[:, :half] = jnp.where(mine_low, out, moved)[:, :half].astype(BF)
    out_ref[:, half:] = keep_ref[:, 2 * win : 2 * win + width - half].astype(BF)


def finish(which, recv, keep, width):
    tokens = recv.shape[0]
    smem = pl.BlockSpec(memory_space=pltpu.SMEM)
    vmem = pl.BlockSpec(memory_space=pltpu.VMEM)
    return pl.pallas_call(
        functools.partial(finish_kernel, width=width),
        in_specs=[smem, vmem, vmem],
        out_shape=jax.ShapeDtypeStruct((tokens, width), BF),
        compiler_params=pltpu.CompilerParams(vmem_limit_bytes=24 * 2**20),
        name="finish",
    )(which, recv, keep)


def fold_kernel(keep_ref, *refs):
    count = (len(refs) - 1) // 2
    got_refs, send_refs, left_ref = refs[:count], refs[count:-1], refs[-1]
    for (lo, hi), got_ref, send_ref in zip(bounds(keep_ref.shape[1]), got_refs, send_refs):
        for q in range(keep_ref.shape[0]):
            total = (keep_ref[q, lo:hi].astype(F32) + got_ref[q].astype(F32)).astype(BF)
            if q % 2:
                send_ref[q // 2] = total
            else:
                left_ref[q // 2, lo:hi] = total


def fold(keep, got):
    shapes = [jax.ShapeDtypeStruct((x.shape[0] // 2,) + x.shape[1:], BF) for x in (*got, keep)]
    found = pl.pallas_call(
        fold_kernel,
        out_shape=tuple(shapes),
        compiler_params=pltpu.CompilerParams(vmem_limit_bytes=8 * 2**20),
        name="fold",
    )(keep, *got)
    return found[:-1], found[-1]


def close_kernel(keep_ref, *refs):
    out_ref = refs[-1]
    for (lo, hi), got_ref in zip(bounds(keep_ref.shape[1]), refs):
        out_ref[lo:hi] = (keep_ref[0, lo:hi].astype(F32) + got_ref[0].astype(F32)).astype(BF)


def close(keep, got):
    return pl.pallas_call(
        close_kernel,
        out_shape=jax.ShapeDtypeStruct(keep.shape[1:], BF),
        compiler_params=pltpu.CompilerParams(vmem_limit_bytes=8 * 2**20),
        name="close",
    )(keep, *got)


def join_kernel(*refs):
    count = len(refs) // 3
    for i in range(count):
        have_ref, got_ref, out_ref = refs[2 * i], refs[2 * i + 1], refs[2 * count + i]
        size = have_ref.shape[0]
        out_ref[:size] = have_ref[...]
        out_ref[size:] = got_ref[...]


def join(pairs):
    shapes = [jax.ShapeDtypeStruct((2 * have.shape[0],) + have.shape[1:], BF) for have, _ in pairs]
    return pl.pallas_call(
        join_kernel,
        out_shape=tuple(shapes),
        compiler_params=pltpu.CompilerParams(vmem_limit_bytes=8 * 2**20),
        name="join",
    )(*[x for pair in pairs for x in pair])


def reduce_kernel(parts_ref, out_ref, *, factor):
    out_ref[...] = (jnp.sum(parts_ref[...].astype(F32), axis=0) * factor).astype(BF)


def reduce(parts, factor):
    return pl.pallas_call(
        functools.partial(reduce_kernel, factor=factor),
        out_shape=jax.ShapeDtypeStruct(parts.shape[1:], BF),
        compiler_params=pltpu.CompilerParams(vmem_limit_bytes=4 * 2**20),
        name="reduce",
    )(parts)


def trio_kernel(own_ref, below_ref, above_ref, all_ref, two_ref):
    size = own_ref.shape[0]
    for i, ref in enumerate((below_ref, own_ref, above_ref)):
        all_ref[i * size : (i + 1) * size] = ref[...]
        if i < 2:
            two_ref[i * size : (i + 1) * size] = ref[...]


def trio(own, below, above):
    size = own.shape[0]
    return pl.pallas_call(
        trio_kernel,
        out_shape=tuple(jax.ShapeDtypeStruct((n * size,) + own.shape[1:], BF) for n in (3, 2)),
        compiler_params=pltpu.CompilerParams(vmem_limit_bytes=4 * 2**20),
        name="trio",
    )(own, below, above)


def place_kernel(clip_ref, near_ref, below_ref, above_ref, *refs, clips):
    out_refs, all_s = refs[:-1], refs[-1]
    size = all_s.shape[0] // clips
    for ref, first in ((near_ref, -1), (below_ref, -4), (above_ref, 2)):
        for i in range(ref.shape[0] // size):
            at = lax.rem(clip_ref[0] + (first + i + clips), clips) * size
            all_s[pl.ds(at, size)] = ref[i * size : (i + 1) * size]
    for (lo, hi), out_ref in zip(bounds(clips * size), out_refs):
        out_ref[0] = all_s[lo:hi]


def place(clip, near, below, above, clips):
    total = near.shape[0] // 3 * clips
    smem = pl.BlockSpec(memory_space=pltpu.SMEM)
    vmem = pl.BlockSpec(memory_space=pltpu.VMEM)
    return pl.pallas_call(
        functools.partial(place_kernel, clips=clips),
        in_specs=[smem, vmem, vmem, vmem],
        out_shape=tuple(jax.ShapeDtypeStruct((1, hi - lo, ROWS, LANES), BF) for lo, hi in bounds(total)),
        scratch_shapes=[pltpu.VMEM((total, ROWS, LANES), BF)],
        compiler_params=pltpu.CompilerParams(vmem_limit_bytes=4 * 2**20),
        name="place",
    )(clip, near, below, above)


def untile_kernel(where_ref, half_ref, *refs):
    pieces, (out_ref, tiles_s) = refs[:-2], refs[-2:]
    size = tiles_s.shape[0] // 16
    pieces = iter(pieces)
    for side in range(2):
        half = half_ref[0] ^ side
        for far in range(2):
            for (lo, hi), order in zip(bounds(size), ORDERS):
                piece = next(pieces)
                for q in range(4):
                    k = picked(q, (order[2], order[1])) ^ (order[0] * far)
                    at = (half * 8 + (where_ref[0] ^ k)) * size + lo
                    tiles_s[pl.ds(at, hi - lo)] = piece[q]
    rows = out_ref.shape[0] // 2
    tiles = rows // ROWS
    for half in range(2):
        for j in range(out_ref.shape[1] // LANES):
            start = half * 8 * size + j * tiles
            block = tiles_s[start : start + tiles].reshape(rows, LANES)
            out_ref[half * rows : (half + 1) * rows, j * LANES : (j + 1) * LANES] = block


def untile(where, half, pieces, rows, width):
    smem = pl.BlockSpec(memory_space=pltpu.SMEM)
    vmem = pl.BlockSpec(memory_space=pltpu.VMEM)
    tiles = sum(4 * piece.shape[1] for piece in pieces)
    return pl.pallas_call(
        untile_kernel,
        in_specs=[smem, smem] + [vmem] * len(pieces),
        out_shape=jax.ShapeDtypeStruct((rows, width), BF),
        scratch_shapes=[pltpu.VMEM((tiles, ROWS, LANES), BF)],
        compiler_params=pltpu.CompilerParams(vmem_limit_bytes=16 * 2**20),
        name="untile",
    )(where, half, *pieces)


def swap(x, axes, k):
    count = math.prod(lax.axis_size(a) for a in axes)
    return lax.ppermute(x, axes, [(i, i ^ k) for i in range(count)])


def exchange(x, axis):
    parts = x.reshape((-1,) + x.shape[-3:])
    return lax.all_to_all(parts, axis, split_axis=0, concat_axis=0, tiled=True)


def meet(blocks, level):
    return [swap(block, PLANE, order[level]) for block, order in zip(blocks, ORDERS)]


def sum_plane(found, beside):
    send, keep = found[:-1], found[-1]
    got, beside = lax.optimization_barrier((meet(send, 0), beside))
    send, keep = fold(keep, got)
    send, keep = fold(keep, meet(send, 1))
    return close(keep, meet(send, 2)), beside


def shift(x, axis, step):
    count = lax.axis_size(axis)
    return lax.ppermute(x, axis, [(i, (i + step) % count) for i in range(count)])


def gather_clips(own, home):
    below, above = shift(own, "dp", 1), shift(own, "dp", -1)
    near, two = trio(own, below, above)
    return near, shift(near, "dp", 3), shift(two, "dp", -3), home


def gather_plane(have, where, half, rows, width, beside):
    got, beside = lax.optimization_barrier((meet(have, 2), beside))
    have = join(list(zip(have, got)))
    have = join(list(zip(have, meet(have, 1))))
    pieces = list(have) + meet(have, 0)
    pieces = pieces + [swap(piece, ("core",), 1) for piece in pieces]
    return untile(where, half, pieces, rows, width), beside


def body(latent, mod_shift, mod_scale, w_qkv, q_gain, k_gain, cotangent):
    _, _, patches, width = latent.shape
    hw = w_qkv.shape[2]
    hd = q_gain.shape[0]
    heads = hw // hd
    frames = 1
    for a in SEQ:
        frames *= lax.axis_size(a)
    own_patches = patches // frames
    clips = lax.axis_size("dp")
    wt = w_qkv.transpose(1, 2, 0).reshape(3 * hw, width)
    x = pack(latent[0, 0], cotangent[0, 0].T).reshape(frames, own_patches, width + hw)
    x = lax.all_to_all(x, SEQ, split_axis=0, concat_axis=0, tiled=True).reshape(patches, width + hw)
    affine = jnp.concatenate([mod_shift, 1.0 + mod_scale])
    core = lax.axis_index("core").astype(jnp.int32).reshape(1)
    which = lax.axis_index("tensor").astype(jnp.int32).reshape(1)
    where = lax.axis_index(PLANE).astype(jnp.int32).reshape(1)
    mod, gp_keep, gp_send, att_t = attend(
        core, x, affine, wt, q_gain[:, None], k_gain[:, None], own_patches, heads, hd
    )
    used = (3 * hw // 2 // ROWS) * (width // LANES)
    group = 8 * clips
    padded = -(-used // group) * group
    gp_other, mod_other = swap(gp_send, ("core",), 1), swap(mod, ("core",), 1)
    found = outer(where, gp_keep, gp_other, mod, mod_other, padded)
    send, keep = split(core, which, x, affine, wt, gp_keep, gp_send, att_t)
    own, send = sum_plane(found, send)
    own, send = lax.optimization_barrier((own, send))
    recv = lax.ppermute(send, "tensor", [(0, 1), (1, 0)])
    own = exchange(own.reshape((clips, own.shape[0] // clips) + own.shape[1:]), "dp")
    own = reduce(own, 1.0 / math.sqrt(clips * frames * patches))
    own, recv = lax.optimization_barrier((own, recv))
    home = finish(which, recv, keep, width).reshape(frames, own_patches, width)
    near, below, above, home = gather_clips(own, home)
    home = lax.all_to_all(home, SEQ, split_axis=0, concat_axis=0, tiled=True)
    clip = lax.axis_index("dp").astype(jnp.int32).reshape(1)
    have = place(clip, near, below, above, clips)
    grad_qkv, home = gather_plane(have, where, core, 3 * hw, width, home)
    grad_t, att_t = unpack(home.reshape(patches, width))
    grad_qkv = grad_qkv.reshape(3, hw, width).transpose(2, 0, 1)
    return (att_t.T[None, None], grad_t.T[None, None], grad_qkv)


def solution(mesh):
    fine = Mesh(mesh.devices.reshape(mesh.shape["dp"], 2, 4, 2, 2), ("dp",) + SEQ + ("tensor",))
    in_specs = (
        P("dp", SEQ, None, None),
        P("dp", None),
        P("dp", None),
        P(None, None, "tensor"),
        P(),
        P(),
        P("dp", SEQ, None, "tensor"),
    )
    out_specs = (
        P("dp", SEQ, None, "tensor"),
        P("dp", SEQ, None, "tensor"),
        P(None, None, "tensor"),
    )
    return jax.shard_map(body, mesh=fine, in_specs=in_specs, out_specs=out_specs, check_vma=False)
```

```python
import functools
import math

import jax
import jax.numpy as jnp
from jax import lax
from jax.experimental import pallas as pl
from jax.experimental.pallas import tpu as pltpu
from jax.sharding import Mesh, PartitionSpec as P

BF = jnp.bfloat16
F32 = jnp.float32
EPS = 1e-06
NN = (((1,), (0,)), ((), ()))
NT = (((1,), (1,)), ((), ()))
LOG2E = math.log2(math.e)
ROWS, LANES = 16, 128
PLANE = ("xlo", "y")
SEQ = PLANE + ("core",)


def mm(a, b, dims):
    return lax.dot_general(a, b, dims, preferred_element_type=F32)


def eye(n):
    rows = lax.broadcasted_iota(jnp.int32, (n, n), 0)
    cols = lax.broadcasted_iota(jnp.int32, (n, n), 1)
    return jnp.where(rows == cols, 1.0, 0.0).astype(BF)


def fetch(pairs, sems):
    copies = [pltpu.make_async_copy(src, dst, sems.at[i]) for i, (src, dst) in enumerate(pairs)]
    for copy in copies:
        copy.start()
    return copies


def pack_kernel(latent_hbm, cot_hbm, out_ref, latent_s, cot_s, sems):
    width = latent_s.shape[1]
    first, second = fetch([(cot_hbm, cot_s), (latent_hbm, latent_s)], sems)
    ident = eye(latent_s.shape[0])
    first.wait()
    out_ref[:, width:] = mm(ident, cot_s[...], NT).astype(BF)
    second.wait()
    out_ref[:, :width] = latent_s[...]


def pack(latent, cot_t):
    tokens, width = latent.shape
    hbm = pl.BlockSpec(memory_space=pltpu.HBM)
    return pl.pallas_call(
        pack_kernel,
        in_specs=[hbm, hbm],
        out_shape=jax.ShapeDtypeStruct((tokens, width + cot_t.shape[0]), BF),
        scratch_shapes=[
            pltpu.VMEM(latent.shape, BF),
            pltpu.VMEM(cot_t.shape, BF),
            pltpu.SemaphoreType.DMA((2,)),
        ],
        compiler_params=pltpu.CompilerParams(vmem_limit_bytes=60 * 2**20),
        name="pack",
    )(latent, cot_t)


def unpack_kernel(rows_ref, first_ref, second_ref):
    ident = eye(LANES)
    half = first_ref.shape[0]
    for start in range(0, 2 * half, LANES):
        found = mm(ident, rows_ref[:, start : start + LANES], NT).astype(BF)
        cut = min(max(half - start, 0), LANES)
        if cut:
            first_ref[start : start + cut] = found[:cut]
        if cut < LANES:
            second_ref[start + cut - half : start + LANES - half] = found[cut:]


def unpack(rows):
    tokens, width = rows.shape
    shape = jax.ShapeDtypeStruct((width // 2, tokens), BF)
    return pl.pallas_call(
        unpack_kernel,
        out_shape=(shape, shape),
        compiler_params=pltpu.CompilerParams(vmem_limit_bytes=8 * 2**20),
        name="unpack",
    )(rows)


def unit_of(values):
    width = values.shape[1]
    centred = values - jnp.sum(values, axis=1, keepdims=True) * (1.0 / width)
    inverse = lax.rsqrt(jnp.sum(centred * centred, axis=1, keepdims=True) * (1.0 / width) + EPS)
    return centred * inverse, inverse


def attend_kernel(core_ref, x_ref, affine_ref, wt_hbm, qg_ref, kg_ref,
                  mod_ref, gp_keep_ref, gp_send_ref, att_ref,
                  wt_s, rows_s, weights_s, w_s, grad_s, q_s, k_s, v_s, cot_s, sems, *, patches, heads, hd):
    tokens, _ = x_ref.shape
    width = affine_ref.shape[1]
    hw = heads * hd
    parts = [pl.ds(part * hw, hw) for part in range(3)]
    copies = fetch([(wt_hbm.at[rows], wt_s.at[rows]) for rows in parts], sems)
    unit, _ = unit_of(x_ref[:, :width].astype(F32))
    mod_ref[...] = (unit * affine_ref[1:2] + affine_ref[0:1]).astype(BF)
    mod = mod_ref[...]
    ident = eye(tokens)
    for start in range(0, hw, tokens):
        size = min(tokens, hw - start)
        block = x_ref[:, width + start : width + start + size]
        cot_s[start : start + size, :] = mm(ident[:size, :size], block, NT)

    def project(part):
        copies[part].wait()
        return mm(wt_s[part * hw : (part + 1) * hw, :], mod, NT).astype(BF).astype(F32)

    def norm(rows):
        inv = lax.rsqrt(jnp.sum(rows * rows, axis=0, keepdims=True) * (1.0 / hd) + EPS)
        return rows * inv, inv

    def back(hat, inv, gain, grad):
        weighted = grad * gain
        mean = jnp.sum(hat * weighted, axis=0, keepdims=True) * (1.0 / hd)
        return inv * (weighted - hat * mean)

    def put(part, h, rows):
        start = part * hw + h * hd
        rows_s[start : start + hd, :] = rows

    root = 1.0 / math.sqrt(hd)
    q_gain = qg_ref[...] * (root * LOG2E)
    k_gain = kg_ref[...]
    q_back = qg_ref[...] * root
    k_back = kg_ref[...] * (1.0 / LOG2E)
    each = [slice(h * hd, (h + 1) * hd) for h in range(heads)]

    spot = lax.broadcasted_iota(jnp.int32, (patches, tokens), 0)
    token = lax.broadcasted_iota(jnp.int32, (patches, tokens), 1)
    spots = jnp.where(lax.rem(token, patches) == spot, 16.0, 0.0)
    top = lax.broadcasted_iota(jnp.int32, (8, tokens), 0) == 0
    zeros = jnp.zeros((-(hd + patches + 8) % LANES, tokens), F32)
    q_tail = [spots, jnp.where(top, 16.0, 0.0), zeros]
    k_tail = [spots, jnp.where(top, -16.0, 0.0), zeros]
    v_tail = [jnp.where(top, 1.0, 0.0), jnp.zeros((-(hd + 8) % LANES, tokens), F32)]
    blank = jnp.zeros((-hd % LANES, tokens), F32)

    def rows_of(ref):
        found = []
        for h in range(0, heads, 2):
            both = mm(ident, ref[h : h + 2].reshape(2 * LANES, tokens), NT).astype(BF)
            found += [both[:, :LANES], both[:, LANES:]]
        return found

    q_all = project(0)
    q_inv = []
    for h, at in enumerate(each):
        hat, inv = norm(q_all[at])
        q_inv.append(inv)
        q_s[h] = jnp.concatenate([hat * q_gain] + q_tail).astype(BF)
    k_all = project(1)
    k_inv = []
    for h, at in enumerate(each):
        hat, inv = norm(k_all[at])
        k_inv.append(inv)
        k_s[h] = jnp.concatenate([hat * k_gain] + k_tail).astype(BF)
    v_all = project(2)
    for h, at in enumerate(each):
        v_s[h] = jnp.concatenate([v_all[at]] + v_tail).astype(BF)
    k_rows = rows_of(k_s)
    for h in range(heads):
        weights = jnp.exp2(mm(k_rows[h], q_s[h], NN))
        weights_s[h] = weights
        w_s[h] = weights.astype(BF)
    v_rows = rows_of(v_s)
    deltas, cots = [], []
    for h, at in enumerate(each):
        summed = mm(v_s[h], w_s[h], NN)
        share = 1.0 / summed[hd : hd + 1]
        out = summed[:hd] * share
        att_ref[at, :] = out.astype(BF)
        cot_share = cot_s[at, :] * share
        cots.append(jnp.concatenate([cot_share, blank]).astype(BF))
        deltas.append(jnp.sum(out * cot_share, axis=0, keepdims=True))
    for h in range(heads):
        grad_s[h] = (weights_s[h] * (mm(v_rows[h], cots[h], NN) - deltas[h])).astype(BF)
        put(2, h, mm(cots[h], w_s[h], NT)[:hd])
    for h, at in enumerate(each):
        put(0, h, back(q_all[at] * q_inv[h], q_inv[h], q_back, mm(k_s[h], grad_s[h], NN)[:hd]))
        put(1, h, back(k_all[at] * k_inv[h], k_inv[h], k_back, mm(q_s[h], grad_s[h], NT)[:hd]))
    size = gp_keep_ref.shape[0]
    gp_keep_ref[...] = rows_s[pl.ds(pl.multiple_of(core_ref[0] * size, ROWS), size), :].astype(BF)
    gp_send_ref[...] = rows_s[pl.ds(pl.multiple_of((1 - core_ref[0]) * size, ROWS), size), :].astype(BF)


def attend(core, x, affine, wt, qg, kg, patches, heads, hd):
    tokens = x.shape[0]
    width = wt.shape[1]
    hw = heads * hd
    smem = pl.BlockSpec(memory_space=pltpu.SMEM)
    vmem = pl.BlockSpec(memory_space=pltpu.VMEM)
    half = jax.ShapeDtypeStruct((3 * hw // 2, tokens), BF)
    tall = pltpu.VMEM((heads, LANES, tokens), BF)
    return pl.pallas_call(
        functools.partial(attend_kernel, patches=patches, heads=heads, hd=hd),
        in_specs=[smem, vmem, vmem, pl.BlockSpec(memory_space=pltpu.HBM), vmem, vmem],
        out_shape=(
            jax.ShapeDtypeStruct((tokens, width), BF),
            half,
            half,
            jax.ShapeDtypeStruct((hw, tokens), BF),
        ),
        scratch_shapes=[
            pltpu.VMEM((3 * hw, width), BF),
            pltpu.VMEM((3 * hw, tokens), F32),
            pltpu.VMEM((heads, tokens, tokens), F32),
            pltpu.VMEM((heads, tokens, tokens), BF),
            pltpu.VMEM((heads, tokens, tokens), BF),
            tall,
            tall,
            tall,
            pltpu.VMEM((hw, tokens), F32),
            pltpu.SemaphoreType.DMA((3,)),
        ],
        compiler_params=pltpu.CompilerParams(vmem_limit_bytes=50 * 2**20),
        name="attend",
    )(core, x, affine, wt, qg, kg)


def split_kernel(core_ref, which_ref, x_ref, affine_ref, wt_hbm, gp_keep_ref, gp_send_ref, att_ref,
                 send_ref, keep_ref, wt_s, gp_s, sems):
    tokens, _ = x_ref.shape
    width = affine_ref.shape[1]
    hw = att_ref.shape[0]
    parts = [pl.ds(part * hw, hw) for part in range(3)]
    copies = fetch([(wt_hbm.at[rows], wt_s.at[rows]) for rows in parts], sems)
    unit, inverse = unit_of(x_ref[:, :width].astype(F32))
    ident = eye(tokens)
    size = gp_keep_ref.shape[0]
    gp_s[pl.ds(pl.multiple_of(core_ref[0] * size, ROWS), size), :] = gp_keep_ref[...]
    gp_s[pl.ds(pl.multiple_of((1 - core_ref[0]) * size, ROWS), size), :] = gp_send_ref[...]
    grad = jnp.zeros((tokens, width), F32)
    for part in range(3):
        at = slice(part * hw, (part + 1) * hw)
        rows = mm(ident, gp_s[at, :], NT).astype(BF)
        copies[part].wait()
        grad = grad + mm(rows, wt_s[at, :], NN)
    half = width // 2
    win = send_ref.shape[1]
    mine_low = which_ref[0] == 0
    scaled = grad * affine_ref[1:2]
    first = jnp.sum(scaled, axis=1, keepdims=True)
    second = jnp.sum(scaled * unit, axis=1, keepdims=True)
    col = lax.broadcasted_iota(jnp.int32, (tokens, win), 1)
    here = jnp.where(mine_low, half, 0)
    there = jnp.where(mine_low, 0, half)
    low, high = scaled[:, :win], scaled[:, width - win :]
    send = jnp.where(mine_low, high, low)
    keep = jnp.where(mine_low, low, high)
    for place, term in enumerate((first, second)):
        coarse = term.astype(BF).astype(F32)
        send = jnp.where(col == there + 2 * place, coarse, send)
        send = jnp.where(col == there + 2 * place + 1, term - coarse, send)
    for place, term in enumerate((first, second, inverse)):
        keep = jnp.where(col == here + place, term, keep)
    send_ref[...] = send.astype(BF)
    keep_ref[:, :win] = keep
    keep_ref[:, win : 2 * win] = jnp.where(mine_low, unit[:, :win], unit[:, width - win :])
    keep_ref[:, 2 * win : 2 * win + hw] = mm(ident, att_ref[...], NT)


def split(core, which, x, affine, wt, gp_keep, gp_send, att):
    tokens = x.shape[0]
    hw = att.shape[0]
    win = window_of(wt.shape[1] // 2)
    smem = pl.BlockSpec(memory_space=pltpu.SMEM)
    vmem = pl.BlockSpec(memory_space=pltpu.VMEM)
    return pl.pallas_call(
        split_kernel,
        in_specs=[smem, smem, vmem, vmem, pl.BlockSpec(memory_space=pltpu.HBM), vmem, vmem, vmem],
        out_shape=(
            jax.ShapeDtypeStruct((tokens, win), BF),
            jax.ShapeDtypeStruct((tokens, 2 * win + window_of(hw)), F32),
        ),
        scratch_shapes=[
            pltpu.VMEM(wt.shape, BF),
            pltpu.VMEM((wt.shape[0], tokens), BF),
            pltpu.SemaphoreType.DMA((3,)),
        ],
        compiler_params=pltpu.CompilerParams(vmem_limit_bytes=40 * 2**20),
        name="split",
    )(core, which, x, affine, wt, gp_keep, gp_send, att)


def outer_kernel(where_ref, gp_a, gp_b, mod_a, mod_b, *refs):
    out_refs, tiles_s = refs[:-1], refs[-1]
    rows, width = gp_a.shape[0], mod_a.shape[1]
    tiles = rows // ROWS
    used = tiles * (width // LANES)
    tiles_s[used:] = jnp.zeros((tiles_s.shape[0] - used, ROWS, LANES), BF)
    gp = jnp.concatenate([gp_a[...], gp_b[...]], axis=1)
    for start in range(0, width, 2 * LANES):
        stop = min(start + 2 * LANES, width)
        mod = jnp.concatenate([mod_a[:, start:stop], mod_b[:, start:stop]], axis=0)
        found = mm(gp, mod, NN).astype(BF)
        for at in range(0, stop - start, LANES):
            j = (start + at) // LANES
            tiles_s[j * tiles : (j + 1) * tiles] = found[:, at : at + LANES].reshape(tiles, ROWS, LANES)
    size = tiles_s.shape[0] // 8
    for (lo, hi), order, send_ref, keep_ref in zip(bounds(size), ORDERS, out_refs[::2], out_refs[1::2]):
        for q in range(4):
            k = picked(q, order[1:])
            at = (where_ref[0] ^ k) * size + lo
            keep_ref[q] = tiles_s[pl.ds(at, hi - lo)]
            at = (where_ref[0] ^ (k ^ order[0])) * size + lo
            send_ref[q] = tiles_s[pl.ds(at, hi - lo)]


def outer(where, gp_a, gp_b, mod_a, mod_b, padded):
    smem = pl.BlockSpec(memory_space=pltpu.SMEM)
    vmem = pl.BlockSpec(memory_space=pltpu.VMEM)
    shapes = [jax.ShapeDtypeStruct((4, hi - lo, ROWS, LANES), BF) for lo, hi in bounds(padded // 8)]
    return pl.pallas_call(
        outer_kernel,
        in_specs=[smem] + [vmem] * 4,
        out_shape=tuple(shape for shape in shapes for _ in range(2)),
        scratch_shapes=[pltpu.VMEM((padded, ROWS, LANES), BF)],
        compiler_params=pltpu.CompilerParams(vmem_limit_bytes=16 * 2**20),
        name="outer",
    )(where, gp_a, gp_b, mod_a, mod_b)


ORDERS = ((1, 3, 4), (3, 4, 1), (4, 1, 3))


def bounds(size):
    cuts = [0, -(-size // 3), -(-2 * size // 3), size]
    return list(zip(cuts[:-1], cuts[1:]))


def picked(q, masks):
    return (masks[0] if q % 2 else 0) ^ (masks[1] if q // 2 else 0)


def window_of(half):
    return -(-half // LANES) * LANES


def finish_kernel(which_ref, recv_ref, keep_ref, out_ref, *, width):
    half = width // 2
    win = recv_ref.shape[1]
    mine_low = which_ref[0] == 0
    recv = recv_ref[...].astype(F32)
    keep = keep_ref[:, :win]
    unit = keep_ref[:, win : 2 * win]

    def column(block, place):
        return jnp.where(mine_low, block[:, half + place : half + place + 1], block[:, place : place + 1])

    first = column(keep, 0) + (column(recv, 0) + column(recv, 1))
    second = column(keep, 1) + (column(recv, 2) + column(recv, 3))
    inverse = column(keep, 2)
    grad = keep + recv
    out = inverse * (grad - first * (1.0 / width) - unit * (second * (1.0 / width)))
    moved = pltpu.roll(out, win - (win - half), 1)
    out_ref[:, :half] = jnp.where(mine_low, out, moved)[:, :half].astype(BF)
    out_ref[:, half:] = keep_ref[:, 2 * win : 2 * win + width - half].astype(BF)


def finish(which, recv, keep, width):
    tokens = recv.shape[0]
    smem = pl.BlockSpec(memory_space=pltpu.SMEM)
    vmem = pl.BlockSpec(memory_space=pltpu.VMEM)
    return pl.pallas_call(
        functools.partial(finish_kernel, width=width),
        in_specs=[smem, vmem, vmem],
        out_shape=jax.ShapeDtypeStruct((tokens, width), BF),
        compiler_params=pltpu.CompilerParams(vmem_limit_bytes=24 * 2**20),
        name="finish",
    )(which, recv, keep)


def fold_kernel(*refs):
    count = len(refs) // 4
    for i in range(count):
        keep_ref, got_ref = refs[2 * i : 2 * i + 2]
        send_ref, left_ref = refs[2 * count + 2 * i : 2 * count + 2 * i + 2]
        for q in range(keep_ref.shape[0]):
            total = (keep_ref[q].astype(F32) + got_ref[q].astype(F32)).astype(BF)
            if q % 2:
                send_ref[q // 2] = total
            else:
                left_ref[q // 2] = total


def fold(pairs):
    shapes = []
    for keep, _ in pairs:
        shapes += [jax.ShapeDtypeStruct((keep.shape[0] // 2,) + keep.shape[1:], BF)] * 2
    found = pl.pallas_call(
        fold_kernel,
        out_shape=tuple(shapes),
        compiler_params=pltpu.CompilerParams(vmem_limit_bytes=8 * 2**20),
        name="fold",
    )(*[x for pair in pairs for x in pair])
    return found[::2], found[1::2]


def close_kernel(*refs):
    out_ref, at = refs[-1], 0
    for keep_ref, got_ref in zip(refs[:-1:2], refs[1:-1:2]):
        count = keep_ref.shape[1]
        out_ref[at : at + count] = (keep_ref[0].astype(F32) + got_ref[0].astype(F32)).astype(BF)
        at += count


def close(pairs):
    count = sum(keep.shape[1] for keep, _ in pairs)
    return pl.pallas_call(
        close_kernel,
        out_shape=jax.ShapeDtypeStruct((count, ROWS, LANES), BF),
        compiler_params=pltpu.CompilerParams(vmem_limit_bytes=8 * 2**20),
        name="close",
    )(*[x for pair in pairs for x in pair])


def join_kernel(*refs):
    count = len(refs) // 3
    for i in range(count):
        have_ref, got_ref, out_ref = refs[2 * i], refs[2 * i + 1], refs[2 * count + i]
        size = have_ref.shape[0]
        out_ref[:size] = have_ref[...]
        out_ref[size:] = got_ref[...]


def join(pairs):
    shapes = [jax.ShapeDtypeStruct((2 * have.shape[0],) + have.shape[1:], BF) for have, _ in pairs]
    return pl.pallas_call(
        join_kernel,
        out_shape=tuple(shapes),
        compiler_params=pltpu.CompilerParams(vmem_limit_bytes=8 * 2**20),
        name="join",
    )(*[x for pair in pairs for x in pair])


def reduce_kernel(parts_ref, out_ref, *, factor):
    out_ref[...] = (jnp.sum(parts_ref[...].astype(F32), axis=0) * factor).astype(BF)


def reduce(parts, factor):
    return pl.pallas_call(
        functools.partial(reduce_kernel, factor=factor),
        out_shape=jax.ShapeDtypeStruct(parts.shape[1:], BF),
        compiler_params=pltpu.CompilerParams(vmem_limit_bytes=4 * 2**20),
        name="reduce",
    )(parts)


def place_kernel(clip_ref, *refs):
    clips = len(refs) - 4
    pieces, out_refs, all_s = refs[:clips], refs[clips:-1], refs[-1]
    size = pieces[0].shape[0]
    for shift, piece in enumerate(pieces):
        all_s[pl.ds(lax.rem(clip_ref[0] + shift, clips) * size, size)] = piece[...]
    for (lo, hi), out_ref in zip(bounds(clips * size), out_refs):
        out_ref[0] = all_s[lo:hi]


def place(clip, pieces):
    total = len(pieces) * pieces[0].shape[0]
    smem = pl.BlockSpec(memory_space=pltpu.SMEM)
    vmem = pl.BlockSpec(memory_space=pltpu.VMEM)
    return pl.pallas_call(
        place_kernel,
        in_specs=[smem] + [vmem] * len(pieces),
        out_shape=tuple(jax.ShapeDtypeStruct((1, hi - lo, ROWS, LANES), BF) for lo, hi in bounds(total)),
        scratch_shapes=[pltpu.VMEM((total, ROWS, LANES), BF)],
        compiler_params=pltpu.CompilerParams(vmem_limit_bytes=4 * 2**20),
        name="place",
    )(clip, *pieces)


def untile_kernel(where_ref, half_ref, *refs):
    pieces, (out_ref, tiles_s) = refs[:-2], refs[-2:]
    size = tiles_s.shape[0] // 16
    pieces = iter(pieces)
    for side in range(2):
        half = half_ref[0] ^ side
        for far in range(2):
            for (lo, hi), order in zip(bounds(size), ORDERS):
                piece = next(pieces)
                for q in range(4):
                    k = picked(q, (order[2], order[1])) ^ (order[0] * far)
                    at = (half * 8 + (where_ref[0] ^ k)) * size + lo
                    tiles_s[pl.ds(at, hi - lo)] = piece[q]
    rows = out_ref.shape[0] // 2
    tiles = rows // ROWS
    for half in range(2):
        for j in range(out_ref.shape[1] // LANES):
            start = half * 8 * size + j * tiles
            block = tiles_s[start : start + tiles].reshape(rows, LANES)
            out_ref[half * rows : (half + 1) * rows, j * LANES : (j + 1) * LANES] = block


def untile(where, half, pieces, rows, width):
    smem = pl.BlockSpec(memory_space=pltpu.SMEM)
    vmem = pl.BlockSpec(memory_space=pltpu.VMEM)
    tiles = sum(4 * piece.shape[1] for piece in pieces)
    return pl.pallas_call(
        untile_kernel,
        in_specs=[smem, smem] + [vmem] * len(pieces),
        out_shape=jax.ShapeDtypeStruct((rows, width), BF),
        scratch_shapes=[pltpu.VMEM((tiles, ROWS, LANES), BF)],
        compiler_params=pltpu.CompilerParams(vmem_limit_bytes=16 * 2**20),
        name="untile",
    )(where, half, *pieces)


def swap(x, axes, k):
    count = math.prod(lax.axis_size(a) for a in axes)
    return lax.ppermute(x, axes, [(i, i ^ k) for i in range(count)])


def exchange(x, axis):
    parts = x.reshape((-1,) + x.shape[-3:])
    return lax.all_to_all(parts, axis, split_axis=0, concat_axis=0, tiled=True)


def meet(blocks, level):
    return [swap(block, PLANE, order[level]) for block, order in zip(blocks, ORDERS)]


def sum_plane(found, beside):
    send, keep = found[::2], found[1::2]
    got, beside = lax.optimization_barrier((meet(send, 0), beside))
    send, keep = fold(list(zip(keep, got)))
    send, keep = fold(list(zip(keep, meet(send, 1))))
    return close(list(zip(keep, meet(send, 2)))), beside


def ring(own, axis, home):
    count = lax.axis_size(axis)
    pieces = [own] * count
    up = down = own
    for step in range(1, count // 2 + 1):
        if step == 2:
            up, down, home = lax.optimization_barrier((up, down, home))
        up = lax.ppermute(up, axis, [(i, (i + 1) % count) for i in range(count)])
        pieces[count - step] = up
        if step < count - step:
            down = lax.ppermute(down, axis, [(i, (i - 1) % count) for i in range(count)])
            pieces[step] = down
    return pieces, home


def gather_plane(have, where, half, rows, width):
    have = join(list(zip(have, meet(have, 2))))
    have = join(list(zip(have, meet(have, 1))))
    pieces = list(have) + meet(have, 0)
    pieces = pieces + [swap(piece, ("core",), 1) for piece in pieces]
    return untile(where, half, pieces, rows, width)


def body(latent, mod_shift, mod_scale, w_qkv, q_gain, k_gain, cotangent):
    _, _, patches, width = latent.shape
    hw = w_qkv.shape[2]
    hd = q_gain.shape[0]
    heads = hw // hd
    frames = 1
    for a in SEQ:
        frames *= lax.axis_size(a)
    own_patches = patches // frames
    clips = lax.axis_size("dp")
    wt = w_qkv.transpose(1, 2, 0).reshape(3 * hw, width)
    x = pack(latent[0, 0], cotangent[0, 0].T).reshape(frames, own_patches, width + hw)
    x = lax.all_to_all(x, SEQ, split_axis=0, concat_axis=0, tiled=True).reshape(patches, width + hw)
    affine = jnp.concatenate([mod_shift, 1.0 + mod_scale])
    core = lax.axis_index("core").astype(jnp.int32).reshape(1)
    which = lax.axis_index("tensor").astype(jnp.int32).reshape(1)
    where = lax.axis_index(PLANE).astype(jnp.int32).reshape(1)
    mod, gp_keep, gp_send, att_t = attend(
        core, x, affine, wt, q_gain[:, None], k_gain[:, None], own_patches, heads, hd
    )
    used = (3 * hw // 2 // ROWS) * (width // LANES)
    group = 8 * clips
    padded = -(-used // group) * group
    gp_other, mod_other = swap(gp_send, ("core",), 1), swap(mod, ("core",), 1)
    found = outer(where, gp_keep, gp_other, mod, mod_other, padded)
    send, keep = split(core, which, x, affine, wt, gp_keep, gp_send, att_t)
    own, send = sum_plane(found, send)
    recv = lax.ppermute(send, "tensor", [(0, 1), (1, 0)])
    home = finish(which, recv, keep, width).reshape(frames, own_patches, width)
    own, home = lax.optimization_barrier((own, home))
    own = exchange(own.reshape((clips, own.shape[0] // clips) + own.shape[1:]), "dp")
    own = reduce(own, 1.0 / math.sqrt(clips * frames * patches))
    pieces, home = ring(own, "dp", home)
    home = lax.all_to_all(home, SEQ, split_axis=0, concat_axis=0, tiled=True)
    pieces, home = lax.optimization_barrier((pieces, home))
    grad_t, att_t = unpack(home.reshape(patches, width))
    have = place(lax.axis_index("dp").astype(jnp.int32).reshape(1), pieces)
    grad_qkv = gather_plane(have, where, core, 3 * hw, width)
    grad_qkv = grad_qkv.reshape(3, hw, width).transpose(2, 0, 1)
    return (att_t.T[None, None], grad_t.T[None, None], grad_qkv)


def solution(mesh):
    fine = Mesh(mesh.devices.reshape(mesh.shape["dp"], 2, 4, 2, 2), ("dp",) + SEQ + ("tensor",))
    in_specs = (
        P("dp", SEQ, None, None),
        P("dp", None),
        P("dp", None),
        P(None, None, "tensor"),
        P(),
        P(),
        P("dp", SEQ, None, "tensor"),
    )
    out_specs = (
        P("dp", SEQ, None, "tensor"),
        P("dp", SEQ, None, "tensor"),
        P(None, None, "tensor"),
    )
    return jax.shard_map(body, mesh=fine, in_specs=in_specs, out_specs=out_specs, check_vma=False)
```

```python
import functools
import math

import jax
import jax.numpy as jnp
from jax import lax
from jax.experimental import pallas as pl
from jax.experimental.pallas import tpu as pltpu
from jax.sharding import Mesh, PartitionSpec as P

BF = jnp.bfloat16
F32 = jnp.float32
EPS = 1e-06
NN = (((1,), (0,)), ((), ()))
NT = (((1,), (1,)), ((), ()))
LOG2E = math.log2(math.e)
ROWS, LANES = 16, 128
PLANE = ("xlo", "y")
SEQ = PLANE + ("core",)


def mm(a, b, dims):
    return lax.dot_general(a, b, dims, preferred_element_type=F32)


def eye(n):
    rows = lax.broadcasted_iota(jnp.int32, (n, n), 0)
    cols = lax.broadcasted_iota(jnp.int32, (n, n), 1)
    return jnp.where(rows == cols, 1.0, 0.0).astype(BF)


def fetch(pairs, sems):
    copies = [pltpu.make_async_copy(src, dst, sems.at[i]) for i, (src, dst) in enumerate(pairs)]
    for copy in copies:
        copy.start()
    return copies


def pack_kernel(latent_hbm, cot_hbm, out_ref, latent_s, cot_s, sems):
    width = latent_s.shape[1]
    first, second = fetch([(cot_hbm, cot_s), (latent_hbm, latent_s)], sems)
    ident = eye(latent_s.shape[0])
    first.wait()
    out_ref[:, width:] = mm(ident, cot_s[...], NT).astype(BF)
    second.wait()
    out_ref[:, :width] = latent_s[...]


def pack(latent, cot_t):
    tokens, width = latent.shape
    hbm = pl.BlockSpec(memory_space=pltpu.HBM)
    return pl.pallas_call(
        pack_kernel,
        in_specs=[hbm, hbm],
        out_shape=jax.ShapeDtypeStruct((tokens, width + cot_t.shape[0]), BF),
        scratch_shapes=[
            pltpu.VMEM(latent.shape, BF),
            pltpu.VMEM(cot_t.shape, BF),
            pltpu.SemaphoreType.DMA((2,)),
        ],
        compiler_params=pltpu.CompilerParams(vmem_limit_bytes=60 * 2**20),
        name="pack",
    )(latent, cot_t)


def unpack_kernel(rows_ref, first_ref, second_ref):
    ident = eye(LANES)
    half = first_ref.shape[0]
    for start in range(0, 2 * half, LANES):
        found = mm(ident, rows_ref[:, start : start + LANES], NT).astype(BF)
        cut = min(max(half - start, 0), LANES)
        if cut:
            first_ref[start : start + cut] = found[:cut]
        if cut < LANES:
            second_ref[start + cut - half : start + LANES - half] = found[cut:]


def unpack(rows):
    tokens, width = rows.shape
    shape = jax.ShapeDtypeStruct((width // 2, tokens), BF)
    return pl.pallas_call(
        unpack_kernel,
        out_shape=(shape, shape),
        compiler_params=pltpu.CompilerParams(vmem_limit_bytes=8 * 2**20),
        name="unpack",
    )(rows)


def unit_of(values):
    width = values.shape[1]
    centred = values - jnp.sum(values, axis=1, keepdims=True) * (1.0 / width)
    inverse = lax.rsqrt(jnp.sum(centred * centred, axis=1, keepdims=True) * (1.0 / width) + EPS)
    return centred * inverse, inverse


def attend_kernel(core_ref, x_ref, affine_ref, wt_hbm, qg_ref, kg_ref,
                  mod_ref, gp_keep_ref, gp_send_ref, att_ref,
                  wt_s, rows_s, weights_s, w_s, grad_s, q_s, k_s, v_s, cot_s, sems, *, patches, heads, hd):
    tokens, _ = x_ref.shape
    width = affine_ref.shape[1]
    hw = heads * hd
    parts = [pl.ds(part * hw, hw) for part in range(3)]
    copies = fetch([(wt_hbm.at[rows], wt_s.at[rows]) for rows in parts], sems)
    unit, _ = unit_of(x_ref[:, :width].astype(F32))
    mod_ref[...] = (unit * affine_ref[1:2] + affine_ref[0:1]).astype(BF)
    mod = mod_ref[...]
    ident = eye(tokens)
    for start in range(0, hw, tokens):
        size = min(tokens, hw - start)
        block = x_ref[:, width + start : width + start + size]
        cot_s[start : start + size, :] = mm(ident[:size, :size], block, NT)

    def project(part):
        copies[part].wait()
        return mm(wt_s[part * hw : (part + 1) * hw, :], mod, NT).astype(BF).astype(F32)

    def norm(rows):
        inv = lax.rsqrt(jnp.sum(rows * rows, axis=0, keepdims=True) * (1.0 / hd) + EPS)
        return rows * inv, inv

    def back(hat, inv, gain, grad):
        weighted = grad * gain
        mean = jnp.sum(hat * weighted, axis=0, keepdims=True) * (1.0 / hd)
        return inv * (weighted - hat * mean)

    def put(part, h, rows):
        start = part * hw + h * hd
        rows_s[start : start + hd, :] = rows

    root = 1.0 / math.sqrt(hd)
    q_gain = qg_ref[...] * (root * LOG2E)
    k_gain = kg_ref[...]
    q_back = qg_ref[...] * root
    k_back = kg_ref[...] * (1.0 / LOG2E)
    each = [slice(h * hd, (h + 1) * hd) for h in range(heads)]

    spot = lax.broadcasted_iota(jnp.int32, (patches, tokens), 0)
    token = lax.broadcasted_iota(jnp.int32, (patches, tokens), 1)
    spots = jnp.where(lax.rem(token, patches) == spot, 16.0, 0.0)
    top = lax.broadcasted_iota(jnp.int32, (8, tokens), 0) == 0
    zeros = jnp.zeros((-(hd + patches + 8) % LANES, tokens), F32)
    q_tail = [spots, jnp.where(top, 16.0, 0.0), zeros]
    k_tail = [spots, jnp.where(top, -16.0, 0.0), zeros]
    v_tail = [jnp.where(top, 1.0, 0.0), jnp.zeros((-(hd + 8) % LANES, tokens), F32)]
    blank = jnp.zeros((-hd % LANES, tokens), F32)

    def rows_of(ref):
        found = []
        for h in range(0, heads, 2):
            both = mm(ident, ref[h : h + 2].reshape(2 * LANES, tokens), NT).astype(BF)
            found += [both[:, :LANES], both[:, LANES:]]
        return found

    q_all = project(0)
    q_inv = []
    for h, at in enumerate(each):
        hat, inv = norm(q_all[at])
        q_inv.append(inv)
        q_s[h] = jnp.concatenate([hat * q_gain] + q_tail).astype(BF)
    k_all = project(1)
    k_inv = []
    for h, at in enumerate(each):
        hat, inv = norm(k_all[at])
        k_inv.append(inv)
        k_s[h] = jnp.concatenate([hat * k_gain] + k_tail).astype(BF)
    v_all = project(2)
    for h, at in enumerate(each):
        v_s[h] = jnp.concatenate([v_all[at]] + v_tail).astype(BF)
    k_rows = rows_of(k_s)
    for h in range(heads):
        weights = jnp.exp2(mm(k_rows[h], q_s[h], NN))
        weights_s[h] = weights
        w_s[h] = weights.astype(BF)
    v_rows = rows_of(v_s)
    deltas, cots = [], []
    for h, at in enumerate(each):
        summed = mm(v_s[h], w_s[h], NN)
        share = 1.0 / summed[hd : hd + 1]
        out = summed[:hd] * share
        att_ref[at, :] = out.astype(BF)
        cot_share = cot_s[at, :] * share
        cots.append(jnp.concatenate([cot_share, blank]).astype(BF))
        deltas.append(jnp.sum(out * cot_share, axis=0, keepdims=True))
    for h in range(heads):
        grad_s[h] = (weights_s[h] * (mm(v_rows[h], cots[h], NN) - deltas[h])).astype(BF)
        put(2, h, mm(cots[h], w_s[h], NT)[:hd])
    for h, at in enumerate(each):
        put(0, h, back(q_all[at] * q_inv[h], q_inv[h], q_back, mm(k_s[h], grad_s[h], NN)[:hd]))
        put(1, h, back(k_all[at] * k_inv[h], k_inv[h], k_back, mm(q_s[h], grad_s[h], NT)[:hd]))
    size = gp_keep_ref.shape[0]
    gp_keep_ref[...] = rows_s[pl.ds(pl.multiple_of(core_ref[0] * size, ROWS), size), :].astype(BF)
    gp_send_ref[...] = rows_s[pl.ds(pl.multiple_of((1 - core_ref[0]) * size, ROWS), size), :].astype(BF)


def attend(core, x, affine, wt, qg, kg, patches, heads, hd):
    tokens = x.shape[0]
    width = wt.shape[1]
    hw = heads * hd
    smem = pl.BlockSpec(memory_space=pltpu.SMEM)
    vmem = pl.BlockSpec(memory_space=pltpu.VMEM)
    half = jax.ShapeDtypeStruct((3 * hw // 2, tokens), BF)
    tall = pltpu.VMEM((heads, LANES, tokens), BF)
    return pl.pallas_call(
        functools.partial(attend_kernel, patches=patches, heads=heads, hd=hd),
        in_specs=[smem, vmem, vmem, pl.BlockSpec(memory_space=pltpu.HBM), vmem, vmem],
        out_shape=(
            jax.ShapeDtypeStruct((tokens, width), BF),
            half,
            half,
            jax.ShapeDtypeStruct((hw, tokens), BF),
        ),
        scratch_shapes=[
            pltpu.VMEM((3 * hw, width), BF),
            pltpu.VMEM((3 * hw, tokens), F32),
            pltpu.VMEM((heads, tokens, tokens), F32),
            pltpu.VMEM((heads, tokens, tokens), BF),
            pltpu.VMEM((heads, tokens, tokens), BF),
            tall,
            tall,
            tall,
            pltpu.VMEM((hw, tokens), F32),
            pltpu.SemaphoreType.DMA((3,)),
        ],
        compiler_params=pltpu.CompilerParams(vmem_limit_bytes=52 * 2**20),
        name="attend",
    )(core, x, affine, wt, qg, kg)


def split_kernel(core_ref, which_ref, x_hbm, affine_hbm, wt_hbm, gp_keep_hbm, gp_send_hbm, att_hbm,
                 send_ref, keep_ref, x_ref, affine_ref, wt_s, gp_keep_ref, gp_send_ref, att_ref, gp_s, sems):
    tokens, _ = x_ref.shape
    width = affine_ref.shape[1]
    hw = att_ref.shape[0]
    parts = [pl.ds(part * hw, hw) for part in range(3)]
    copies = fetch(
        [(x_hbm, x_ref), (gp_keep_hbm, gp_keep_ref), (gp_send_hbm, gp_send_ref)]
        + [(wt_hbm.at[rows], wt_s.at[rows]) for rows in parts]
        + [(affine_hbm, affine_ref), (att_hbm, att_ref)],
        sems,
    )
    for copy in copies[:3]:
        copy.wait()
    unit, inverse = unit_of(x_ref[:, :width].astype(F32))
    ident = eye(tokens)
    size = gp_keep_ref.shape[0]
    gp_s[pl.ds(pl.multiple_of(core_ref[0] * size, ROWS), size), :] = gp_keep_ref[...]
    gp_s[pl.ds(pl.multiple_of((1 - core_ref[0]) * size, ROWS), size), :] = gp_send_ref[...]
    grad = jnp.zeros((tokens, width), F32)
    for part in range(3):
        at = slice(part * hw, (part + 1) * hw)
        rows = mm(ident, gp_s[at, :], NT).astype(BF)
        copies[3 + part].wait()
        grad = grad + mm(rows, wt_s[at, :], NN)
    half = width // 2
    win = send_ref.shape[1]
    mine_low = which_ref[0] == 0
    for copy in copies[6:]:
        copy.wait()
    scaled = grad * affine_ref[1:2]
    first = jnp.sum(scaled, axis=1, keepdims=True)
    second = jnp.sum(scaled * unit, axis=1, keepdims=True)
    col = lax.broadcasted_iota(jnp.int32, (tokens, win), 1)
    here = jnp.where(mine_low, half, 0)
    there = jnp.where(mine_low, 0, half)
    low, high = scaled[:, :win], scaled[:, width - win :]
    send = jnp.where(mine_low, high, low)
    keep = jnp.where(mine_low, low, high)
    for place, term in enumerate((first, second)):
        coarse = term.astype(BF).astype(F32)
        send = jnp.where(col == there + 2 * place, coarse, send)
        send = jnp.where(col == there + 2 * place + 1, term - coarse, send)
    for place, term in enumerate((first, second, inverse)):
        keep = jnp.where(col == here + place, term, keep)
    send_ref[...] = send.astype(BF)
    keep_ref[:, :win] = keep
    keep_ref[:, win : 2 * win] = jnp.where(mine_low, unit[:, :win], unit[:, width - win :])
    keep_ref[:, 2 * win : 2 * win + hw] = mm(ident, att_ref[...], NT)


def split(core, which, x, affine, wt, gp_keep, gp_send, att):
    tokens = x.shape[0]
    hw = att.shape[0]
    win = window_of(wt.shape[1] // 2)
    smem = pl.BlockSpec(memory_space=pltpu.SMEM)
    vmem = pl.BlockSpec(memory_space=pltpu.VMEM)
    return pl.pallas_call(
        split_kernel,
        in_specs=[smem, smem] + [pl.BlockSpec(memory_space=pltpu.HBM)] * 6,
        out_shape=(
            jax.ShapeDtypeStruct((tokens, win), BF),
            jax.ShapeDtypeStruct((tokens, 2 * win + window_of(hw)), F32),
        ),
        scratch_shapes=[pltpu.VMEM(a.shape, a.dtype) for a in (x, affine, wt, gp_keep, gp_send, att)]
        + [pltpu.VMEM((wt.shape[0], tokens), BF), pltpu.SemaphoreType.DMA((8,))],
        compiler_params=pltpu.CompilerParams(vmem_limit_bytes=58 * 2**20),
        name="split",
    )(core, which, x, affine, wt, gp_keep, gp_send, att)


def outer_kernel(where_ref, core_ref, gp_a, gp_b, mod_a, mod_b, *refs):
    out_refs, tiles_s = refs[:-1], refs[-1]
    rows, width = gp_a.shape[0], mod_a.shape[1]
    tiles = rows // ROWS
    used = tiles * (width // LANES)
    tiles_s[used:] = jnp.zeros((tiles_s.shape[0] - used, ROWS, LANES), BF)
    gp = jnp.concatenate([gp_a[...], gp_b[...]], axis=1)
    for start in range(0, width, 2 * LANES):
        stop = min(start + 2 * LANES, width)
        mod = jnp.concatenate([mod_a[:, start:stop], mod_b[:, start:stop]], axis=0)
        found = mm(gp, mod, NN).astype(BF)
        for at in range(0, stop - start, LANES):
            j = (start + at) // LANES
            tiles_s[j * tiles : (j + 1) * tiles] = found[:, at : at + LANES].reshape(tiles, ROWS, LANES)
    size = tiles_s.shape[0] // 8
    keep_ref = out_refs[-1]
    for (lo, hi), orders, send_ref in zip(bounds(size), ORDERS, out_refs):
        order = masks_of(orders, core_ref[0])
        for q in range(4):
            k = picked(q, order[1], order[2])
            at = (where_ref[0] ^ k) * size + lo
            keep_ref[q, lo:hi] = tiles_s[pl.ds(at, hi - lo)]
            at = (where_ref[0] ^ (k ^ order[0])) * size + lo
            send_ref[q] = tiles_s[pl.ds(at, hi - lo)]


def outer(where, core, gp_a, gp_b, mod_a, mod_b, padded):
    smem = pl.BlockSpec(memory_space=pltpu.SMEM)
    vmem = pl.BlockSpec(memory_space=pltpu.VMEM)
    size = padded // 8
    shapes = [jax.ShapeDtypeStruct((4, n, ROWS, LANES), BF) for n in [hi - lo for lo, hi in bounds(size)] + [size]]
    return pl.pallas_call(
        outer_kernel,
        in_specs=[smem, smem] + [vmem] * 4,
        out_shape=tuple(shapes),
        scratch_shapes=[pltpu.VMEM((padded, ROWS, LANES), BF)],
        compiler_params=pltpu.CompilerParams(vmem_limit_bytes=16 * 2**20),
        name="outer",
    )(where, core, gp_a, gp_b, mod_a, mod_b)


ORDERS = (((1, 3, 4), (4, 1, 3)), ((3, 4, 1), (3, 4, 1)))


def bounds(size):
    cut = -(-2 * size // 3)
    return [(0, cut), (cut, size)]


def masks_of(orders, core):
    return [jnp.where(core == 0, a, b) for a, b in zip(*orders)]


def picked(q, first, second):
    return (first if q % 2 else 0) ^ (second if q // 2 else 0)


def window_of(half):
    return -(-half // LANES) * LANES


def finish_kernel(which_ref, recv_ref, keep_ref, out_ref, *, width):
    half = width // 2
    win = recv_ref.shape[1]
    mine_low = which_ref[0] == 0
    recv = recv_ref[...].astype(F32)
    keep = keep_ref[:, :win]
    unit = keep_ref[:, win : 2 * win]

    def column(block, place):
        return jnp.where(mine_low, block[:, half + place : half + place + 1], block[:, place : place + 1])

    first = column(keep, 0) + (column(recv, 0) + column(recv, 1))
    second = column(keep, 1) + (column(recv, 2) + column(recv, 3))
    inverse = column(keep, 2)
    grad = keep + recv
    out = inverse * (grad - first * (1.0 / width) - unit * (second * (1.0 / width)))
    moved = pltpu.roll(out, win - (win - half), 1)
    out_ref[:, :half] = jnp.where(mine_low, out, moved)[:, :half].astype(BF)
    out_ref[:, half:] = keep_ref[:, 2 * win : 2 * win + width - half].astype(BF)


def finish(which, recv, keep, width):
    tokens = recv.shape[0]
    smem = pl.BlockSpec(memory_space=pltpu.SMEM)
    vmem = pl.BlockSpec(memory_space=pltpu.VMEM)
    return pl.pallas_call(
        functools.partial(finish_kernel, width=width),
        in_specs=[smem, vmem, vmem],
        out_shape=jax.ShapeDtypeStruct((tokens, width), BF),
        compiler_params=pltpu.CompilerParams(vmem_limit_bytes=24 * 2**20),
        name="finish",
    )(which, recv, keep)


def fold_kernel(keep_ref, *refs):
    count = (len(refs) - 1) // 2
    got_refs, send_refs, left_ref = refs[:count], refs[count:-1], refs[-1]
    for (lo, hi), got_ref, send_ref in zip(bounds(keep_ref.shape[1]), got_refs, send_refs):
        for q in range(keep_ref.shape[0]):
            total = (keep_ref[q, lo:hi].astype(F32) + got_ref[q].astype(F32)).astype(BF)
            if q % 2:
                send_ref[q // 2] = total
            else:
                left_ref[q // 2, lo:hi] = total


def fold(keep, got):
    shapes = [jax.ShapeDtypeStruct((x.shape[0] // 2,) + x.shape[1:], BF) for x in (*got, keep)]
    found = pl.pallas_call(
        fold_kernel,
        out_shape=tuple(shapes),
        compiler_params=pltpu.CompilerParams(vmem_limit_bytes=8 * 2**20),
        name="fold",
    )(keep, *got)
    return found[:-1], found[-1]


def close_kernel(keep_ref, *refs):
    out_ref = refs[-1]
    for (lo, hi), got_ref in zip(bounds(keep_ref.shape[1]), refs):
        out_ref[lo:hi] = (keep_ref[0, lo:hi].astype(F32) + got_ref[0].astype(F32)).astype(BF)
    spare = out_ref.shape[0] - keep_ref.shape[1]
    if spare:
        out_ref[keep_ref.shape[1] :] = jnp.zeros((spare, ROWS, LANES), BF)


def close(keep, got, size):
    return pl.pallas_call(
        close_kernel,
        out_shape=jax.ShapeDtypeStruct((size, ROWS, LANES), BF),
        compiler_params=pltpu.CompilerParams(vmem_limit_bytes=8 * 2**20),
        name="close",
    )(keep, *got)


def join_kernel(*refs):
    count = len(refs) // 3
    for i in range(count):
        have_ref, got_ref, out_ref = refs[2 * i], refs[2 * i + 1], refs[2 * count + i]
        size = have_ref.shape[0]
        out_ref[:size] = have_ref[...]
        out_ref[size:] = got_ref[...]


def join(pairs):
    shapes = [jax.ShapeDtypeStruct((2 * have.shape[0],) + have.shape[1:], BF) for have, _ in pairs]
    return pl.pallas_call(
        join_kernel,
        out_shape=tuple(shapes),
        compiler_params=pltpu.CompilerParams(vmem_limit_bytes=8 * 2**20),
        name="join",
    )(*[x for pair in pairs for x in pair])


def reduce_kernel(parts_ref, out_ref, *, factor):
    out_ref[...] = (jnp.sum(parts_ref[...].astype(F32), axis=0) * factor).astype(BF)


def reduce(parts, factor):
    return pl.pallas_call(
        functools.partial(reduce_kernel, factor=factor),
        out_shape=jax.ShapeDtypeStruct(parts.shape[1:], BF),
        compiler_params=pltpu.CompilerParams(vmem_limit_bytes=4 * 2**20),
        name="reduce",
    )(parts)


def trio_kernel(own_ref, below_ref, above_ref, all_ref, two_ref):
    size = own_ref.shape[0]
    for i, ref in enumerate((below_ref, own_ref, above_ref)):
        all_ref[i * size : (i + 1) * size] = ref[...]
        if i < 2:
            two_ref[i * size : (i + 1) * size] = ref[...]


def trio(own, below, above):
    size = own.shape[0]
    return pl.pallas_call(
        trio_kernel,
        out_shape=tuple(jax.ShapeDtypeStruct((n * size,) + own.shape[1:], BF) for n in (3, 2)),
        compiler_params=pltpu.CompilerParams(vmem_limit_bytes=4 * 2**20),
        name="trio",
    )(own, below, above)


def place_kernel(clip_ref, near_ref, below_ref, above_ref, *refs, clips):
    out_refs, all_s = refs[:-1], refs[-1]
    size = all_s.shape[0] // clips
    for ref, first in ((near_ref, -1), (below_ref, -4), (above_ref, 2)):
        for i in range(ref.shape[0] // size):
            at = lax.rem(clip_ref[0] + (first + i + clips), clips) * size
            all_s[pl.ds(at, size)] = ref[i * size : (i + 1) * size]
    for (lo, hi), out_ref in zip(bounds(sum(ref.shape[1] for ref in out_refs)), out_refs):
        out_ref[0] = all_s[lo:hi]


def place(clip, near, below, above, clips, size):
    total = near.shape[0] // 3 * clips
    smem = pl.BlockSpec(memory_space=pltpu.SMEM)
    vmem = pl.BlockSpec(memory_space=pltpu.VMEM)
    return pl.pallas_call(
        functools.partial(place_kernel, clips=clips),
        in_specs=[smem, vmem, vmem, vmem],
        out_shape=tuple(jax.ShapeDtypeStruct((1, hi - lo, ROWS, LANES), BF) for lo, hi in bounds(size)),
        scratch_shapes=[pltpu.VMEM((total, ROWS, LANES), BF)],
        compiler_params=pltpu.CompilerParams(vmem_limit_bytes=4 * 2**20),
        name="place",
    )(clip, near, below, above)


def untile_kernel(where_ref, half_ref, *refs):
    pieces, (out_ref, tiles_s) = refs[:-2], refs[-2:]
    size = tiles_s.shape[0] // 16
    pieces = iter(pieces)
    for side in range(2):
        half = half_ref[0] ^ side
        for far in range(2):
            for (lo, hi), orders in zip(bounds(size), ORDERS):
                piece = next(pieces)
                order = masks_of(orders, half)
                for q in range(4):
                    k = picked(q, order[2], order[1]) ^ (order[0] * far)
                    at = (half * 8 + (where_ref[0] ^ k)) * size + lo
                    tiles_s[pl.ds(at, hi - lo)] = piece[q]
    rows = out_ref.shape[0] // 2
    tiles = rows // ROWS
    for half in range(2):
        for j in range(out_ref.shape[1] // LANES):
            start = half * 8 * size + j * tiles
            block = tiles_s[start : start + tiles].reshape(rows, LANES)
            out_ref[half * rows : (half + 1) * rows, j * LANES : (j + 1) * LANES] = block


def untile(where, half, pieces, rows, width):
    smem = pl.BlockSpec(memory_space=pltpu.SMEM)
    vmem = pl.BlockSpec(memory_space=pltpu.VMEM)
    tiles = sum(4 * piece.shape[1] for piece in pieces)
    return pl.pallas_call(
        untile_kernel,
        in_specs=[smem, smem] + [vmem] * len(pieces),
        out_shape=jax.ShapeDtypeStruct((rows, width), BF),
        scratch_shapes=[pltpu.VMEM((tiles, ROWS, LANES), BF)],
        compiler_params=pltpu.CompilerParams(vmem_limit_bytes=16 * 2**20),
        name="untile",
    )(where, half, *pieces)


def swap(x, axes, k):
    count = math.prod(lax.axis_size(a) for a in axes)
    return lax.ppermute(x, axes, [(i, i ^ k) for i in range(count)])


def exchange(x, axis):
    parts = x.reshape((-1,) + x.shape[-3:])
    return lax.all_to_all(parts, axis, split_axis=0, concat_axis=0, tiled=True)


def plane_size():
    return lax.axis_size("xlo") * lax.axis_size("y")


def meet(blocks, level):
    found = []
    for block, orders in zip(blocks, ORDERS):
        pairs = [(p * 2 + c, (p ^ orders[c][level]) * 2 + c) for p in range(plane_size()) for c in range(2)]
        found.append(lax.ppermute(block, SEQ, pairs))
    return found


def sum_plane(found, beside, size):
    send, keep = found[:-1], found[-1]
    got, beside = lax.optimization_barrier((meet(send, 0), beside))
    send, keep = fold(keep, got)
    send, keep = fold(keep, meet(send, 1))
    return close(keep, meet(send, 2), size), beside


def shift(x, axis, step):
    count = lax.axis_size(axis)
    return lax.ppermute(x, axis, [(i, (i + step) % count) for i in range(count)])


def gather_clips(own, home):
    below, above = shift(own, "dp", 1), shift(own, "dp", -1)
    near, two = trio(own, below, above)
    return near, shift(near, "dp", 3), shift(two, "dp", -3), home


def gather_plane(have, where, half, rows, width, beside):
    got, beside = lax.optimization_barrier((meet(have, 2), beside))
    have = join(list(zip(have, got)))
    have = join(list(zip(have, meet(have, 1))))
    pieces = list(have) + meet(have, 0)
    pieces = pieces + [swap(piece, ("core",), 1) for piece in pieces]
    return untile(where, half, pieces, rows, width), beside


def body(latent, mod_shift, mod_scale, w_qkv, q_gain, k_gain, cotangent):
    _, _, patches, width = latent.shape
    hw = w_qkv.shape[2]
    hd = q_gain.shape[0]
    heads = hw // hd
    frames = 1
    for a in SEQ:
        frames *= lax.axis_size(a)
    own_patches = patches // frames
    clips = lax.axis_size("dp")
    wt = w_qkv.transpose(1, 2, 0).reshape(3 * hw, width)
    x = pack(latent[0, 0], cotangent[0, 0].T).reshape(frames, own_patches, width + hw)
    x = lax.all_to_all(x, SEQ, split_axis=0, concat_axis=0, tiled=True).reshape(patches, width + hw)
    affine = jnp.concatenate([mod_shift, 1.0 + mod_scale])
    core = lax.axis_index("core").astype(jnp.int32).reshape(1)
    which = lax.axis_index("tensor").astype(jnp.int32).reshape(1)
    where = lax.axis_index(PLANE).astype(jnp.int32).reshape(1)
    mod, gp_keep, gp_send, att_t = attend(
        core, x, affine, wt, q_gain[:, None], k_gain[:, None], own_patches, heads, hd
    )
    used = (3 * hw // 2 // ROWS) * (width // LANES)
    size = -(-used // plane_size())
    gp_other, mod_other = swap(gp_send, ("core",), 1), swap(mod, ("core",), 1)
    found = outer(where, core, gp_keep, gp_other, mod, mod_other, size * plane_size())
    send, keep = split(core, which, x, affine, wt, gp_keep, gp_send, att_t)
    own, send = sum_plane(found, send, -(-size // clips) * clips)
    own, send = lax.optimization_barrier((own, send))
    recv = lax.ppermute(send, "tensor", [(0, 1), (1, 0)])
    own = exchange(own.reshape((clips, own.shape[0] // clips) + own.shape[1:]), "dp")
    own = reduce(own, 1.0 / math.sqrt(clips * frames * patches))
    own, recv = lax.optimization_barrier((own, recv))
    home = finish(which, recv, keep, width).reshape(frames, own_patches, width)
    near, below, above, home = gather_clips(own, home)
    home = lax.all_to_all(home, SEQ, split_axis=0, concat_axis=0, tiled=True)
    clip = lax.axis_index("dp").astype(jnp.int32).reshape(1)
    have = place(clip, near, below, above, clips, size)
    grad_qkv, home = gather_plane(have, where, core, 3 * hw, width, home)
    grad_t, att_t = unpack(home.reshape(patches, width))
    grad_qkv = grad_qkv.reshape(3, hw, width).transpose(2, 0, 1)
    return (att_t.T[None, None], grad_t.T[None, None], grad_qkv)


def solution(mesh):
    fine = Mesh(mesh.devices.reshape(mesh.shape["dp"], 2, 4, 2, 2), ("dp",) + SEQ + ("tensor",))
    in_specs = (
        P("dp", SEQ, None, None),
        P("dp", None),
        P("dp", None),
        P(None, None, "tensor"),
        P(),
        P(),
        P("dp", SEQ, None, "tensor"),
    )
    out_specs = (
        P("dp", SEQ, None, "tensor"),
        P("dp", SEQ, None, "tensor"),
        P(None, None, "tensor"),
    )
    return jax.shard_map(body, mesh=fine, in_specs=in_specs, out_specs=out_specs, check_vma=False)
```

```python
import functools
import math

import jax
import jax.numpy as jnp
from jax import lax
from jax.experimental import pallas as pl
from jax.experimental.pallas import tpu as pltpu
from jax.sharding import Mesh, PartitionSpec as P

BF = jnp.bfloat16
F32 = jnp.float32
EPS = 1e-06
NN = (((1,), (0,)), ((), ()))
NT = (((1,), (1,)), ((), ()))
LOG2E = math.log2(math.e)
ROWS, LANES = 16, 128
PLANE = ("xlo", "y")
SEQ = PLANE + ("core",)


def mm(a, b, dims):
    return lax.dot_general(a, b, dims, preferred_element_type=F32)


def eye(n):
    rows = lax.broadcasted_iota(jnp.int32, (n, n), 0)
    cols = lax.broadcasted_iota(jnp.int32, (n, n), 1)
    return jnp.where(rows == cols, 1.0, 0.0).astype(BF)


def fetch(pairs, sems):
    copies = [pltpu.make_async_copy(src, dst, sems.at[i]) for i, (src, dst) in enumerate(pairs)]
    for copy in copies:
        copy.start()
    return copies


def pack_kernel(latent_hbm, cot_hbm, out_ref, latent_s, cot_s, sems):
    width = latent_s.shape[1]
    first, second = fetch([(cot_hbm, cot_s), (latent_hbm, latent_s)], sems)
    ident = eye(latent_s.shape[0])
    first.wait()
    out_ref[:, width:] = mm(ident, cot_s[...], NT).astype(BF)
    second.wait()
    out_ref[:, :width] = latent_s[...]


def pack(latent, cot_t):
    tokens, width = latent.shape
    hbm = pl.BlockSpec(memory_space=pltpu.HBM)
    return pl.pallas_call(
        pack_kernel,
        in_specs=[hbm, hbm],
        out_shape=jax.ShapeDtypeStruct((tokens, width + cot_t.shape[0]), BF),
        scratch_shapes=[
            pltpu.VMEM(latent.shape, BF),
            pltpu.VMEM(cot_t.shape, BF),
            pltpu.SemaphoreType.DMA((2,)),
        ],
        compiler_params=pltpu.CompilerParams(vmem_limit_bytes=60 * 2**20),
        name="pack",
    )(latent, cot_t)


def unpack_kernel(rows_ref, first_ref, second_ref):
    ident = eye(LANES)
    half = first_ref.shape[0]
    for start in range(0, 2 * half, LANES):
        found = mm(ident, rows_ref[:, start : start + LANES], NT).astype(BF)
        cut = min(max(half - start, 0), LANES)
        if cut:
            first_ref[start : start + cut] = found[:cut]
        if cut < LANES:
            second_ref[start + cut - half : start + LANES - half] = found[cut:]


def unpack(rows):
    tokens, width = rows.shape
    shape = jax.ShapeDtypeStruct((width // 2, tokens), BF)
    return pl.pallas_call(
        unpack_kernel,
        out_shape=(shape, shape),
        compiler_params=pltpu.CompilerParams(vmem_limit_bytes=8 * 2**20),
        name="unpack",
    )(rows)


def unit_of(values):
    width = values.shape[1]
    centred = values - jnp.sum(values, axis=1, keepdims=True) * (1.0 / width)
    inverse = lax.rsqrt(jnp.sum(centred * centred, axis=1, keepdims=True) * (1.0 / width) + EPS)
    return centred * inverse, inverse


def attend_kernel(core_ref, x_ref, affine_ref, wt_hbm, qg_ref, kg_ref,
                  mod_ref, gp_keep_ref, gp_send_ref, att_ref,
                  wt_s, rows_s, weights_s, w_s, grad_s, q_s, k_s, v_s, cot_s, sems, *, patches, heads, hd):
    tokens, _ = x_ref.shape
    width = affine_ref.shape[1]
    hw = heads * hd
    parts = [pl.ds(part * hw, hw) for part in range(3)]
    copies = fetch([(wt_hbm.at[rows], wt_s.at[rows]) for rows in parts], sems)
    unit, _ = unit_of(x_ref[:, :width].astype(F32))
    mod_ref[...] = (unit * affine_ref[1:2] + affine_ref[0:1]).astype(BF)
    mod = mod_ref[...]
    ident = eye(tokens)
    for start in range(0, hw, tokens):
        size = min(tokens, hw - start)
        block = x_ref[:, width + start : width + start + size]
        cot_s[start : start + size, :] = mm(ident[:size, :size], block, NT)

    def project(part):
        copies[part].wait()
        return mm(wt_s[part * hw : (part + 1) * hw, :], mod, NT).astype(BF).astype(F32)

    def norm(rows):
        inv = lax.rsqrt(jnp.sum(rows * rows, axis=0, keepdims=True) * (1.0 / hd) + EPS)
        return rows * inv, inv

    def back(hat, inv, gain, grad):
        weighted = grad * gain
        mean = jnp.sum(hat * weighted, axis=0, keepdims=True) * (1.0 / hd)
        return inv * (weighted - hat * mean)

    def put(part, h, rows):
        start = part * hw + h * hd
        rows_s[start : start + hd, :] = rows

    root = 1.0 / math.sqrt(hd)
    q_gain = qg_ref[...] * (root * LOG2E)
    k_gain = kg_ref[...]
    q_back = qg_ref[...] * root
    k_back = kg_ref[...] * (1.0 / LOG2E)
    each = [slice(h * hd, (h + 1) * hd) for h in range(heads)]

    spot = lax.broadcasted_iota(jnp.int32, (patches, tokens), 0)
    token = lax.broadcasted_iota(jnp.int32, (patches, tokens), 1)
    spots = jnp.where(lax.rem(token, patches) == spot, 16.0, 0.0)
    top = lax.broadcasted_iota(jnp.int32, (8, tokens), 0) == 0
    zeros = jnp.zeros((-(hd + patches + 8) % LANES, tokens), F32)
    q_tail = [spots, jnp.where(top, 16.0, 0.0), zeros]
    k_tail = [spots, jnp.where(top, -16.0, 0.0), zeros]
    v_tail = [jnp.where(top, 1.0, 0.0), jnp.zeros((-(hd + 8) % LANES, tokens), F32)]
    blank = jnp.zeros((-hd % LANES, tokens), F32)

    def rows_of(ref):
        found = []
        for h in range(0, heads, 2):
            both = mm(ident, ref[h : h + 2].reshape(2 * LANES, tokens), NT).astype(BF)
            found += [both[:, :LANES], both[:, LANES:]]
        return found

    q_all = project(0)
    q_inv = []
    for h, at in enumerate(each):
        hat, inv = norm(q_all[at])
        q_inv.append(inv)
        q_s[h] = jnp.concatenate([hat * q_gain] + q_tail).astype(BF)
    k_all = project(1)
    k_inv = []
    for h, at in enumerate(each):
        hat, inv = norm(k_all[at])
        k_inv.append(inv)
        k_s[h] = jnp.concatenate([hat * k_gain] + k_tail).astype(BF)
    v_all = project(2)
    for h, at in enumerate(each):
        v_s[h] = jnp.concatenate([v_all[at]] + v_tail).astype(BF)
    k_rows = rows_of(k_s)
    for h in range(heads):
        weights = jnp.exp2(mm(k_rows[h], q_s[h], NN))
        weights_s[h] = weights
        w_s[h] = weights.astype(BF)
    v_rows = rows_of(v_s)
    deltas, cots = [], []
    for h, at in enumerate(each):
        summed = mm(v_s[h], w_s[h], NN)
        share = 1.0 / summed[hd : hd + 1]
        out = summed[:hd] * share
        att_ref[at, :] = out.astype(BF)
        cot_share = cot_s[at, :] * share
        cots.append(jnp.concatenate([cot_share, blank]).astype(BF))
        deltas.append(jnp.sum(out * cot_share, axis=0, keepdims=True))
    for h in range(heads):
        grad_s[h] = (weights_s[h] * (mm(v_rows[h], cots[h], NN) - deltas[h])).astype(BF)
        put(2, h, mm(cots[h], w_s[h], NT)[:hd])
    for h, at in enumerate(each):
        put(0, h, back(q_all[at] * q_inv[h], q_inv[h], q_back, mm(k_s[h], grad_s[h], NN)[:hd]))
        put(1, h, back(k_all[at] * k_inv[h], k_inv[h], k_back, mm(q_s[h], grad_s[h], NT)[:hd]))
    size = gp_keep_ref.shape[0]
    gp_keep_ref[...] = rows_s[pl.ds(pl.multiple_of(core_ref[0] * size, ROWS), size), :].astype(BF)
    gp_send_ref[...] = rows_s[pl.ds(pl.multiple_of((1 - core_ref[0]) * size, ROWS), size), :].astype(BF)


def attend(core, x, affine, wt, qg, kg, patches, heads, hd):
    tokens = x.shape[0]
    width = wt.shape[1]
    hw = heads * hd
    smem = pl.BlockSpec(memory_space=pltpu.SMEM)
    vmem = pl.BlockSpec(memory_space=pltpu.VMEM)
    half = jax.ShapeDtypeStruct((3 * hw // 2, tokens), BF)
    tall = pltpu.VMEM((heads, LANES, tokens), BF)
    return pl.pallas_call(
        functools.partial(attend_kernel, patches=patches, heads=heads, hd=hd),
        in_specs=[smem, vmem, vmem, pl.BlockSpec(memory_space=pltpu.HBM), vmem, vmem],
        out_shape=(
            jax.ShapeDtypeStruct((tokens, width), BF),
            half,
            half,
            jax.ShapeDtypeStruct((hw, tokens), BF),
        ),
        scratch_shapes=[
            pltpu.VMEM((3 * hw, width), BF),
            pltpu.VMEM((3 * hw, tokens), F32),
            pltpu.VMEM((heads, tokens, tokens), F32),
            pltpu.VMEM((heads, tokens, tokens), BF),
            pltpu.VMEM((heads, tokens, tokens), BF),
            tall,
            tall,
            tall,
            pltpu.VMEM((hw, tokens), F32),
            pltpu.SemaphoreType.DMA((3,)),
        ],
        compiler_params=pltpu.CompilerParams(vmem_limit_bytes=52 * 2**20),
        name="attend",
    )(core, x, affine, wt, qg, kg)


def split_kernel(core_ref, which_ref, x_hbm, affine_hbm, wt_hbm, gp_keep_hbm, gp_send_hbm, att_hbm,
                 send_ref, keep_ref, x_ref, affine_ref, wt_s, gp_keep_ref, gp_send_ref, att_ref, gp_s, sems):
    tokens, _ = x_ref.shape
    width = affine_ref.shape[1]
    hw = att_ref.shape[0]
    parts = [pl.ds(part * hw, hw) for part in range(3)]
    copies = fetch(
        [(x_hbm, x_ref), (gp_keep_hbm, gp_keep_ref), (gp_send_hbm, gp_send_ref)]
        + [(wt_hbm.at[rows], wt_s.at[rows]) for rows in parts]
        + [(affine_hbm, affine_ref), (att_hbm, att_ref)],
        sems,
    )
    for copy in copies[:3]:
        copy.wait()
    unit, inverse = unit_of(x_ref[:, :width].astype(F32))
    ident = eye(tokens)
    size = gp_keep_ref.shape[0]
    gp_s[pl.ds(pl.multiple_of(core_ref[0] * size, ROWS), size), :] = gp_keep_ref[...]
    gp_s[pl.ds(pl.multiple_of((1 - core_ref[0]) * size, ROWS), size), :] = gp_send_ref[...]
    grad = jnp.zeros((tokens, width), F32)
    for part in range(3):
        at = slice(part * hw, (part + 1) * hw)
        rows = mm(ident, gp_s[at, :], NT).astype(BF)
        copies[3 + part].wait()
        grad = grad + mm(rows, wt_s[at, :], NN)
    half = width // 2
    win = send_ref.shape[1]
    mine_low = which_ref[0] == 0
    for copy in copies[6:]:
        copy.wait()
    scaled = grad * affine_ref[1:2]
    first = jnp.sum(scaled, axis=1, keepdims=True)
    second = jnp.sum(scaled * unit, axis=1, keepdims=True)
    col = lax.broadcasted_iota(jnp.int32, (tokens, win), 1)
    here = jnp.where(mine_low, half, 0)
    there = jnp.where(mine_low, 0, half)
    low, high = scaled[:, :win], scaled[:, width - win :]
    send = jnp.where(mine_low, high, low)
    keep = jnp.where(mine_low, low, high)
    for place, term in enumerate((first, second)):
        coarse = term.astype(BF).astype(F32)
        send = jnp.where(col == there + 2 * place, coarse, send)
        send = jnp.where(col == there + 2 * place + 1, term - coarse, send)
    for place, term in enumerate((first, second, inverse)):
        keep = jnp.where(col == here + place, term, keep)
    send_ref[...] = send.astype(BF)
    keep_ref[:, :win] = keep
    keep_ref[:, win : 2 * win] = jnp.where(mine_low, unit[:, :win], unit[:, width - win :])
    keep_ref[:, 2 * win : 2 * win + hw] = mm(ident, att_ref[...], NT)


def split(core, which, x, affine, wt, gp_keep, gp_send, att):
    tokens = x.shape[0]
    hw = att.shape[0]
    win = window_of(wt.shape[1] // 2)
    smem = pl.BlockSpec(memory_space=pltpu.SMEM)
    vmem = pl.BlockSpec(memory_space=pltpu.VMEM)
    return pl.pallas_call(
        split_kernel,
        in_specs=[smem, smem] + [pl.BlockSpec(memory_space=pltpu.HBM)] * 6,
        out_shape=(
            jax.ShapeDtypeStruct((tokens, win), BF),
            jax.ShapeDtypeStruct((tokens, 2 * win + window_of(hw)), F32),
        ),
        scratch_shapes=[pltpu.VMEM(a.shape, a.dtype) for a in (x, affine, wt, gp_keep, gp_send, att)]
        + [pltpu.VMEM((wt.shape[0], tokens), BF), pltpu.SemaphoreType.DMA((8,))],
        compiler_params=pltpu.CompilerParams(vmem_limit_bytes=58 * 2**20),
        name="split",
    )(core, which, x, affine, wt, gp_keep, gp_send, att)


def outer_kernel(where_ref, core_ref, gp_a, gp_b, mod_a, mod_b, *refs):
    out_refs, tiles_s = refs[:-1], refs[-1]
    rows, width = gp_a.shape[0], mod_a.shape[1]
    tiles = rows // ROWS
    used = tiles * (width // LANES)
    tiles_s[used:] = jnp.zeros((tiles_s.shape[0] - used, ROWS, LANES), BF)
    gp = jnp.concatenate([gp_a[...], gp_b[...]], axis=1)
    for start in range(0, width, 2 * LANES):
        stop = min(start + 2 * LANES, width)
        mod = jnp.concatenate([mod_a[:, start:stop], mod_b[:, start:stop]], axis=0)
        found = mm(gp, mod, NN).astype(BF)
        for at in range(0, stop - start, LANES):
            j = (start + at) // LANES
            tiles_s[j * tiles : (j + 1) * tiles] = found[:, at : at + LANES].reshape(tiles, ROWS, LANES)
    size = tiles_s.shape[0] // 8
    keep_ref = out_refs[-1]
    for (lo, hi), orders, send_ref in zip(bounds(size), ORDERS, out_refs):
        order = masks_of(orders, core_ref[0])
        for q in range(4):
            k = picked(q, order[1], order[2])
            at = (where_ref[0] ^ k) * size + lo
            keep_ref[q, lo:hi] = tiles_s[pl.ds(at, hi - lo)]
            at = (where_ref[0] ^ (k ^ order[0])) * size + lo
            send_ref[q] = tiles_s[pl.ds(at, hi - lo)]


def outer(where, core, gp_a, gp_b, mod_a, mod_b, padded):
    smem = pl.BlockSpec(memory_space=pltpu.SMEM)
    vmem = pl.BlockSpec(memory_space=pltpu.VMEM)
    size = padded // 8
    shapes = [jax.ShapeDtypeStruct((4, n, ROWS, LANES), BF) for n in [hi - lo for lo, hi in bounds(size)] + [size]]
    return pl.pallas_call(
        outer_kernel,
        in_specs=[smem, smem] + [vmem] * 4,
        out_shape=tuple(shapes),
        scratch_shapes=[pltpu.VMEM((padded, ROWS, LANES), BF)],
        compiler_params=pltpu.CompilerParams(vmem_limit_bytes=16 * 2**20),
        name="outer",
    )(where, core, gp_a, gp_b, mod_a, mod_b)


ORDERS = (((1, 3, 4), (4, 1, 3)), ((3, 4, 1), (3, 4, 1)))


def bounds(size):
    cut = -(-2 * size // 3)
    return [(0, cut), (cut, size)]


def masks_of(orders, core):
    return [jnp.where(core == 0, a, b) for a, b in zip(*orders)]


def picked(q, first, second):
    return (first if q % 2 else 0) ^ (second if q // 2 else 0)


def window_of(half):
    return -(-half // LANES) * LANES


def finish_kernel(which_ref, recv_ref, keep_ref, out_ref, *, width):
    half = width // 2
    win = recv_ref.shape[1]
    mine_low = which_ref[0] == 0
    recv = recv_ref[...].astype(F32)
    keep = keep_ref[:, :win]
    unit = keep_ref[:, win : 2 * win]

    def column(block, place):
        return jnp.where(mine_low, block[:, half + place : half + place + 1], block[:, place : place + 1])

    first = column(keep, 0) + (column(recv, 0) + column(recv, 1))
    second = column(keep, 1) + (column(recv, 2) + column(recv, 3))
    inverse = column(keep, 2)
    grad = keep + recv
    out = inverse * (grad - first * (1.0 / width) - unit * (second * (1.0 / width)))
    moved = pltpu.roll(out, win - (win - half), 1)
    out_ref[:, :half] = jnp.where(mine_low, out, moved)[:, :half].astype(BF)
    out_ref[:, half:] = keep_ref[:, 2 * win : 2 * win + width - half].astype(BF)


def finish(which, recv, keep, width):
    tokens = recv.shape[0]
    smem = pl.BlockSpec(memory_space=pltpu.SMEM)
    vmem = pl.BlockSpec(memory_space=pltpu.VMEM)
    return pl.pallas_call(
        functools.partial(finish_kernel, width=width),
        in_specs=[smem, vmem, vmem],
        out_shape=jax.ShapeDtypeStruct((tokens, width), BF),
        compiler_params=pltpu.CompilerParams(vmem_limit_bytes=24 * 2**20),
        name="finish",
    )(which, recv, keep)


def fold_kernel(keep_ref, *refs):
    count = (len(refs) - 1) // 2
    got_refs, send_refs, left_ref = refs[:count], refs[count:-1], refs[-1]
    for (lo, hi), got_ref, send_ref in zip(bounds(keep_ref.shape[1]), got_refs, send_refs):
        for q in range(keep_ref.shape[0]):
            total = (keep_ref[q, lo:hi].astype(F32) + got_ref[q].astype(F32)).astype(BF)
            if q % 2:
                send_ref[q // 2] = total
            else:
                left_ref[q // 2, lo:hi] = total


def fold(keep, got):
    shapes = [jax.ShapeDtypeStruct((x.shape[0] // 2,) + x.shape[1:], BF) for x in (*got, keep)]
    found = pl.pallas_call(
        fold_kernel,
        out_shape=tuple(shapes),
        compiler_params=pltpu.CompilerParams(vmem_limit_bytes=8 * 2**20),
        name="fold",
    )(keep, *got)
    return found[:-1], found[-1]


def close_kernel(keep_ref, *refs):
    out_ref = refs[-1]
    for (lo, hi), got_ref in zip(bounds(keep_ref.shape[1]), refs):
        out_ref[lo:hi] = (keep_ref[0, lo:hi].astype(F32) + got_ref[0].astype(F32)).astype(BF)
    spare = out_ref.shape[0] - keep_ref.shape[1]
    if spare:
        out_ref[keep_ref.shape[1] :] = jnp.zeros((spare, ROWS, LANES), BF)


def close(keep, got, size):
    return pl.pallas_call(
        close_kernel,
        out_shape=jax.ShapeDtypeStruct((size, ROWS, LANES), BF),
        compiler_params=pltpu.CompilerParams(vmem_limit_bytes=8 * 2**20),
        name="close",
    )(keep, *got)


def join_kernel(*refs):
    count = len(refs) // 3
    for i in range(count):
        have_ref, got_ref, out_ref = refs[2 * i], refs[2 * i + 1], refs[2 * count + i]
        size = have_ref.shape[0]
        out_ref[:size] = have_ref[...]
        out_ref[size:] = got_ref[...]


def join(pairs):
    shapes = [jax.ShapeDtypeStruct((2 * have.shape[0],) + have.shape[1:], BF) for have, _ in pairs]
    return pl.pallas_call(
        join_kernel,
        out_shape=tuple(shapes),
        compiler_params=pltpu.CompilerParams(vmem_limit_bytes=8 * 2**20),
        name="join",
    )(*[x for pair in pairs for x in pair])


def reduce_kernel(parts_ref, out_ref, *, factor):
    out_ref[...] = (jnp.sum(parts_ref[...].astype(F32), axis=0) * factor).astype(BF)


def reduce(parts, factor):
    return pl.pallas_call(
        functools.partial(reduce_kernel, factor=factor),
        out_shape=jax.ShapeDtypeStruct(parts.shape[1:], BF),
        compiler_params=pltpu.CompilerParams(vmem_limit_bytes=4 * 2**20),
        name="reduce",
    )(parts)


def trio_kernel(own_ref, below_ref, above_ref, all_ref, two_ref):
    size = own_ref.shape[0]
    for i, ref in enumerate((below_ref, own_ref, above_ref)):
        all_ref[i * size : (i + 1) * size] = ref[...]
        if i < 2:
            two_ref[i * size : (i + 1) * size] = ref[...]


def trio(own, below, above):
    size = own.shape[0]
    return pl.pallas_call(
        trio_kernel,
        out_shape=tuple(jax.ShapeDtypeStruct((n * size,) + own.shape[1:], BF) for n in (3, 2)),
        compiler_params=pltpu.CompilerParams(vmem_limit_bytes=4 * 2**20),
        name="trio",
    )(own, below, above)


def place_kernel(clip_ref, near_ref, below_ref, above_ref, *refs, clips):
    out_refs, all_s = refs[:-1], refs[-1]
    size = all_s.shape[0] // clips
    for ref, first in ((near_ref, -1), (below_ref, -4), (above_ref, 2)):
        for i in range(ref.shape[0] // size):
            at = lax.rem(clip_ref[0] + (first + i + clips), clips) * size
            all_s[pl.ds(at, size)] = ref[i * size : (i + 1) * size]
    for (lo, hi), out_ref in zip(bounds(sum(ref.shape[1] for ref in out_refs)), out_refs):
        out_ref[0] = all_s[lo:hi]


def place(clip, near, below, above, clips, size):
    total = near.shape[0] // 3 * clips
    smem = pl.BlockSpec(memory_space=pltpu.SMEM)
    vmem = pl.BlockSpec(memory_space=pltpu.VMEM)
    return pl.pallas_call(
        functools.partial(place_kernel, clips=clips),
        in_specs=[smem, vmem, vmem, vmem],
        out_shape=tuple(jax.ShapeDtypeStruct((1, hi - lo, ROWS, LANES), BF) for lo, hi in bounds(size)),
        scratch_shapes=[pltpu.VMEM((total, ROWS, LANES), BF)],
        compiler_params=pltpu.CompilerParams(vmem_limit_bytes=4 * 2**20),
        name="place",
    )(clip, near, below, above)


def untile_kernel(where_ref, half_ref, *refs):
    pieces, (out_ref, tiles_s) = refs[:-2], refs[-2:]
    size = tiles_s.shape[0] // 16
    pieces = iter(pieces)
    for side in range(2):
        half = half_ref[0] ^ side
        for far in range(2):
            for (lo, hi), orders in zip(bounds(size), ORDERS):
                piece = next(pieces)
                order = masks_of(orders, half)
                for q in range(4):
                    k = picked(q, order[2], order[1]) ^ (order[0] * far)
                    at = (half * 8 + (where_ref[0] ^ k)) * size + lo
                    tiles_s[pl.ds(at, hi - lo)] = piece[q]
    rows = out_ref.shape[0] // 2
    tiles = rows // ROWS
    for half in range(2):
        for j in range(out_ref.shape[1] // LANES):
            start = half * 8 * size + j * tiles
            block = tiles_s[start : start + tiles].reshape(rows, LANES)
            out_ref[half * rows : (half + 1) * rows, j * LANES : (j + 1) * LANES] = block


def untile(where, half, pieces, rows, width):
    smem = pl.BlockSpec(memory_space=pltpu.SMEM)
    vmem = pl.BlockSpec(memory_space=pltpu.VMEM)
    tiles = sum(4 * piece.shape[1] for piece in pieces)
    return pl.pallas_call(
        untile_kernel,
        in_specs=[smem, smem] + [vmem] * len(pieces),
        out_shape=jax.ShapeDtypeStruct((rows, width), BF),
        scratch_shapes=[pltpu.VMEM((tiles, ROWS, LANES), BF)],
        compiler_params=pltpu.CompilerParams(vmem_limit_bytes=16 * 2**20),
        name="untile",
    )(where, half, *pieces)


def swap(x, axes, k):
    count = math.prod(lax.axis_size(a) for a in axes)
    return lax.ppermute(x, axes, [(i, i ^ k) for i in range(count)])


def exchange(x, axis):
    parts = x.reshape((-1,) + x.shape[-3:])
    return lax.all_to_all(parts, axis, split_axis=0, concat_axis=0, tiled=True)


def plane_size():
    return lax.axis_size("xlo") * lax.axis_size("y")


def meet(blocks, level):
    found = []
    for block, orders in zip(blocks, ORDERS):
        pairs = [(p * 2 + c, (p ^ orders[c][level]) * 2 + c) for p in range(plane_size()) for c in range(2)]
        found.append(lax.ppermute(block, SEQ, pairs))
    return found


def sum_plane(found, beside, size):
    send, keep = found[:-1], found[-1]
    got, beside = lax.optimization_barrier((meet(send, 0), beside))
    send, keep = fold(keep, got)
    send, keep = fold(keep, meet(send, 1))
    return close(keep, meet(send, 2), size), beside


def shift(x, axis, step):
    count = lax.axis_size(axis)
    return lax.ppermute(x, axis, [(i, (i + step) % count) for i in range(count)])


def gather_clips(own, home):
    below, above = shift(own, "dp", 1), shift(own, "dp", -1)
    near, two = trio(own, below, above)
    return near, shift(near, "dp", 3), shift(two, "dp", -3), home


def gather_plane(have, where, half, rows, width, beside):
    got, beside = lax.optimization_barrier((meet(have, 2), beside))
    have = join(list(zip(have, got)))
    have = join(list(zip(have, meet(have, 1))))
    got = meet(have, 0)
    got[-1], have, beside = lax.optimization_barrier((got[-1], have, unpack(beside)))
    pieces = list(have) + got
    pieces = pieces + [swap(piece, ("core",), 1) for piece in pieces]
    return untile(where, half, pieces, rows, width), beside


def body(latent, mod_shift, mod_scale, w_qkv, q_gain, k_gain, cotangent):
    _, _, patches, width = latent.shape
    hw = w_qkv.shape[2]
    hd = q_gain.shape[0]
    heads = hw // hd
    frames = 1
    for a in SEQ:
        frames *= lax.axis_size(a)
    own_patches = patches // frames
    clips = lax.axis_size("dp")
    wt = w_qkv.transpose(1, 2, 0).reshape(3 * hw, width)
    x = pack(latent[0, 0], cotangent[0, 0].T).reshape(frames, own_patches, width + hw)
    x = lax.all_to_all(x, SEQ, split_axis=0, concat_axis=0, tiled=True).reshape(patches, width + hw)
    affine = jnp.concatenate([mod_shift, 1.0 + mod_scale])
    core = lax.axis_index("core").astype(jnp.int32).reshape(1)
    which = lax.axis_index("tensor").astype(jnp.int32).reshape(1)
    where = lax.axis_index(PLANE).astype(jnp.int32).reshape(1)
    mod, gp_keep, gp_send, att_t = attend(
        core, x, affine, wt, q_gain[:, None], k_gain[:, None], own_patches, heads, hd
    )
    used = (3 * hw // 2 // ROWS) * (width // LANES)
    size = -(-used // plane_size())
    gp_other, mod_other = swap(gp_send, ("core",), 1), swap(mod, ("core",), 1)
    found = outer(where, core, gp_keep, gp_other, mod, mod_other, size * plane_size())
    send, keep = split(core, which, x, affine, wt, gp_keep, gp_send, att_t)
    own, send = sum_plane(found, send, -(-size // clips) * clips)
    own, send = lax.optimization_barrier((own, send))
    recv = lax.ppermute(send, "tensor", [(0, 1), (1, 0)])
    own = exchange(own.reshape((clips, own.shape[0] // clips) + own.shape[1:]), "dp")
    own = reduce(own, 1.0 / math.sqrt(clips * frames * patches))
    own, recv = lax.optimization_barrier((own, recv))
    home = finish(which, recv, keep, width).reshape(frames, own_patches, width)
    near, below, above, home = gather_clips(own, home)
    home = lax.all_to_all(home, SEQ, split_axis=0, concat_axis=0, tiled=True)
    clip = lax.axis_index("dp").astype(jnp.int32).reshape(1)
    have = place(clip, near, below, above, clips, size)
    home = home.reshape(patches, width)
    grad_qkv, (grad_t, att_t) = gather_plane(have, where, core, 3 * hw, width, home)
    grad_qkv = grad_qkv.reshape(3, hw, width).transpose(2, 0, 1)
    return (att_t.T[None, None], grad_t.T[None, None], grad_qkv)


def solution(mesh):
    fine = Mesh(mesh.devices.reshape(mesh.shape["dp"], 2, 4, 2, 2), ("dp",) + SEQ + ("tensor",))
    in_specs = (
        P("dp", SEQ, None, None),
        P("dp", None),
        P("dp", None),
        P(None, None, "tensor"),
        P(),
        P(),
        P("dp", SEQ, None, "tensor"),
    )
    out_specs = (
        P("dp", SEQ, None, "tensor"),
        P("dp", SEQ, None, "tensor"),
        P(None, None, "tensor"),
    )
    return jax.shard_map(body, mesh=fine, in_specs=in_specs, out_specs=out_specs, check_vma=False)
```

```python
import functools
import math

import jax
import jax.numpy as jnp
from jax import lax
from jax.experimental import pallas as pl
from jax.experimental.pallas import tpu as pltpu
from jax.sharding import Mesh, PartitionSpec as P

BF = jnp.bfloat16
F32 = jnp.float32
EPS = 1e-06
NN = (((1,), (0,)), ((), ()))
NT = (((1,), (1,)), ((), ()))
LOG2E = math.log2(math.e)
ROWS, LANES = 16, 128
PLANE = ("xlo", "y")
SEQ = PLANE + ("core",)


def mm(a, b, dims):
    return lax.dot_general(a, b, dims, preferred_element_type=F32)


def eye(n):
    rows = lax.broadcasted_iota(jnp.int32, (n, n), 0)
    cols = lax.broadcasted_iota(jnp.int32, (n, n), 1)
    return jnp.where(rows == cols, 1.0, 0.0).astype(BF)


def fetch(pairs, sems):
    copies = [pltpu.make_async_copy(src, dst, sems.at[i]) for i, (src, dst) in enumerate(pairs)]
    for copy in copies:
        copy.start()
    return copies


def pack_kernel(latent_hbm, cot_hbm, out_ref, latent_s, cot_s, sems):
    width = latent_s.shape[1]
    first, second = fetch([(cot_hbm, cot_s), (latent_hbm, latent_s)], sems)
    ident = eye(latent_s.shape[0])
    first.wait()
    out_ref[:, width:] = mm(ident, cot_s[...], NT).astype(BF)
    second.wait()
    out_ref[:, :width] = latent_s[...]


def pack(latent, cot_t):
    tokens, width = latent.shape
    hbm = pl.BlockSpec(memory_space=pltpu.HBM)
    return pl.pallas_call(
        pack_kernel,
        in_specs=[hbm, hbm],
        out_shape=jax.ShapeDtypeStruct((tokens, width + cot_t.shape[0]), BF),
        scratch_shapes=[
            pltpu.VMEM(latent.shape, BF),
            pltpu.VMEM(cot_t.shape, BF),
            pltpu.SemaphoreType.DMA((2,)),
        ],
        compiler_params=pltpu.CompilerParams(vmem_limit_bytes=60 * 2**20),
        name="pack",
    )(latent, cot_t)


def unpack_kernel(rows_ref, first_ref, second_ref):
    ident = eye(LANES)
    half = first_ref.shape[0]
    for start in range(0, 2 * half, LANES):
        found = mm(ident, rows_ref[:, start : start + LANES], NT).astype(BF)
        cut = min(max(half - start, 0), LANES)
        if cut:
            first_ref[start : start + cut] = found[:cut]
        if cut < LANES:
            second_ref[start + cut - half : start + LANES - half] = found[cut:]


def unpack(rows):
    tokens, width = rows.shape
    shape = jax.ShapeDtypeStruct((width // 2, tokens), BF)
    return pl.pallas_call(
        unpack_kernel,
        out_shape=(shape, shape),
        compiler_params=pltpu.CompilerParams(vmem_limit_bytes=8 * 2**20),
        name="unpack",
    )(rows)


def unit_of(values):
    width = values.shape[1]
    centred = values - jnp.sum(values, axis=1, keepdims=True) * (1.0 / width)
    inverse = lax.rsqrt(jnp.sum(centred * centred, axis=1, keepdims=True) * (1.0 / width) + EPS)
    return centred * inverse, inverse


def attend_kernel(core_ref, x_ref, affine_ref, wt_hbm, qg_ref, kg_ref,
                  mod_ref, gp_keep_ref, gp_send_ref, att_ref,
                  wt_s, rows_s, weights_s, w_s, grad_s, q_s, k_s, v_s, cot_s, sems, *, patches, heads, hd):
    tokens, _ = x_ref.shape
    width = affine_ref.shape[1]
    hw = heads * hd
    parts = [pl.ds(part * hw, hw) for part in range(3)]
    copies = fetch([(wt_hbm.at[rows], wt_s.at[rows]) for rows in parts], sems)
    unit, _ = unit_of(x_ref[:, :width].astype(F32))
    mod_ref[...] = (unit * affine_ref[1:2] + affine_ref[0:1]).astype(BF)
    mod = mod_ref[...]
    ident = eye(tokens)
    for start in range(0, hw, tokens):
        size = min(tokens, hw - start)
        block = x_ref[:, width + start : width + start + size]
        cot_s[start : start + size, :] = mm(ident[:size, :size], block, NT)

    def project(part):
        copies[part].wait()
        return mm(wt_s[part * hw : (part + 1) * hw, :], mod, NT).astype(BF).astype(F32)

    def norm(rows):
        inv = lax.rsqrt(jnp.sum(rows * rows, axis=0, keepdims=True) * (1.0 / hd) + EPS)
        return rows * inv, inv

    def back(hat, inv, gain, grad):
        weighted = grad * gain
        mean = jnp.sum(hat * weighted, axis=0, keepdims=True) * (1.0 / hd)
        return inv * (weighted - hat * mean)

    def put(part, h, rows):
        start = part * hw + h * hd
        rows_s[start : start + hd, :] = rows

    root = 1.0 / math.sqrt(hd)
    q_gain = qg_ref[...] * (root * LOG2E)
    k_gain = kg_ref[...]
    q_back = qg_ref[...] * root
    k_back = kg_ref[...] * (1.0 / LOG2E)
    each = [slice(h * hd, (h + 1) * hd) for h in range(heads)]

    spot = lax.broadcasted_iota(jnp.int32, (patches, tokens), 0)
    token = lax.broadcasted_iota(jnp.int32, (patches, tokens), 1)
    spots = jnp.where(lax.rem(token, patches) == spot, 16.0, 0.0)
    top = lax.broadcasted_iota(jnp.int32, (8, tokens), 0) == 0
    zeros = jnp.zeros((-(hd + patches + 8) % LANES, tokens), F32)
    q_tail = [spots, jnp.where(top, 16.0, 0.0), zeros]
    k_tail = [spots, jnp.where(top, -16.0, 0.0), zeros]
    v_tail = [jnp.where(top, 1.0, 0.0), jnp.zeros((-(hd + 8) % LANES, tokens), F32)]
    blank = jnp.zeros((-hd % LANES, tokens), F32)

    def rows_of(ref):
        found = []
        for h in range(0, heads, 2):
            both = mm(ident, ref[h : h + 2].reshape(2 * LANES, tokens), NT).astype(BF)
            found += [both[:, :LANES], both[:, LANES:]]
        return found

    q_all = project(0)
    q_inv = []
    for h, at in enumerate(each):
        hat, inv = norm(q_all[at])
        q_inv.append(inv)
        q_s[h] = jnp.concatenate([hat * q_gain] + q_tail).astype(BF)
    k_all = project(1)
    k_inv = []
    for h, at in enumerate(each):
        hat, inv = norm(k_all[at])
        k_inv.append(inv)
        k_s[h] = jnp.concatenate([hat * k_gain] + k_tail).astype(BF)
    v_all = project(2)
    for h, at in enumerate(each):
        v_s[h] = jnp.concatenate([v_all[at]] + v_tail).astype(BF)
    k_rows = rows_of(k_s)
    for h in range(heads):
        weights = jnp.exp2(mm(k_rows[h], q_s[h], NN))
        weights_s[h] = weights
        w_s[h] = weights.astype(BF)
    v_rows = rows_of(v_s)
    deltas, cots = [], []
    for h, at in enumerate(each):
        summed = mm(v_s[h], w_s[h], NN)
        share = 1.0 / summed[hd : hd + 1]
        out = summed[:hd] * share
        att_ref[at, :] = out.astype(BF)
        cot_share = cot_s[at, :] * share
        cots.append(jnp.concatenate([cot_share, blank]).astype(BF))
        deltas.append(jnp.sum(out * cot_share, axis=0, keepdims=True))
    for h in range(heads):
        grad_s[h] = (weights_s[h] * (mm(v_rows[h], cots[h], NN) - deltas[h])).astype(BF)
        put(2, h, mm(cots[h], w_s[h], NT)[:hd])
    for h, at in enumerate(each):
        put(0, h, back(q_all[at] * q_inv[h], q_inv[h], q_back, mm(k_s[h], grad_s[h], NN)[:hd]))
        put(1, h, back(k_all[at] * k_inv[h], k_inv[h], k_back, mm(q_s[h], grad_s[h], NT)[:hd]))
    size = gp_keep_ref.shape[0]
    gp_keep_ref[...] = rows_s[pl.ds(pl.multiple_of(core_ref[0] * size, ROWS), size), :].astype(BF)
    gp_send_ref[...] = rows_s[pl.ds(pl.multiple_of((1 - core_ref[0]) * size, ROWS), size), :].astype(BF)


def attend(core, x, affine, wt, qg, kg, patches, heads, hd):
    tokens = x.shape[0]
    width = wt.shape[1]
    hw = heads * hd
    smem = pl.BlockSpec(memory_space=pltpu.SMEM)
    vmem = pl.BlockSpec(memory_space=pltpu.VMEM)
    half = jax.ShapeDtypeStruct((3 * hw // 2, tokens), BF)
    tall = pltpu.VMEM((heads, LANES, tokens), BF)
    return pl.pallas_call(
        functools.partial(attend_kernel, patches=patches, heads=heads, hd=hd),
        in_specs=[smem, vmem, vmem, pl.BlockSpec(memory_space=pltpu.HBM), vmem, vmem],
        out_shape=(
            jax.ShapeDtypeStruct((tokens, width), BF),
            half,
            half,
            jax.ShapeDtypeStruct((hw, tokens), BF),
        ),
        scratch_shapes=[
            pltpu.VMEM((3 * hw, width), BF),
            pltpu.VMEM((3 * hw, tokens), F32),
            pltpu.VMEM((heads, tokens, tokens), F32),
            pltpu.VMEM((heads, tokens, tokens), BF),
            pltpu.VMEM((heads, tokens, tokens), BF),
            tall,
            tall,
            tall,
            pltpu.VMEM((hw, tokens), F32),
            pltpu.SemaphoreType.DMA((3,)),
        ],
        compiler_params=pltpu.CompilerParams(vmem_limit_bytes=52 * 2**20),
        name="attend",
    )(core, x, affine, wt, qg, kg)


def split_kernel(core_ref, which_ref, x_hbm, affine_hbm, wt_hbm, gp_keep_hbm, gp_send_hbm, att_hbm,
                 send_ref, keep_ref, x_ref, affine_ref, wt_s, gp_keep_ref, gp_send_ref, att_ref, gp_s, sems):
    tokens, _ = x_ref.shape
    width = affine_ref.shape[1]
    hw = att_ref.shape[0]
    parts = [pl.ds(part * hw, hw) for part in range(3)]
    copies = fetch(
        [(x_hbm, x_ref), (gp_keep_hbm, gp_keep_ref), (gp_send_hbm, gp_send_ref)]
        + [(wt_hbm.at[rows], wt_s.at[rows]) for rows in parts]
        + [(affine_hbm, affine_ref), (att_hbm, att_ref)],
        sems,
    )
    for copy in copies[:3]:
        copy.wait()
    unit, inverse = unit_of(x_ref[:, :width].astype(F32))
    ident = eye(tokens)
    size = gp_keep_ref.shape[0]
    gp_s[pl.ds(pl.multiple_of(core_ref[0] * size, ROWS), size), :] = gp_keep_ref[...]
    gp_s[pl.ds(pl.multiple_of((1 - core_ref[0]) * size, ROWS), size), :] = gp_send_ref[...]
    grad = jnp.zeros((tokens, width), F32)
    for part in range(3):
        at = slice(part * hw, (part + 1) * hw)
        rows = mm(ident, gp_s[at, :], NT).astype(BF)
        copies[3 + part].wait()
        grad = grad + mm(rows, wt_s[at, :], NN)
    half = width // 2
    win = send_ref.shape[1]
    mine_low = which_ref[0] == 0
    for copy in copies[6:]:
        copy.wait()
    scaled = grad * affine_ref[1:2]
    first = jnp.sum(scaled, axis=1, keepdims=True)
    second = jnp.sum(scaled * unit, axis=1, keepdims=True)
    col = lax.broadcasted_iota(jnp.int32, (tokens, win), 1)
    here = jnp.where(mine_low, half, 0)
    there = jnp.where(mine_low, 0, half)
    low, high = scaled[:, :win], scaled[:, width - win :]
    send = jnp.where(mine_low, high, low)
    keep = jnp.where(mine_low, low, high)
    for place, term in enumerate((first, second)):
        coarse = term.astype(BF).astype(F32)
        send = jnp.where(col == there + 2 * place, coarse, send)
        send = jnp.where(col == there + 2 * place + 1, term - coarse, send)
    for place, term in enumerate((first, second, inverse)):
        keep = jnp.where(col == here + place, term, keep)
    send_ref[...] = send.astype(BF)
    keep_ref[:, :win] = keep
    keep_ref[:, win : 2 * win] = jnp.where(mine_low, unit[:, :win], unit[:, width - win :])
    keep_ref[:, 2 * win : 2 * win + hw] = mm(ident, att_ref[...], NT)


def split(core, which, x, affine, wt, gp_keep, gp_send, att):
    tokens = x.shape[0]
    hw = att.shape[0]
    win = window_of(wt.shape[1] // 2)
    smem = pl.BlockSpec(memory_space=pltpu.SMEM)
    vmem = pl.BlockSpec(memory_space=pltpu.VMEM)
    return pl.pallas_call(
        split_kernel,
        in_specs=[smem, smem] + [pl.BlockSpec(memory_space=pltpu.HBM)] * 6,
        out_shape=(
            jax.ShapeDtypeStruct((tokens, win), BF),
            jax.ShapeDtypeStruct((tokens, 2 * win + window_of(hw)), F32),
        ),
        scratch_shapes=[pltpu.VMEM(a.shape, a.dtype) for a in (x, affine, wt, gp_keep, gp_send, att)]
        + [pltpu.VMEM((wt.shape[0], tokens), BF), pltpu.SemaphoreType.DMA((8,))],
        compiler_params=pltpu.CompilerParams(vmem_limit_bytes=58 * 2**20),
        name="split",
    )(core, which, x, affine, wt, gp_keep, gp_send, att)


def outer_kernel(where_ref, core_ref, gp_a, gp_b, mod_a, mod_b, *refs):
    out_refs, tiles_s = refs[:-1], refs[-1]
    rows, width = gp_a.shape[0], mod_a.shape[1]
    tiles = rows // ROWS
    used = tiles * (width // LANES)
    tiles_s[used:] = jnp.zeros((tiles_s.shape[0] - used, ROWS, LANES), BF)
    gp = jnp.concatenate([gp_a[...], gp_b[...]], axis=1)
    for start in range(0, width, 2 * LANES):
        stop = min(start + 2 * LANES, width)
        mod = jnp.concatenate([mod_a[:, start:stop], mod_b[:, start:stop]], axis=0)
        found = mm(gp, mod, NN).astype(BF)
        for at in range(0, stop - start, LANES):
            j = (start + at) // LANES
            tiles_s[j * tiles : (j + 1) * tiles] = found[:, at : at + LANES].reshape(tiles, ROWS, LANES)
    size = tiles_s.shape[0] // 8
    keep_ref = out_refs[-1]
    for (lo, hi), orders, send_ref in zip(bounds(size), ORDERS, out_refs):
        order = masks_of(orders, core_ref[0])
        for q in range(4):
            k = picked(q, order[1], order[2])
            at = (where_ref[0] ^ k) * size + lo
            keep_ref[q, lo:hi] = tiles_s[pl.ds(at, hi - lo)]
            at = (where_ref[0] ^ (k ^ order[0])) * size + lo
            send_ref[q] = tiles_s[pl.ds(at, hi - lo)]


def outer(where, core, gp_a, gp_b, mod_a, mod_b, padded):
    smem = pl.BlockSpec(memory_space=pltpu.SMEM)
    vmem = pl.BlockSpec(memory_space=pltpu.VMEM)
    size = padded // 8
    shapes = [jax.ShapeDtypeStruct((4, n, ROWS, LANES), BF) for n in [hi - lo for lo, hi in bounds(size)] + [size]]
    return pl.pallas_call(
        outer_kernel,
        in_specs=[smem, smem] + [vmem] * 4,
        out_shape=tuple(shapes),
        scratch_shapes=[pltpu.VMEM((padded, ROWS, LANES), BF)],
        compiler_params=pltpu.CompilerParams(vmem_limit_bytes=16 * 2**20),
        name="outer",
    )(where, core, gp_a, gp_b, mod_a, mod_b)


ORDERS = (((1, 3, 4), (4, 1, 3)), ((3, 4, 1), (3, 4, 1)))


def bounds(size):
    cut = -(-2 * size // 3)
    return [(0, cut), (cut, size)]


def masks_of(orders, core):
    return [jnp.where(core == 0, a, b) for a, b in zip(*orders)]


def picked(q, first, second):
    return (first if q % 2 else 0) ^ (second if q // 2 else 0)


def window_of(half):
    return -(-half // LANES) * LANES


def finish_kernel(which_ref, recv_ref, keep_ref, out_ref, *, width):
    half = width // 2
    win = recv_ref.shape[1]
    mine_low = which_ref[0] == 0
    recv = recv_ref[...].astype(F32)
    keep = keep_ref[:, :win]
    unit = keep_ref[:, win : 2 * win]

    def column(block, place):
        return jnp.where(mine_low, block[:, half + place : half + place + 1], block[:, place : place + 1])

    first = column(keep, 0) + (column(recv, 0) + column(recv, 1))
    second = column(keep, 1) + (column(recv, 2) + column(recv, 3))
    inverse = column(keep, 2)
    grad = keep + recv
    out = inverse * (grad - first * (1.0 / width) - unit * (second * (1.0 / width)))
    moved = pltpu.roll(out, win - (win - half), 1)
    out_ref[:, :half] = jnp.where(mine_low, out, moved)[:, :half].astype(BF)
    out_ref[:, half:] = keep_ref[:, 2 * win : 2 * win + width - half].astype(BF)


def finish(which, recv, keep, width):
    tokens = recv.shape[0]
    smem = pl.BlockSpec(memory_space=pltpu.SMEM)
    vmem = pl.BlockSpec(memory_space=pltpu.VMEM)
    return pl.pallas_call(
        functools.partial(finish_kernel, width=width),
        in_specs=[smem, vmem, vmem],
        out_shape=jax.ShapeDtypeStruct((tokens, width), BF),
        compiler_params=pltpu.CompilerParams(vmem_limit_bytes=24 * 2**20),
        name="finish",
    )(which, recv, keep)


def fold_kernel(keep_ref, *refs):
    count = (len(refs) - 1) // 2
    got_refs, send_refs, left_ref = refs[:count], refs[count:-1], refs[-1]
    for (lo, hi), got_ref, send_ref in zip(bounds(keep_ref.shape[1]), got_refs, send_refs):
        for q in range(keep_ref.shape[0]):
            total = (keep_ref[q, lo:hi].astype(F32) + got_ref[q].astype(F32)).astype(BF)
            if q % 2:
                send_ref[q // 2] = total
            else:
                left_ref[q // 2, lo:hi] = total


def fold(keep, got):
    shapes = [jax.ShapeDtypeStruct((x.shape[0] // 2,) + x.shape[1:], BF) for x in (*got, keep)]
    found = pl.pallas_call(
        fold_kernel,
        out_shape=tuple(shapes),
        compiler_params=pltpu.CompilerParams(vmem_limit_bytes=8 * 2**20),
        name="fold",
    )(keep, *got)
    return found[:-1], found[-1]


def close_kernel(keep_ref, *refs):
    out_ref = refs[-1]
    for (lo, hi), got_ref in zip(bounds(keep_ref.shape[1]), refs):
        out_ref[lo:hi] = (keep_ref[0, lo:hi].astype(F32) + got_ref[0].astype(F32)).astype(BF)
    spare = out_ref.shape[0] - keep_ref.shape[1]
    if spare:
        out_ref[keep_ref.shape[1] :] = jnp.zeros((spare, ROWS, LANES), BF)


def close(keep, got, size):
    return pl.pallas_call(
        close_kernel,
        out_shape=jax.ShapeDtypeStruct((size, ROWS, LANES), BF),
        compiler_params=pltpu.CompilerParams(vmem_limit_bytes=8 * 2**20),
        name="close",
    )(keep, *got)


def join_kernel(*refs):
    count = len(refs) // 3
    for i in range(count):
        have_ref, got_ref, out_ref = refs[2 * i], refs[2 * i + 1], refs[2 * count + i]
        size = have_ref.shape[0]
        out_ref[:size] = have_ref[...]
        out_ref[size:] = got_ref[...]


def join(pairs):
    shapes = [jax.ShapeDtypeStruct((2 * have.shape[0],) + have.shape[1:], BF) for have, _ in pairs]
    return pl.pallas_call(
        join_kernel,
        out_shape=tuple(shapes),
        compiler_params=pltpu.CompilerParams(vmem_limit_bytes=8 * 2**20),
        name="join",
    )(*[x for pair in pairs for x in pair])


def reduce_kernel(parts_ref, out_ref, *, factor):
    out_ref[...] = (jnp.sum(parts_ref[...].astype(F32), axis=0) * factor).astype(BF)


def reduce(parts, factor):
    return pl.pallas_call(
        functools.partial(reduce_kernel, factor=factor),
        out_shape=jax.ShapeDtypeStruct(parts.shape[1:], BF),
        compiler_params=pltpu.CompilerParams(vmem_limit_bytes=4 * 2**20),
        name="reduce",
    )(parts)


def trio_kernel(own_ref, below_ref, above_ref, all_ref, two_ref):
    size = own_ref.shape[0]
    for i, ref in enumerate((below_ref, own_ref, above_ref)):
        all_ref[i * size : (i + 1) * size] = ref[...]
        if i < 2:
            two_ref[i * size : (i + 1) * size] = ref[...]


def trio(own, below, above):
    size = own.shape[0]
    return pl.pallas_call(
        trio_kernel,
        out_shape=tuple(jax.ShapeDtypeStruct((n * size,) + own.shape[1:], BF) for n in (3, 2)),
        compiler_params=pltpu.CompilerParams(vmem_limit_bytes=4 * 2**20),
        name="trio",
    )(own, below, above)


def place_kernel(clip_ref, near_ref, below_ref, above_ref, *refs, clips):
    out_refs, all_s = refs[:-1], refs[-1]
    size = all_s.shape[0] // clips
    for ref, first in ((near_ref, -1), (below_ref, -4), (above_ref, 2)):
        for i in range(ref.shape[0] // size):
            at = lax.rem(clip_ref[0] + (first + i + clips), clips) * size
            all_s[pl.ds(at, size)] = ref[i * size : (i + 1) * size]
    for (lo, hi), out_ref in zip(bounds(sum(ref.shape[1] for ref in out_refs)), out_refs):
        out_ref[0] = all_s[lo:hi]


def place(clip, near, below, above, clips, size):
    total = near.shape[0] // 3 * clips
    smem = pl.BlockSpec(memory_space=pltpu.SMEM)
    vmem = pl.BlockSpec(memory_space=pltpu.VMEM)
    return pl.pallas_call(
        functools.partial(place_kernel, clips=clips),
        in_specs=[smem, vmem, vmem, vmem],
        out_shape=tuple(jax.ShapeDtypeStruct((1, hi - lo, ROWS, LANES), BF) for lo, hi in bounds(size)),
        scratch_shapes=[pltpu.VMEM((total, ROWS, LANES), BF)],
        compiler_params=pltpu.CompilerParams(vmem_limit_bytes=4 * 2**20),
        name="place",
    )(clip, near, below, above)


def untile_kernel(where_ref, half_ref, *refs):
    pieces, (out_ref, tiles_s) = refs[:-2], refs[-2:]
    size = tiles_s.shape[0] // 16
    pieces = iter(pieces)
    for side in range(2):
        half = half_ref[0] ^ side
        for far in range(2):
            for (lo, hi), orders in zip(bounds(size), ORDERS):
                piece = next(pieces)
                order = masks_of(orders, half)
                for q in range(4):
                    k = picked(q, order[2], order[1]) ^ (order[0] * far)
                    at = (half * 8 + (where_ref[0] ^ k)) * size + lo
                    tiles_s[pl.ds(at, hi - lo)] = piece[q]
    rows = out_ref.shape[0] // 2
    tiles = rows // ROWS
    for half in range(2):
        for j in range(out_ref.shape[1] // LANES):
            start = half * 8 * size + j * tiles
            block = tiles_s[start : start + tiles].reshape(rows, LANES)
            out_ref[half * rows : (half + 1) * rows, j * LANES : (j + 1) * LANES] = block


def untile(where, half, pieces, rows, width):
    smem = pl.BlockSpec(memory_space=pltpu.SMEM)
    vmem = pl.BlockSpec(memory_space=pltpu.VMEM)
    tiles = sum(4 * piece.shape[1] for piece in pieces)
    return pl.pallas_call(
        untile_kernel,
        in_specs=[smem, smem] + [vmem] * len(pieces),
        out_shape=jax.ShapeDtypeStruct((rows, width), BF),
        scratch_shapes=[pltpu.VMEM((tiles, ROWS, LANES), BF)],
        compiler_params=pltpu.CompilerParams(vmem_limit_bytes=16 * 2**20),
        name="untile",
    )(where, half, *pieces)


def swap(x, axes, k):
    count = math.prod(lax.axis_size(a) for a in axes)
    return lax.ppermute(x, axes, [(i, i ^ k) for i in range(count)])


def exchange(x, axis):
    parts = x.reshape((-1,) + x.shape[-3:])
    return lax.all_to_all(parts, axis, split_axis=0, concat_axis=0, tiled=True)


def plane_size():
    return lax.axis_size("xlo") * lax.axis_size("y")


def meet(blocks, level):
    found = []
    for block, orders in zip(blocks, ORDERS):
        pairs = [(p * 2 + c, (p ^ orders[c][level]) * 2 + c) for p in range(plane_size()) for c in range(2)]
        found.append(lax.ppermute(block, SEQ, pairs))
    return found


def sum_plane(found, beside, size):
    send, keep = found[:-1], found[-1]
    got, beside = lax.optimization_barrier((meet(send, 0), beside))
    send, keep = fold(keep, got)
    send, keep = fold(keep, meet(send, 1))
    return close(keep, meet(send, 2), size), beside


def shift(x, axis, step):
    count = lax.axis_size(axis)
    return lax.ppermute(x, axis, [(i, (i + step) % count) for i in range(count)])


def gather_clips(own, home):
    near, two = trio(own, shift(own, "dp", 1), shift(own, "dp", -1))
    near, two, home = lax.optimization_barrier((near, two, home))
    return near, shift(near, "dp", 3), shift(two, "dp", -3), home


def gather_plane(have, where, half, rows, width, beside):
    got, beside = lax.optimization_barrier((meet(have, 2), beside))
    have = join(list(zip(have, got)))
    have = join(list(zip(have, meet(have, 1))))
    got = meet(have, 0)
    got[-1], have, beside = lax.optimization_barrier((got[-1], have, unpack(beside)))
    pieces = list(have) + got
    pieces = pieces + [swap(piece, ("core",), 1) for piece in pieces]
    return untile(where, half, pieces, rows, width), beside


def body(latent, mod_shift, mod_scale, w_qkv, q_gain, k_gain, cotangent):
    _, _, patches, width = latent.shape
    hw = w_qkv.shape[2]
    hd = q_gain.shape[0]
    heads = hw // hd
    frames = 1
    for a in SEQ:
        frames *= lax.axis_size(a)
    own_patches = patches // frames
    clips = lax.axis_size("dp")
    wt = w_qkv.transpose(1, 2, 0).reshape(3 * hw, width)
    x = pack(latent[0, 0], cotangent[0, 0].T).reshape(frames, own_patches, width + hw)
    x = lax.all_to_all(x, SEQ, split_axis=0, concat_axis=0, tiled=True).reshape(patches, width + hw)
    affine = jnp.concatenate([mod_shift, 1.0 + mod_scale])
    core = lax.axis_index("core").astype(jnp.int32).reshape(1)
    which = lax.axis_index("tensor").astype(jnp.int32).reshape(1)
    where = lax.axis_index(PLANE).astype(jnp.int32).reshape(1)
    mod, gp_keep, gp_send, att_t = attend(
        core, x, affine, wt, q_gain[:, None], k_gain[:, None], own_patches, heads, hd
    )
    used = (3 * hw // 2 // ROWS) * (width // LANES)
    size = -(-used // plane_size())
    gp_other, mod_other = swap(gp_send, ("core",), 1), swap(mod, ("core",), 1)
    found = outer(where, core, gp_keep, gp_other, mod, mod_other, size * plane_size())
    send, keep = split(core, which, x, affine, wt, gp_keep, gp_send, att_t)
    own, send = sum_plane(found, send, -(-size // clips) * clips)
    own, send = lax.optimization_barrier((own, send))
    recv = lax.ppermute(send, "tensor", [(0, 1), (1, 0)])
    own = exchange(own.reshape((clips, own.shape[0] // clips) + own.shape[1:]), "dp")
    own, recv = lax.optimization_barrier((own, recv))
    own = reduce(own, 1.0 / math.sqrt(clips * frames * patches))
    home = finish(which, recv, keep, width).reshape(frames, own_patches, width)
    near, below, above, home = gather_clips(own, home)
    home = lax.all_to_all(home, SEQ, split_axis=0, concat_axis=0, tiled=True)
    clip = lax.axis_index("dp").astype(jnp.int32).reshape(1)
    have = place(clip, near, below, above, clips, size)
    home = home.reshape(patches, width)
    grad_qkv, (grad_t, att_t) = gather_plane(have, where, core, 3 * hw, width, home)
    grad_qkv = grad_qkv.reshape(3, hw, width).transpose(2, 0, 1)
    return (att_t.T[None, None], grad_t.T[None, None], grad_qkv)


def solution(mesh):
    fine = Mesh(mesh.devices.reshape(mesh.shape["dp"], 2, 4, 2, 2), ("dp",) + SEQ + ("tensor",))
    in_specs = (
        P("dp", SEQ, None, None),
        P("dp", None),
        P("dp", None),
        P(None, None, "tensor"),
        P(),
        P(),
        P("dp", SEQ, None, "tensor"),
    )
    out_specs = (
        P("dp", SEQ, None, "tensor"),
        P("dp", SEQ, None, "tensor"),
        P(None, None, "tensor"),
    )
    return jax.shard_map(body, mesh=fine, in_specs=in_specs, out_specs=out_specs, check_vma=False)
```

```python
import functools
import math

import jax
import jax.numpy as jnp
from jax import lax
from jax.experimental import pallas as pl
from jax.experimental.pallas import tpu as pltpu
from jax.sharding import Mesh, PartitionSpec as P

BF = jnp.bfloat16
F32 = jnp.float32
EPS = 1e-06
NN = (((1,), (0,)), ((), ()))
NT = (((1,), (1,)), ((), ()))
LOG2E = math.log2(math.e)
ROWS, LANES = 16, 128
PLANE = ("xlo", "y")
SEQ = PLANE + ("core",)


def mm(a, b, dims):
    return lax.dot_general(a, b, dims, preferred_element_type=F32)


def eye(n):
    rows = lax.broadcasted_iota(jnp.int32, (n, n), 0)
    cols = lax.broadcasted_iota(jnp.int32, (n, n), 1)
    return jnp.where(rows == cols, 1.0, 0.0).astype(BF)


def fetch(pairs, sems):
    copies = [pltpu.make_async_copy(src, dst, sems.at[i]) for i, (src, dst) in enumerate(pairs)]
    for copy in copies:
        copy.start()
    return copies


def pack_kernel(latent_hbm, cot_hbm, out_ref, latent_s, cot_s, sems):
    width = latent_s.shape[1]
    first, second = fetch([(cot_hbm, cot_s), (latent_hbm, latent_s)], sems)
    ident = eye(latent_s.shape[0])
    first.wait()
    out_ref[:, width:] = mm(ident, cot_s[...], NT).astype(BF)
    second.wait()
    out_ref[:, :width] = latent_s[...]


def pack(latent, cot_t):
    tokens, width = latent.shape
    hbm = pl.BlockSpec(memory_space=pltpu.HBM)
    return pl.pallas_call(
        pack_kernel,
        in_specs=[hbm, hbm],
        out_shape=jax.ShapeDtypeStruct((tokens, width + cot_t.shape[0]), BF),
        scratch_shapes=[
            pltpu.VMEM(latent.shape, BF),
            pltpu.VMEM(cot_t.shape, BF),
            pltpu.SemaphoreType.DMA((2,)),
        ],
        compiler_params=pltpu.CompilerParams(vmem_limit_bytes=60 * 2**20),
        name="pack",
    )(latent, cot_t)


def unpack_kernel(rows_ref, first_ref, second_ref):
    ident = eye(LANES)
    half = first_ref.shape[0]
    for start in range(0, 2 * half, LANES):
        found = mm(ident, rows_ref[:, start : start + LANES], NT).astype(BF)
        cut = min(max(half - start, 0), LANES)
        if cut:
            first_ref[start : start + cut] = found[:cut]
        if cut < LANES:
            second_ref[start + cut - half : start + LANES - half] = found[cut:]


def unpack(rows):
    tokens, width = rows.shape
    shape = jax.ShapeDtypeStruct((width // 2, tokens), BF)
    return pl.pallas_call(
        unpack_kernel,
        out_shape=(shape, shape),
        compiler_params=pltpu.CompilerParams(vmem_limit_bytes=8 * 2**20),
        name="unpack",
    )(rows)


def unit_of(values):
    width = values.shape[1]
    centred = values - jnp.sum(values, axis=1, keepdims=True) * (1.0 / width)
    inverse = lax.rsqrt(jnp.sum(centred * centred, axis=1, keepdims=True) * (1.0 / width) + EPS)
    return centred * inverse, inverse


def attend_kernel(core_ref, x_ref, affine_ref, wt_hbm, qg_ref, kg_ref,
                  mod_ref, gp_keep_ref, gp_send_ref, att_ref,
                  wt_s, rows_s, weights_s, w_s, grad_s, q_s, k_s, v_s, cot_s, sems, *, patches, heads, hd):
    tokens, _ = x_ref.shape
    width = affine_ref.shape[1]
    hw = heads * hd
    parts = [pl.ds(part * hw, hw) for part in range(3)]
    copies = fetch([(wt_hbm.at[rows], wt_s.at[rows]) for rows in parts], sems)
    unit, _ = unit_of(x_ref[:, :width].astype(F32))
    mod_ref[...] = (unit * affine_ref[1:2] + affine_ref[0:1]).astype(BF)
    mod = mod_ref[...]
    ident = eye(tokens)
    for start in range(0, hw, tokens):
        size = min(tokens, hw - start)
        block = x_ref[:, width + start : width + start + size]
        cot_s[start : start + size, :] = mm(ident[:size, :size], block, NT)

    def project(part):
        copies[part].wait()
        return mm(wt_s[part * hw : (part + 1) * hw, :], mod, NT).astype(BF).astype(F32)

    def norm(rows):
        inv = lax.rsqrt(jnp.sum(rows * rows, axis=0, keepdims=True) * (1.0 / hd) + EPS)
        return rows * inv, inv

    def back(hat, inv, gain, grad):
        weighted = grad * gain
        mean = jnp.sum(hat * weighted, axis=0, keepdims=True) * (1.0 / hd)
        return inv * (weighted - hat * mean)

    def put(part, h, rows):
        start = part * hw + h * hd
        rows_s[start : start + hd, :] = rows

    root = 1.0 / math.sqrt(hd)
    q_gain = qg_ref[...] * (root * LOG2E)
    k_gain = kg_ref[...]
    q_back = qg_ref[...] * root
    k_back = kg_ref[...] * (1.0 / LOG2E)
    each = [slice(h * hd, (h + 1) * hd) for h in range(heads)]

    spot = lax.broadcasted_iota(jnp.int32, (patches, tokens), 0)
    token = lax.broadcasted_iota(jnp.int32, (patches, tokens), 1)
    spots = jnp.where(lax.rem(token, patches) == spot, 16.0, 0.0)
    top = lax.broadcasted_iota(jnp.int32, (8, tokens), 0) == 0
    zeros = jnp.zeros((-(hd + patches + 8) % LANES, tokens), F32)
    q_tail = [spots, jnp.where(top, 16.0, 0.0), zeros]
    k_tail = [spots, jnp.where(top, -16.0, 0.0), zeros]
    v_tail = [jnp.where(top, 1.0, 0.0), jnp.zeros((-(hd + 8) % LANES, tokens), F32)]
    blank = jnp.zeros((-hd % LANES, tokens), F32)

    def rows_of(ref):
        found = []
        for h in range(0, heads, 2):
            both = mm(ident, ref[h : h + 2].reshape(2 * LANES, tokens), NT).astype(BF)
            found += [both[:, :LANES], both[:, LANES:]]
        return found

    q_all = project(0)
    q_inv = []
    for h, at in enumerate(each):
        hat, inv = norm(q_all[at])
        q_inv.append(inv)
        q_s[h] = jnp.concatenate([hat * q_gain] + q_tail).astype(BF)
    k_all = project(1)
    k_inv = []
    for h, at in enumerate(each):
        hat, inv = norm(k_all[at])
        k_inv.append(inv)
        k_s[h] = jnp.concatenate([hat * k_gain] + k_tail).astype(BF)
    v_all = project(2)
    for h, at in enumerate(each):
        v_s[h] = jnp.concatenate([v_all[at]] + v_tail).astype(BF)
    k_rows = rows_of(k_s)
    for h in range(heads):
        weights = jnp.exp2(mm(k_rows[h], q_s[h], NN))
        weights_s[h] = weights
        w_s[h] = weights.astype(BF)
    v_rows = rows_of(v_s)
    deltas, cots = [], []
    for h, at in enumerate(each):
        summed = mm(v_s[h], w_s[h], NN)
        share = 1.0 / summed[hd : hd + 1]
        out = summed[:hd] * share
        att_ref[at, :] = out.astype(BF)
        cot_share = cot_s[at, :] * share
        cots.append(jnp.concatenate([cot_share, blank]).astype(BF))
        deltas.append(jnp.sum(out * cot_share, axis=0, keepdims=True))
    for h in range(heads):
        grad_s[h] = (weights_s[h] * (mm(v_rows[h], cots[h], NN) - deltas[h])).astype(BF)
        put(2, h, mm(cots[h], w_s[h], NT)[:hd])
    for h, at in enumerate(each):
        put(0, h, back(q_all[at] * q_inv[h], q_inv[h], q_back, mm(k_s[h], grad_s[h], NN)[:hd]))
        put(1, h, back(k_all[at] * k_inv[h], k_inv[h], k_back, mm(q_s[h], grad_s[h], NT)[:hd]))
    size = gp_keep_ref.shape[0]
    gp_keep_ref[...] = rows_s[pl.ds(pl.multiple_of(core_ref[0] * size, ROWS), size), :].astype(BF)
    gp_send_ref[...] = rows_s[pl.ds(pl.multiple_of((1 - core_ref[0]) * size, ROWS), size), :].astype(BF)


def attend(core, x, affine, wt, qg, kg, patches, heads, hd):
    tokens = x.shape[0]
    width = wt.shape[1]
    hw = heads * hd
    smem = pl.BlockSpec(memory_space=pltpu.SMEM)
    vmem = pl.BlockSpec(memory_space=pltpu.VMEM)
    half = jax.ShapeDtypeStruct((3 * hw // 2, tokens), BF)
    tall = pltpu.VMEM((heads, LANES, tokens), BF)
    return pl.pallas_call(
        functools.partial(attend_kernel, patches=patches, heads=heads, hd=hd),
        in_specs=[smem, vmem, vmem, pl.BlockSpec(memory_space=pltpu.HBM), vmem, vmem],
        out_shape=(
            jax.ShapeDtypeStruct((tokens, width), BF),
            half,
            half,
            jax.ShapeDtypeStruct((hw, tokens), BF),
        ),
        scratch_shapes=[
            pltpu.VMEM((3 * hw, width), BF),
            pltpu.VMEM((3 * hw, tokens), F32),
            pltpu.VMEM((heads, tokens, tokens), F32),
            pltpu.VMEM((heads, tokens, tokens), BF),
            pltpu.VMEM((heads, tokens, tokens), BF),
            tall,
            tall,
            tall,
            pltpu.VMEM((hw, tokens), F32),
            pltpu.SemaphoreType.DMA((3,)),
        ],
        compiler_params=pltpu.CompilerParams(vmem_limit_bytes=52 * 2**20),
        name="attend",
    )(core, x, affine, wt, qg, kg)


def split_kernel(core_ref, which_ref, x_hbm, affine_hbm, wt_hbm, gp_keep_hbm, gp_send_hbm, att_hbm,
                 send_ref, keep_ref, x_ref, affine_ref, wt_s, gp_keep_ref, gp_send_ref, att_ref, gp_s, sems):
    tokens, _ = x_ref.shape
    width = affine_ref.shape[1]
    hw = att_ref.shape[0]
    parts = [pl.ds(part * hw, hw) for part in range(3)]
    copies = fetch(
        [(x_hbm, x_ref), (gp_keep_hbm, gp_keep_ref), (gp_send_hbm, gp_send_ref)]
        + [(wt_hbm.at[rows], wt_s.at[rows]) for rows in parts]
        + [(affine_hbm, affine_ref), (att_hbm, att_ref)],
        sems,
    )
    for copy in copies[:3]:
        copy.wait()
    unit, inverse = unit_of(x_ref[:, :width].astype(F32))
    ident = eye(tokens)
    size = gp_keep_ref.shape[0]
    gp_s[pl.ds(pl.multiple_of(core_ref[0] * size, ROWS), size), :] = gp_keep_ref[...]
    gp_s[pl.ds(pl.multiple_of((1 - core_ref[0]) * size, ROWS), size), :] = gp_send_ref[...]
    grad = jnp.zeros((tokens, width), F32)
    for part in range(3):
        at = slice(part * hw, (part + 1) * hw)
        rows = mm(ident, gp_s[at, :], NT).astype(BF)
        copies[3 + part].wait()
        grad = grad + mm(rows, wt_s[at, :], NN)
    half = width // 2
    win = send_ref.shape[1]
    mine_low = which_ref[0] == 0
    for copy in copies[6:]:
        copy.wait()
    scaled = grad * affine_ref[1:2]
    first = jnp.sum(scaled, axis=1, keepdims=True)
    second = jnp.sum(scaled * unit, axis=1, keepdims=True)
    col = lax.broadcasted_iota(jnp.int32, (tokens, win), 1)
    here = jnp.where(mine_low, half, 0)
    there = jnp.where(mine_low, 0, half)
    low, high = scaled[:, :win], scaled[:, width - win :]
    send = jnp.where(mine_low, high, low)
    keep = jnp.where(mine_low, low, high)
    for place, term in enumerate((first, second)):
        coarse = term.astype(BF).astype(F32)
        send = jnp.where(col == there + 2 * place, coarse, send)
        send = jnp.where(col == there + 2 * place + 1, term - coarse, send)
    for place, term in enumerate((first, second, inverse)):
        keep = jnp.where(col == here + place, term, keep)
    send_ref[...] = send.astype(BF)
    keep_ref[:, :win] = keep
    keep_ref[:, win : 2 * win] = jnp.where(mine_low, unit[:, :win], unit[:, width - win :])
    keep_ref[:, 2 * win : 2 * win + hw] = mm(ident, att_ref[...], NT)


def split(core, which, x, affine, wt, gp_keep, gp_send, att):
    tokens = x.shape[0]
    hw = att.shape[0]
    win = window_of(wt.shape[1] // 2)
    smem = pl.BlockSpec(memory_space=pltpu.SMEM)
    vmem = pl.BlockSpec(memory_space=pltpu.VMEM)
    return pl.pallas_call(
        split_kernel,
        in_specs=[smem, smem] + [pl.BlockSpec(memory_space=pltpu.HBM)] * 6,
        out_shape=(
            jax.ShapeDtypeStruct((tokens, win), BF),
            jax.ShapeDtypeStruct((tokens, 2 * win + window_of(hw)), F32),
        ),
        scratch_shapes=[pltpu.VMEM(a.shape, a.dtype) for a in (x, affine, wt, gp_keep, gp_send, att)]
        + [pltpu.VMEM((wt.shape[0], tokens), BF), pltpu.SemaphoreType.DMA((8,))],
        compiler_params=pltpu.CompilerParams(vmem_limit_bytes=58 * 2**20),
        name="split",
    )(core, which, x, affine, wt, gp_keep, gp_send, att)


def outer_kernel(where_ref, core_ref, gp_a, gp_b, mod_a, mod_b, *refs):
    out_refs, tiles_s = refs[:-1], refs[-1]
    rows, width = gp_a.shape[0], mod_a.shape[1]
    tiles = rows // ROWS
    used = tiles * (width // LANES)
    tiles_s[used:] = jnp.zeros((tiles_s.shape[0] - used, ROWS, LANES), BF)
    gp = jnp.concatenate([gp_a[...], gp_b[...]], axis=1)
    for start in range(0, width, 2 * LANES):
        stop = min(start + 2 * LANES, width)
        mod = jnp.concatenate([mod_a[:, start:stop], mod_b[:, start:stop]], axis=0)
        found = mm(gp, mod, NN).astype(BF)
        for at in range(0, stop - start, LANES):
            j = (start + at) // LANES
            tiles_s[j * tiles : (j + 1) * tiles] = found[:, at : at + LANES].reshape(tiles, ROWS, LANES)
    size = tiles_s.shape[0] // 8
    keep_ref = out_refs[-1]
    for (lo, hi), orders, send_ref in zip(bounds(size), ORDERS, out_refs):
        order = masks_of(orders, core_ref[0])
        for q in range(4):
            k = picked(q, order[1], order[2])
            at = (where_ref[0] ^ k) * size + lo
            keep_ref[q, lo:hi] = tiles_s[pl.ds(at, hi - lo)]
            at = (where_ref[0] ^ (k ^ order[0])) * size + lo
            send_ref[q] = tiles_s[pl.ds(at, hi - lo)]


def outer(where, core, gp_a, gp_b, mod_a, mod_b, padded):
    smem = pl.BlockSpec(memory_space=pltpu.SMEM)
    vmem = pl.BlockSpec(memory_space=pltpu.VMEM)
    size = padded // 8
    shapes = [jax.ShapeDtypeStruct((4, n, ROWS, LANES), BF) for n in [hi - lo for lo, hi in bounds(size)] + [size]]
    return pl.pallas_call(
        outer_kernel,
        in_specs=[smem, smem] + [vmem] * 4,
        out_shape=tuple(shapes),
        scratch_shapes=[pltpu.VMEM((padded, ROWS, LANES), BF)],
        compiler_params=pltpu.CompilerParams(vmem_limit_bytes=16 * 2**20),
        name="outer",
    )(where, core, gp_a, gp_b, mod_a, mod_b)


ORDERS = (((1, 3, 4), (4, 1, 3)), ((3, 4, 1), (3, 4, 1)))


def bounds(size):
    cut = -(-2 * size // 3)
    return [(0, cut), (cut, size)]


def masks_of(orders, core):
    return [jnp.where(core == 0, a, b) for a, b in zip(*orders)]


def picked(q, first, second):
    return (first if q % 2 else 0) ^ (second if q // 2 else 0)


def window_of(half):
    return -(-half // LANES) * LANES


def finish_kernel(which_ref, recv_ref, keep_ref, out_ref, *, width):
    half = width // 2
    win = recv_ref.shape[1]
    mine_low = which_ref[0] == 0
    recv = recv_ref[...].astype(F32)
    keep = keep_ref[:, :win]
    unit = keep_ref[:, win : 2 * win]

    def column(block, place):
        return jnp.where(mine_low, block[:, half + place : half + place + 1], block[:, place : place + 1])

    first = column(keep, 0) + (column(recv, 0) + column(recv, 1))
    second = column(keep, 1) + (column(recv, 2) + column(recv, 3))
    inverse = column(keep, 2)
    grad = keep + recv
    out = inverse * (grad - first * (1.0 / width) - unit * (second * (1.0 / width)))
    moved = pltpu.roll(out, win - (win - half), 1)
    out_ref[:, :half] = jnp.where(mine_low, out, moved)[:, :half].astype(BF)
    out_ref[:, half:] = keep_ref[:, 2 * win : 2 * win + width - half].astype(BF)


def finish(which, recv, keep, width):
    tokens = recv.shape[0]
    smem = pl.BlockSpec(memory_space=pltpu.SMEM)
    vmem = pl.BlockSpec(memory_space=pltpu.VMEM)
    return pl.pallas_call(
        functools.partial(finish_kernel, width=width),
        in_specs=[smem, vmem, vmem],
        out_shape=jax.ShapeDtypeStruct((tokens, width), BF),
        compiler_params=pltpu.CompilerParams(vmem_limit_bytes=24 * 2**20),
        name="finish",
    )(which, recv, keep)


def fold_kernel(keep_ref, *refs):
    count = (len(refs) - 1) // 2
    got_refs, send_refs, left_ref = refs[:count], refs[count:-1], refs[-1]
    for (lo, hi), got_ref, send_ref in zip(bounds(keep_ref.shape[1]), got_refs, send_refs):
        for q in range(keep_ref.shape[0]):
            total = (keep_ref[q, lo:hi].astype(F32) + got_ref[q].astype(F32)).astype(BF)
            if q % 2:
                send_ref[q // 2] = total
            else:
                left_ref[q // 2, lo:hi] = total


def fold(keep, got):
    shapes = [jax.ShapeDtypeStruct((x.shape[0] // 2,) + x.shape[1:], BF) for x in (*got, keep)]
    found = pl.pallas_call(
        fold_kernel,
        out_shape=tuple(shapes),
        compiler_params=pltpu.CompilerParams(vmem_limit_bytes=8 * 2**20),
        name="fold",
    )(keep, *got)
    return found[:-1], found[-1]


def close_kernel(keep_ref, *refs):
    out_ref = refs[-1]
    for (lo, hi), got_ref in zip(bounds(keep_ref.shape[1]), refs):
        out_ref[lo:hi] = (keep_ref[0, lo:hi].astype(F32) + got_ref[0].astype(F32)).astype(BF)
    spare = out_ref.shape[0] - keep_ref.shape[1]
    if spare:
        out_ref[keep_ref.shape[1] :] = jnp.zeros((spare, ROWS, LANES), BF)


def close(keep, got, size):
    return pl.pallas_call(
        close_kernel,
        out_shape=jax.ShapeDtypeStruct((size, ROWS, LANES), BF),
        compiler_params=pltpu.CompilerParams(vmem_limit_bytes=8 * 2**20),
        name="close",
    )(keep, *got)


def join_kernel(*refs):
    count = len(refs) // 3
    for i in range(count):
        have_ref, got_ref, out_ref = refs[2 * i], refs[2 * i + 1], refs[2 * count + i]
        size = have_ref.shape[0]
        out_ref[:size] = have_ref[...]
        out_ref[size:] = got_ref[...]


def join(pairs):
    shapes = [jax.ShapeDtypeStruct((2 * have.shape[0],) + have.shape[1:], BF) for have, _ in pairs]
    return pl.pallas_call(
        join_kernel,
        out_shape=tuple(shapes),
        compiler_params=pltpu.CompilerParams(vmem_limit_bytes=8 * 2**20),
        name="join",
    )(*[x for pair in pairs for x in pair])


def reduce_kernel(parts_ref, out_ref, *, factor):
    out_ref[...] = (jnp.sum(parts_ref[...].astype(F32), axis=0) * factor).astype(BF)


def reduce(parts, factor):
    return pl.pallas_call(
        functools.partial(reduce_kernel, factor=factor),
        out_shape=jax.ShapeDtypeStruct(parts.shape[1:], BF),
        compiler_params=pltpu.CompilerParams(vmem_limit_bytes=4 * 2**20),
        name="reduce",
    )(parts)


def trio_kernel(own_ref, below_ref, above_ref, all_ref, two_ref):
    size = own_ref.shape[0]
    for i, ref in enumerate((below_ref, own_ref, above_ref)):
        all_ref[i * size : (i + 1) * size] = ref[...]
        if i < 2:
            two_ref[i * size : (i + 1) * size] = ref[...]


def trio(own, below, above):
    size = own.shape[0]
    return pl.pallas_call(
        trio_kernel,
        out_shape=tuple(jax.ShapeDtypeStruct((n * size,) + own.shape[1:], BF) for n in (3, 2)),
        compiler_params=pltpu.CompilerParams(vmem_limit_bytes=4 * 2**20),
        name="trio",
    )(own, below, above)


def place_kernel(clip_ref, near_ref, below_ref, above_ref, *refs, clips):
    out_refs, all_s = refs[:-1], refs[-1]
    size = all_s.shape[0] // clips
    for ref, first in ((near_ref, -1), (below_ref, -4), (above_ref, 2)):
        for i in range(ref.shape[0] // size):
            at = lax.rem(clip_ref[0] + (first + i + clips), clips) * size
            all_s[pl.ds(at, size)] = ref[i * size : (i + 1) * size]
    for (lo, hi), out_ref in zip(bounds(sum(ref.shape[1] for ref in out_refs)), out_refs):
        out_ref[0] = all_s[lo:hi]


def place(clip, near, below, above, clips, size):
    total = near.shape[0] // 3 * clips
    smem = pl.BlockSpec(memory_space=pltpu.SMEM)
    vmem = pl.BlockSpec(memory_space=pltpu.VMEM)
    return pl.pallas_call(
        functools.partial(place_kernel, clips=clips),
        in_specs=[smem, vmem, vmem, vmem],
        out_shape=tuple(jax.ShapeDtypeStruct((1, hi - lo, ROWS, LANES), BF) for lo, hi in bounds(size)),
        scratch_shapes=[pltpu.VMEM((total, ROWS, LANES), BF)],
        compiler_params=pltpu.CompilerParams(vmem_limit_bytes=4 * 2**20),
        name="place",
    )(clip, near, below, above)


def untile_kernel(where_ref, half_ref, *refs):
    pieces, (out_ref, tiles_s) = refs[:-2], refs[-2:]
    size = tiles_s.shape[0] // 16
    pieces = iter(pieces)
    for side in range(2):
        half = half_ref[0] ^ side
        for far in range(2):
            for (lo, hi), orders in zip(bounds(size), ORDERS):
                piece = next(pieces)
                order = masks_of(orders, half)
                for q in range(4):
                    k = picked(q, order[2], order[1]) ^ (order[0] * far)
                    at = (half * 8 + (where_ref[0] ^ k)) * size + lo
                    tiles_s[pl.ds(at, hi - lo)] = piece[q]
    rows = out_ref.shape[0] // 2
    tiles = rows // ROWS
    for half in range(2):
        for j in range(out_ref.shape[1] // LANES):
            start = half * 8 * size + j * tiles
            block = tiles_s[start : start + tiles].reshape(rows, LANES)
            out_ref[half * rows : (half + 1) * rows, j * LANES : (j + 1) * LANES] = block


def untile(where, half, pieces, rows, width):
    smem = pl.BlockSpec(memory_space=pltpu.SMEM)
    vmem = pl.BlockSpec(memory_space=pltpu.VMEM)
    tiles = sum(4 * piece.shape[1] for piece in pieces)
    return pl.pallas_call(
        untile_kernel,
        in_specs=[smem, smem] + [vmem] * len(pieces),
        out_shape=jax.ShapeDtypeStruct((rows, width), BF),
        scratch_shapes=[pltpu.VMEM((tiles, ROWS, LANES), BF)],
        compiler_params=pltpu.CompilerParams(vmem_limit_bytes=16 * 2**20),
        name="untile",
    )(where, half, *pieces)


def swap(x, axes, k):
    count = math.prod(lax.axis_size(a) for a in axes)
    return lax.ppermute(x, axes, [(i, i ^ k) for i in range(count)])


def exchange(x, axis):
    parts = x.reshape((-1,) + x.shape[-3:])
    return lax.all_to_all(parts, axis, split_axis=0, concat_axis=0, tiled=True)


def plane_size():
    return lax.axis_size("xlo") * lax.axis_size("y")


def meet(blocks, level):
    found = []
    for block, orders in zip(blocks, ORDERS):
        pairs = [(p * 2 + c, (p ^ orders[c][level]) * 2 + c) for p in range(plane_size()) for c in range(2)]
        found.append(lax.ppermute(block, SEQ, pairs))
    return found


def sum_plane(found, beside, size):
    send, keep = found[:-1], found[-1]
    got, beside = lax.optimization_barrier((meet(send, 0), beside))
    send, keep = fold(keep, got)
    send, keep = fold(keep, meet(send, 1))
    return close(keep, meet(send, 2), size), beside


def shift(x, axis, step):
    count = lax.axis_size(axis)
    return lax.ppermute(x, axis, [(i, (i + step) % count) for i in range(count)])


def gather_clips(own, beside):
    near, two = trio(own, shift(own, "dp", 1), shift(own, "dp", -1))
    near, two, beside = lax.optimization_barrier((near, two, beside))
    return near, shift(near, "dp", 3), shift(two, "dp", -3), beside


def gather_plane(have, where, half, rows, width, beside):
    have = join(list(zip(have, meet(have, 2))))
    got, beside = lax.optimization_barrier((meet(have, 1), beside))
    have = join(list(zip(have, got)))
    got = meet(have, 0)
    got[-1], have, beside = lax.optimization_barrier((got[-1], have, unpack(beside)))
    pieces = list(have) + got
    pieces = pieces + [swap(piece, ("core",), 1) for piece in pieces]
    return untile(where, half, pieces, rows, width), beside


def body(latent, mod_shift, mod_scale, w_qkv, q_gain, k_gain, cotangent):
    _, _, patches, width = latent.shape
    hw = w_qkv.shape[2]
    hd = q_gain.shape[0]
    heads = hw // hd
    frames = 1
    for a in SEQ:
        frames *= lax.axis_size(a)
    own_patches = patches // frames
    clips = lax.axis_size("dp")
    wt = w_qkv.transpose(1, 2, 0).reshape(3 * hw, width)
    x = pack(latent[0, 0], cotangent[0, 0].T).reshape(frames, own_patches, width + hw)
    x = lax.all_to_all(x, SEQ, split_axis=0, concat_axis=0, tiled=True).reshape(patches, width + hw)
    affine = jnp.concatenate([mod_shift, 1.0 + mod_scale])
    core = lax.axis_index("core").astype(jnp.int32).reshape(1)
    which = lax.axis_index("tensor").astype(jnp.int32).reshape(1)
    where = lax.axis_index(PLANE).astype(jnp.int32).reshape(1)
    mod, gp_keep, gp_send, att_t = attend(
        core, x, affine, wt, q_gain[:, None], k_gain[:, None], own_patches, heads, hd
    )
    used = (3 * hw // 2 // ROWS) * (width // LANES)
    size = -(-used // plane_size())
    gp_other, mod_other = swap(gp_send, ("core",), 1), swap(mod, ("core",), 1)
    found = outer(where, core, gp_keep, gp_other, mod, mod_other, size * plane_size())
    send, keep = split(core, which, x, affine, wt, gp_keep, gp_send, att_t)
    own, send = sum_plane(found, send, -(-size // clips) * clips)
    own, send = lax.optimization_barrier((own, send))
    recv = lax.ppermute(send, "tensor", [(0, 1), (1, 0)])
    own = exchange(own.reshape((clips, own.shape[0] // clips) + own.shape[1:]), "dp")
    own = reduce(own, 1.0 / math.sqrt(clips * frames * patches))
    near, below, above, recv = gather_clips(own, recv)
    home = finish(which, recv, keep, width).reshape(frames, own_patches, width)
    home = lax.all_to_all(home, SEQ, split_axis=0, concat_axis=0, tiled=True)
    clip = lax.axis_index("dp").astype(jnp.int32).reshape(1)
    have = place(clip, near, below, above, clips, size)
    home = home.reshape(patches, width)
    grad_qkv, (grad_t, att_t) = gather_plane(have, where, core, 3 * hw, width, home)
    grad_qkv = grad_qkv.reshape(3, hw, width).transpose(2, 0, 1)
    return (att_t.T[None, None], grad_t.T[None, None], grad_qkv)


def solution(mesh):
    fine = Mesh(mesh.devices.reshape(mesh.shape["dp"], 2, 4, 2, 2), ("dp",) + SEQ + ("tensor",))
    in_specs = (
        P("dp", SEQ, None, None),
        P("dp", None),
        P("dp", None),
        P(None, None, "tensor"),
        P(),
        P(),
        P("dp", SEQ, None, "tensor"),
    )
    out_specs = (
        P("dp", SEQ, None, "tensor"),
        P("dp", SEQ, None, "tensor"),
        P(None, None, "tensor"),
    )
    return jax.shard_map(body, mesh=fine, in_specs=in_specs, out_specs=out_specs, check_vma=False)
```
